256 devices in a mesh: replica: 16 (over x_lo, y, core), shard: 16 (over x_hi, z).
Axes of the slice: x: 4 (x_hi: 2, x_lo: 2; x = x_hi * 2 + x_lo), y: 4, z: 8, core: 2. Of those that a mesh axis runs over, the one named last changes fastest.
Arguments:
- hidden: bfloat16 [4, 512, 5120], P(None, 'replica', 'shard'), may hold values from -6 to 6
- norm_gain: float32 [5120], replicated, may hold values from 0.1 to 1.9
- query_gain: float32 [128], replicated, may hold values from 0.1 to 1.9
- key_gain: float32 [128], replicated, may hold values from 0.1 to 1.9
- base_query: bfloat16 [5120, 4096], P(None, 'shard'), may hold values from -0.078125 to 0.078125
- base_key: bfloat16 [5120, 2048], P(None, 'shard'), may hold values from -0.078125 to 0.078125
- base_value: bfloat16 [5120, 2048], P(None, 'shard'), may hold values from -0.078125 to 0.078125
- base_output: bfloat16 [5120, 4096], P(None, 'shard'), may hold values from -0.09375 to 0.09375
- delta_query: bfloat16 [5120, 4096], P(('replica', 'shard')), may hold values from -4 to 4
- scale_query: int32 [5120, 32], P(('replica', 'shard')), may hold values from 6 to 9
- key_delta_codes: bfloat16 [5120, 1024], P(('replica', 'shard')), may hold values from -4 to 4
- key_scale_codes: int32 [5120, 8], P(('replica', 'shard')), may hold values from 6 to 9
- value_delta_codes: bfloat16 [5120, 1024], P(('replica', 'shard')), may hold values from -4 to 4
- value_scale_codes: int32 [5120, 8], P(('replica', 'shard')), may hold values from 6 to 9
- delta_output: bfloat16 [5120, 4096], P(('replica', 'shard')), may hold values from -4 to 4
- scale_output: int32 [5120, 32], P(('replica', 'shard')), may hold values from 6 to 9
- cache_keys: bfloat16 [512, 64, 2048], P('replica', None, 'shard')
- cache_values: bfloat16 [512, 64, 2048], P('replica', None, 'shard'), may hold values from -6 to 6
- lengths: int32 [512], P('replica'), may hold values from 1 to 64, as said below
- stale_rows: int32 [16, 128], P('replica'), may hold values from 0 to 31
- stale_steps: int32 [16, 128], P('replica'), may hold values from 0 to 3
- stale_back: int32 [16, 128], P('replica'), may hold values from 0 to 67
Outputs:
- attention_out: bfloat16 [4, 512, 5120], P(None, 'replica', 'shard')
- log_ratio: float32 [16, 128], P('replica')
The draws below stay inside these ranges and needn't reach their ends.
Inputs may be any that keep to these rules, and one draw needn't show every extreme that they name: `lengths`: the first row of each engine's 32 rows has 64.
All inputs are finite; a program needn't handle non-finite values.
Results may differ from the reference program's by a relative error of at most 0.02.
The reference program's roundings to bfloat16 on the way count: a program that leaves them out, or rounds other values in their place, can miss the bound.
Values may be sent and summed in bfloat16 or wider, within the bound.
No kernel may reach another device: no remote copies, remote signals or barrier semaphores. Data moves between devices by JAX's collectives and lax.ppermute only.
A program may use at most 128 MiB of HBM per device.

```python
import jax
import jax.numpy as jnp
from jax import lax

MODEL_WIDTH = 5120
HQ = 32
KEY_VALUE_HEADS = 8
HEAD_SIZE = 128
STEPS = 4
R_DEV = 32
CTX = 64
S_DEV = 128
ROWS = 512
HEAD_COPY_SLOTS = 16
N_REPLICA = 16


def draw_cache_keys(key, part):
    key = jax.random.fold_in(key, 11)
    entries = jax.random.normal(key, (ROWS, CTX, HEAD_COPY_SLOTS * HEAD_SIZE), jnp.float32)
    return entries.astype(jnp.bfloat16)


def draw_lengths(key, part):
    key = jax.random.fold_in(key, 7)
    drawn = jax.random.randint(key, (ROWS,), 1, CTX + 1)
    return drawn.at[::R_DEV].set(CTX)


def place_ends(values, stream_key, smallest, high):
    shape = values.shape
    index_at = [jax.random.randint(jax.random.fold_in(stream_key, axis), (), 0, shape[axis]) for axis in range(len(shape))]
    values = values.at[tuple(index_at)].set(smallest)
    longest = shape.index(max(shape))
    index_at[longest] = (index_at[longest] + 1) % shape[longest]
    return values.at[tuple(index_at)].set(high)


def block_scale(stream_key, dims, split, smallest, top_value):
    def one(dim, shards_of):
        heights = jax.random.uniform(jax.random.fold_in(jax.random.fold_in(stream_key, 6), dim), (shards_of,), jnp.float32, smallest / len(split), top_value / len(split))
        return jnp.repeat(jnp.exp(heights), dims[dim] // shards_of).reshape((-1,) + (1,) * (len(dims) - dim - 1))

    loudness = one(*split[0])
    for cut in split[1:]:
        loudness = loudness * one(*cut)
    return loudness


def gaussian(own_key, dims, scale, most, cuts=(), dtype=jnp.bfloat16):
    level = block_scale(own_key, dims, cuts, -0.22, 0.18) if cuts else 1.0
    values = jax.random.normal(own_key, dims, jnp.float32) * scale * level
    return jnp.minimum(jnp.maximum(values, -most), most).astype(dtype)


def setup_inputs(seed: int = 0) -> dict:
    seeds = jax.random.split(jax.random.key(seed), 23)
    hidden = gaussian(seeds[0], (STEPS, ROWS, MODEL_WIDTH), 1.0, 6.0, ((1, 16), (2, 16)))
    norm_gain = jnp.clip(1.0 + 0.18 * jax.random.normal(seeds[1], (MODEL_WIDTH,), jnp.float32), 0.1, 1.9)
    query_gain = jnp.clip(1.0 + 0.18 * jax.random.normal(seeds[2], (HEAD_SIZE,), jnp.float32), 0.1, 1.9)
    key_gain = jnp.clip(1.0 + 0.18 * jax.random.normal(seeds[3], (HEAD_SIZE,), jnp.float32), 0.1, 1.9)
    base_query = gaussian(seeds[4], (MODEL_WIDTH, HQ * HEAD_SIZE), MODEL_WIDTH ** -0.5, 0.078125, ((1, 16),))
    base_key = gaussian(seeds[5], (MODEL_WIDTH, HEAD_COPY_SLOTS * HEAD_SIZE), MODEL_WIDTH ** -0.5, 0.078125, ((1, 16),))
    base_value = gaussian(seeds[6], (MODEL_WIDTH, HEAD_COPY_SLOTS * HEAD_SIZE), MODEL_WIDTH ** -0.5, 0.078125, ((1, 16),))
    base_output = gaussian(seeds[7], (MODEL_WIDTH, HQ * HEAD_SIZE), (HQ * HEAD_SIZE) ** -0.5, 0.09375, ((1, 16),))
    delta_query = gaussian(seeds[8], (MODEL_WIDTH, HQ * HEAD_SIZE), 1.0, 4.0, ((0, 256),))
    scale_query = place_ends(jax.random.randint(seeds[9], (MODEL_WIDTH, HQ), 6, 10), jax.random.fold_in(seeds[9], 1), 6, 9).astype(jnp.int32)
    key_delta_codes = gaussian(seeds[10], (MODEL_WIDTH, KEY_VALUE_HEADS * HEAD_SIZE), 1.0, 4.0, ((0, 256),))
    key_scale_codes = place_ends(jax.random.randint(seeds[11], (MODEL_WIDTH, KEY_VALUE_HEADS), 6, 10), jax.random.fold_in(seeds[11], 1), 6, 9).astype(jnp.int32)
    value_delta_codes = gaussian(seeds[12], (MODEL_WIDTH, KEY_VALUE_HEADS * HEAD_SIZE), 1.0, 4.0, ((0, 256),))
    value_scale_codes = place_ends(jax.random.randint(seeds[13], (MODEL_WIDTH, KEY_VALUE_HEADS), 6, 10), jax.random.fold_in(seeds[13], 1), 6, 9).astype(jnp.int32)
    delta_output = gaussian(seeds[14], (MODEL_WIDTH, HQ * HEAD_SIZE), 1.0, 4.0, ((0, 256),))
    scale_output = place_ends(jax.random.randint(seeds[15], (MODEL_WIDTH, HQ), 6, 10), jax.random.fold_in(seeds[15], 1), 6, 9).astype(jnp.int32)
    cache_keys = draw_cache_keys(jax.random.fold_in(seeds[22], 71), 0)
    cache_values = gaussian(seeds[17], (ROWS, CTX, HEAD_COPY_SLOTS * HEAD_SIZE), 1.0, 6.0, ((0, 16), (2, 16)))
    lengths = draw_lengths(jax.random.fold_in(seeds[22], 71), 0)
    stale_rows = place_ends(jax.random.randint(seeds[19], (N_REPLICA, S_DEV), 0, R_DEV), jax.random.fold_in(seeds[19], 1), 0, R_DEV - 1).astype(jnp.int32)
    stale_steps = place_ends(jax.random.randint(seeds[20], (N_REPLICA, S_DEV), 0, STEPS), jax.random.fold_in(seeds[20], 1), 0, STEPS - 1).astype(jnp.int32)
    stale_back = place_ends(jax.random.randint(seeds[21], (N_REPLICA, S_DEV), 0, CTX + STEPS), jax.random.fold_in(seeds[21], 1), 0, (CTX + STEPS) - 1).astype(jnp.int32)
    return {"hidden": hidden, "norm_gain": norm_gain, "query_gain": query_gain, "key_gain": key_gain, "base_query": base_query, "base_key": base_key, "base_value": base_value, "base_output": base_output, "delta_query": delta_query, "scale_query": scale_query, "key_delta_codes": key_delta_codes, "key_scale_codes": key_scale_codes, "value_delta_codes": value_delta_codes, "value_scale_codes": value_scale_codes, "delta_output": delta_output, "scale_output": scale_output, "cache_keys": cache_keys, "cache_values": cache_values, "lengths": lengths, "stale_rows": stale_rows, "stale_steps": stale_steps, "stale_back": stale_back}


EPSILON = 1e-06
THETA = 1000000.0

def rms_scale(value, gain):
    return value * lax.rsqrt(lax.optimization_barrier(jnp.mean(value * value, axis=-1, keepdims=True)) + EPSILON) * gain

def rotate(value, position):
    half = value.shape[-1] // 2
    freq = THETA ** (-(jnp.arange(half).astype(jnp.float32) * 2.0) / value.shape[-1])
    angle = position.astype(jnp.float32)[..., None, None] * freq
    cosine = jnp.cos(angle)
    sine = jnp.sin(angle)
    first = value[..., :half]
    second = value[..., half:]
    return jnp.concatenate([first * cosine - second * sine, second * cosine + first * sine], axis=-1)

def dequantize(codes, exponents):
    rows_here, width = codes.shape
    heads = exponents.shape[1]
    factor = 1.0 / jnp.left_shift(jnp.ones_like(exponents), exponents).astype(jnp.float32)
    scaled = codes.astype(jnp.float32).reshape(rows_here, heads, width // heads) * factor[:, :, None]
    return scaled.reshape(rows_here, width).astype(jnp.bfloat16)

def expand_slots(values, repeat_count):
    rows_here, width = values.shape
    heads = width // HEAD_SIZE
    spread = jnp.broadcast_to(values.reshape(rows_here, heads, 1, HEAD_SIZE), (rows_here, heads, repeat_count, HEAD_SIZE))
    return spread.reshape(rows_here, heads * repeat_count * HEAD_SIZE)

def refresh(base, delta):
    return (base.astype(jnp.float32) + delta.astype(jnp.float32)).astype(jnp.bfloat16)

def project(normed, weight, gain, position):
    lead = normed.shape[:-1]
    raw = jnp.dot(normed.reshape(-1, normed.shape[-1]), weight, preferred_element_type=jnp.float32)
    raw = raw.reshape(lead + (weight.shape[1] // HEAD_SIZE, HEAD_SIZE))
    return rotate(rms_scale(raw, gain), position).astype(jnp.bfloat16)

def log_scores(query, cache_k, fresh_k, lens, steps):
    a_len, r_len, heads, width = query.shape
    slots = cache_k.shape[2]
    grouped = query.astype(jnp.float32).reshape(a_len, r_len, slots, heads // slots, width)
    past = jnp.einsum('arkgd,rckd->arkgc', grouped, cache_k.astype(jnp.float32))
    fresh = jnp.einsum('arkgd,urkd->arkgu', grouped, fresh_k.astype(jnp.float32))
    scores = jnp.concatenate([past, fresh], axis=-1) * width ** (-0.5)
    past_ok = jnp.arange(cache_k.shape[1])[None, :] < lens[:, None]
    past_ok = jnp.broadcast_to(past_ok[None, :, None, None, :], past.shape)
    fresh_ok = jnp.arange(fresh_k.shape[0])[None, None, :] <= steps[:, :, None]
    fresh_ok = jnp.broadcast_to(fresh_ok[:, :, None, None, :], fresh.shape)
    allowed = jnp.concatenate([past_ok, fresh_ok], axis=-1)
    scores = jnp.where(allowed, scores, -jnp.inf)
    shifted = scores - lax.optimization_barrier(jnp.max(scores, axis=-1, keepdims=True))
    total = lax.optimization_barrier(jnp.sum(jnp.exp(shifted), axis=-1, keepdims=True))
    logp = shifted - jnp.log(total)
    probs = (jnp.exp(shifted) / total).astype(jnp.bfloat16)
    return (logp.reshape(a_len, r_len, heads, -1), probs)

def combine(probs, cache_v, fresh_v):
    a_len, r_len, slots, group, positions = probs.shape
    ctx_len = cache_v.shape[1]
    weights = probs.astype(jnp.float32)
    past = jnp.einsum('arkgc,rckd->arkgd', weights[..., :ctx_len], cache_v.astype(jnp.float32))
    fresh = jnp.einsum('arkgu,urkd->arkgd', weights[..., ctx_len:], fresh_v.astype(jnp.float32))
    return (past + fresh).astype(jnp.bfloat16).reshape(a_len, r_len, slots * group * HEAD_SIZE)

def pick(logp, index):
    return jnp.take_along_axis(logp, index[:, None, None], axis=2)[:, :, 0]

def reference(hidden, norm_gain, query_gain, key_gain, base_query, base_key, base_value, base_output, delta_query, scale_query, key_delta_codes, key_scale_codes, value_delta_codes, value_scale_codes, delta_output, scale_output, cache_keys, cache_values, lengths, stale_rows, stale_steps, stale_back):
    repeat_count = HEAD_COPY_SLOTS // KEY_VALUE_HEADS
    new_query = refresh(base_query, dequantize(delta_query, scale_query))
    new_key = refresh(base_key, expand_slots(dequantize(key_delta_codes, key_scale_codes), repeat_count))
    new_value = refresh(base_value, expand_slots(dequantize(value_delta_codes, value_scale_codes), repeat_count))
    new_output = refresh(base_output, dequantize(delta_output, scale_output))
    normed = rms_scale(hidden.astype(jnp.float32), norm_gain).astype(jnp.bfloat16)
    blocks = (normed.reshape(STEPS, N_REPLICA, R_DEV, MODEL_WIDTH).transpose(1, 0, 2, 3), cache_keys.reshape(N_REPLICA, R_DEV, CTX, HEAD_COPY_SLOTS, HEAD_SIZE), cache_values.reshape(N_REPLICA, R_DEV, CTX, HEAD_COPY_SLOTS, HEAD_SIZE), lengths.reshape(N_REPLICA, R_DEV), stale_rows, stale_steps, stale_back)

    def engine(item):
        block_x, cache_k, cache_v, lens, rows_s, steps_s, back_s = item
        step_ids = jnp.arange(STEPS).astype(jnp.int32)
        positions = lens[None, :] + step_ids[:, None]
        query = project(block_x, new_query, query_gain, positions)
        fresh_k = project(block_x, new_key, key_gain, positions)
        fresh_v = jnp.dot(block_x.reshape(-1, MODEL_WIDTH), new_value, preferred_element_type=jnp.float32)
        fresh_v = fresh_v.reshape(STEPS, R_DEV, HEAD_COPY_SLOTS, HEAD_SIZE).astype(jnp.bfloat16)
        step_grid = jnp.broadcast_to(step_ids[:, None], (STEPS, R_DEV))
        logp_new, probs = log_scores(query, cache_k, fresh_k, lens, step_grid)
        attended = combine(probs, cache_v, fresh_v)
        output = jnp.dot(attended.reshape(-1, HQ * HEAD_SIZE), new_output.T, preferred_element_type=jnp.float32)
        output = output.astype(jnp.bfloat16).reshape(STEPS, R_DEV, MODEL_WIDTH)
        lens_s = lens[rows_s]
        place = lens_s + steps_s - back_s % (lens_s + steps_s + 1)
        index = jnp.where(place >= lens_s, CTX + place - lens_s, place).astype(jnp.int32)
        picked_new = pick(logp_new[steps_s, rows_s], index)
        sample_x = block_x[steps_s, rows_s]
        query_old = project(sample_x[None], base_query, query_gain, (lens_s + steps_s)[None])
        keys_old = project(block_x[:, rows_s], base_key, key_gain, positions[:, rows_s])
        logp_old, unused = log_scores(query_old, cache_k[rows_s], keys_old, lens_s, steps_s[None])
        picked_old = pick(logp_old[0], index)
        ratio = lax.optimization_barrier(jnp.sum(picked_new - picked_old, axis=1)) / HQ
        return (output, ratio)
    outputs, ratios = lax.map(engine, blocks)
    attention_out = outputs.transpose(1, 0, 2, 3).reshape(STEPS, ROWS, MODEL_WIDTH)
    return (attention_out, ratios)
```

```python
import functools

import jax
import jax.numpy as jnp
from jax import lax
from jax.experimental import pallas as pl
from jax.experimental.pallas import tpu as pltpu
from jax.sharding import PartitionSpec as P

HQ = 32
HEAD = 128
WIDTH = 5120
STEPS = 4
ROWS = 32
TOKENS = STEPS * ROWS
CTX = 64
PARTS = 16
OWN = WIDTH // PARTS
CUT = 20
COLS = 768
GROUP = 8
GROUPS = ROWS // GROUP
TAIL = 16
EPSILON = 1e-06
THETA = 1000000.0
SCALE = HEAD ** (-0.5)
NEG = -1e30
CHUNKS = 8
CHUNK = WIDTH // CHUNKS
F32 = jnp.float32
BF16 = jnp.bfloat16
VMEM = pltpu.VMEM


def factors(codes):
    out = jnp.ones(codes.shape, F32)
    for bit in range(5):
        out = out * jnp.where((codes >> bit) & 1 == 1, F32(2.0 ** -(2**bit)), F32(1.0))
    return out


def pack_kernel(dq, sq, dk, sk, dv, sv, do, so, out, buf):
    fq, fk, fv, fo = factors(sq[...]), factors(sk[...]), factors(sv[...]), factors(so[...])

    def piece(codes, factor, head):
        return codes[:, head * HEAD : (head + 1) * HEAD].astype(F32) * factor[:, head : head + 1]

    for dest in range(PARTS):
        half = dest // 2
        pieces = (
            piece(dq, fq, 2 * dest),
            piece(dq, fq, 2 * dest + 1),
            piece(dk, fk, half),
            piece(dv, fv, half),
            piece(do, fo, 2 * dest),
            piece(do, fo, 2 * dest + 1),
        )
        for c, value in enumerate(pieces):
            buf[dest % 2, CUT * c : CUT * (c + 1), :] = value
        out[dest] = buf[dest % 2].astype(BF16)


def refresh_kernel(block, recv, bq, bk, bv, bo, out, buf, delta):
    for src in range(PARTS):
        buf[src % 2] = recv[src].astype(F32)
        for c in range(6):
            delta[CUT * src : CUT * (src + 1), HEAD * c : HEAD * (c + 1)] = buf[
                src % 2, CUT * c : CUT * (c + 1), :
            ]
    out[:, 0:256] = (bq[...].astype(F32) + delta[:, 0:256]).astype(BF16)
    out[:, 256:384] = (bk[...].astype(F32) + delta[:, 256:384]).astype(BF16)
    out[:, 384:512] = (bv[...].astype(F32) + delta[:, 384:512]).astype(BF16)
    out[:, 512:768] = (bo[...].astype(F32) + delta[:, 512:768]).astype(BF16)


def dot_nt(a, b):
    return lax.dot_general(a, b, (((1,), (1,)), ((), ())), preferred_element_type=F32)


def dot(a, b):
    return jnp.dot(a, b, preferred_element_type=F32)


def head_norm_rotate(raw, gain, cosine, sine):
    value = raw * lax.rsqrt(jnp.mean(raw * raw, axis=-1, keepdims=True) + EPSILON) * gain
    swapped = jnp.concatenate([value[:, HEAD // 2 :], value[:, : HEAD // 2]], axis=-1)
    return value * cosine + swapped * sine


def group_scores(group, query, cache, fresh, lens):
    picked = [
        query[h * TOKENS + t * ROWS + group * GROUP : h * TOKENS + t * ROWS + (group + 1) * GROUP, :]
        for h in range(2)
        for t in range(STEPS)
    ]
    q = jnp.concatenate(picked, axis=0).astype(BF16)
    past = dot_nt(q, cache) * SCALE
    new = dot_nt(q, fresh) * SCALE
    n = 2 * STEPS * GROUP
    length = jnp.concatenate([lens[group * GROUP : (group + 1) * GROUP, :]] * (2 * STEPS), axis=0)
    column = lax.broadcasted_iota(jnp.int32, past.shape, 1)
    line = lax.broadcasted_iota(jnp.int32, past.shape, 0)
    past_ok = ((column >> 6) == (line & 7)) & ((column & 63) < length[:, 0:1])
    column = lax.broadcasted_iota(jnp.int32, (n, TOKENS), 1)
    line = lax.broadcasted_iota(jnp.int32, (n, TOKENS), 0)
    new_ok = ((column & 31) == group * GROUP + (line & 7)) & ((column >> 5) <= ((line >> 3) & 3))
    past = jnp.where(past_ok, past, NEG)
    new = jnp.where(new_ok, new, NEG)
    top = jnp.maximum(
        jnp.max(past, axis=-1, keepdims=True), jnp.max(new, axis=-1, keepdims=True)
    )
    past = jnp.exp(past - top)
    new = jnp.exp(new - top)
    total = jnp.sum(past, axis=-1, keepdims=True) + jnp.sum(new, axis=-1, keepdims=True)
    return past, new, total, top + jnp.log(total)


def put_groups(group, ref, value):
    for h in range(2):
        for t in range(STEPS):
            at = h * TOKENS + t * ROWS + group * GROUP
            i = (h * STEPS + t) * GROUP
            ref[at : at + GROUP, :] = value[i : i + GROUP, :]


def sample_logp(query, keys, one_query, lse):
    out = []
    for h in range(2):
        q = dot(one_query, query[h * TOKENS : (h + 1) * TOKENS, :].astype(BF16))
        score = jnp.sum(q * keys, axis=-1, keepdims=True) * SCALE
        line = lse[h * TOKENS : (h + 1) * TOKENS, :].T
        picked = jnp.sum(one_query.astype(F32) * line, axis=-1, keepdims=True)
        out.append(jnp.broadcast_to(score - picked, (TOKENS, HEAD)))
    return out


def prepare_kernel(
    xt, gain, qg, kg, cosine, sine, lens, token, place, base_q, base_k, cache,
    normed, keys_out, one_q_out, one_f_out, old_out,
    total, query, lse,
):
    total[...] = jnp.zeros_like(total)
    for k in range(WIDTH // HEAD):
        x = xt[k * HEAD : (k + 1) * HEAD, :].astype(F32)
        total[...] += jnp.sum(x * x, axis=0, keepdims=True)
    scale = lax.rsqrt(total[...] * (1.0 / WIDTH) + EPSILON)
    for k in range(WIDTH // HEAD):
        x = xt[k * HEAD : (k + 1) * HEAD, :].astype(F32) * scale
        normed[:, k * HEAD : (k + 1) * HEAD] = (
            x.T * gain[:, k * HEAD : (k + 1) * HEAD]
        ).astype(BF16)
    raw = dot(normed[...], base_q[...])
    raw_k = dot(normed[...], base_k[...])
    cos, sin = cosine[...], sine[...]
    for h in range(2):
        query[h * TOKENS : (h + 1) * TOKENS, :] = (
            head_norm_rotate(raw[:, h * HEAD : (h + 1) * HEAD], qg[...], cos, sin)
            .astype(BF16)
            .astype(F32)
        )
    fresh = head_norm_rotate(raw_k, kg[...], cos, sin).astype(BF16)
    for g in range(GROUPS):
        _, _, _, log_sum = group_scores(
            g, query, cache[g * GROUP * CTX : (g + 1) * GROUP * CTX, :], fresh, lens
        )
        put_groups(g, lse, jnp.broadcast_to(log_sum, (log_sum.shape[0], HEAD)))
    tokens = jnp.broadcast_to(token[...], (TOKENS, TOKENS)).T
    places = jnp.broadcast_to(place[...], (TOKENS, TOKENS)).T
    lane = lax.broadcasted_iota(jnp.int32, (TOKENS, TOKENS), 1)
    one_q = jnp.where(tokens == lane, F32(1.0), F32(0.0)).astype(BF16)
    one_f = jnp.where(places == lane + ROWS * CTX, F32(1.0), F32(0.0)).astype(BF16)
    keys = jnp.zeros((TOKENS, HEAD), F32)
    for k in range(ROWS * CTX // HEAD):
        one = jnp.where(places == lane + k * HEAD, F32(1.0), F32(0.0)).astype(BF16)
        keys = keys + dot(one, cache[k * HEAD : (k + 1) * HEAD, :])
    keys_out[...] = keys
    one_q_out[...] = one_q
    one_f_out[...] = one_f
    old = sample_logp(query, keys + dot(one_f, fresh), one_q, lse)
    old_out[0] = old[0]
    old_out[1] = old[1]


def main_kernel(
    normed, weight, qg, kg, cosine, sine, lens, cache, values, keys, one_q, one_f, old,
    out,
    held, query, lse, mixed, sems,
):
    copies = [
        pltpu.make_async_copy(
            weight.at[pl.ds(c * CHUNK, CHUNK)], held.at[pl.ds(c * CHUNK, CHUNK)], sems.at[c]
        )
        for c in range(CHUNKS)
    ]
    for copy in copies:
        copy.start()
    raw = jnp.zeros((TOKENS, 512), F32)
    for c in range(CHUNKS):
        copies[c].wait()
        raw = raw + dot(
            normed[:, c * CHUNK : (c + 1) * CHUNK], held[c * CHUNK : (c + 1) * CHUNK, 0:512]
        )
    cos, sin = cosine[...], sine[...]
    for h in range(2):
        query[h * TOKENS : (h + 1) * TOKENS, :] = (
            head_norm_rotate(raw[:, h * HEAD : (h + 1) * HEAD], qg[...], cos, sin)
            .astype(BF16)
            .astype(F32)
        )
    fresh = head_norm_rotate(raw[:, 256:384], kg[...], cos, sin).astype(BF16)
    fresh_v = raw[:, 384:512].astype(BF16)
    for g in range(GROUPS):
        at = slice(g * GROUP * CTX, (g + 1) * GROUP * CTX)
        past, new, total, log_sum = group_scores(g, query, cache[at, :], fresh, lens)
        put_groups(g, lse, jnp.broadcast_to(log_sum, (log_sum.shape[0], HEAD)))
        mix = dot((past / total).astype(BF16), values[at, :])
        mix = mix + dot((new / total).astype(BF16), fresh_v)
        put_groups(g, mixed, mix)
    attended = jnp.concatenate([mixed[0:TOKENS, :], mixed[TOKENS:, :]], axis=1).astype(BF16)
    for p in range(PARTS):
        part = dot_nt(held[p * OWN : (p + 1) * OWN, 512:768], attended)
        out[p, 0:OWN, :] = part.astype(BF16)
    now = sample_logp(query, keys[...] + dot(one_f[...], fresh), one_q[...], lse)
    term = (now[0] - old[0]) + (now[1] - old[1])
    line = term.T[0:1, :]
    high = line.astype(BF16).astype(F32)
    middle = (line - high).astype(BF16).astype(F32)
    low = line - high - middle
    tail = jnp.concatenate([high, middle, low, jnp.zeros((TAIL - 3, TOKENS), F32)], axis=0)
    tail = tail.astype(BF16)
    for p in range(PARTS):
        out[p, OWN : OWN + TAIL, :] = tail


def finish_kernel(recv, out, ratio):
    for k, n in ((0, 128), (128, 128), (256, 80)):
        total = recv[0, k : k + n, :].astype(F32)
        for src in range(1, PARTS):
            total = total + recv[src, k : k + n, :].astype(F32)
        if n == 128:
            out[:, k : k + n] = total.T.astype(BF16)
        else:
            tail = total[64:67, :]
            ratio[...] = ((tail[2:3, :] + tail[1:2, :]) + tail[0:1, :]) * (1.0 / HQ)
            out[:, k : k + 64] = total[0:64, :].T.astype(BF16)


def params(mib):
    return pltpu.CompilerParams(vmem_limit_bytes=mib * 1024 * 1024)


def shape(dims, dtype):
    return jax.ShapeDtypeStruct(dims, dtype)


def whole():
    return pl.BlockSpec(memory_space=VMEM)


def local(
    hidden,
    norm_gain,
    query_gain,
    key_gain,
    base_query,
    base_key,
    base_value,
    base_output,
    delta_query,
    scale_query,
    key_delta_codes,
    key_scale_codes,
    value_delta_codes,
    value_scale_codes,
    delta_output,
    scale_output,
    cache_keys,
    cache_values,
    lengths,
    stale_rows,
    stale_steps,
    stale_back,
):
    packed = pl.pallas_call(
        pack_kernel,
        name="pack",
        out_shape=shape((PARTS, 6 * CUT, HEAD), BF16),
        in_specs=[whole()] * 8,
        out_specs=whole(),
        scratch_shapes=[VMEM((2, 6 * CUT, HEAD), F32)],
        compiler_params=params(16),
    )(
        delta_query,
        scale_query,
        key_delta_codes,
        key_scale_codes,
        value_delta_codes,
        value_scale_codes,
        delta_output,
        scale_output,
    )
    arrived = lax.all_to_all(packed, "shard", split_axis=0, concat_axis=0, tiled=False)
    arrived, hidden, lengths, stale_rows, stale_steps, stale_back = lax.optimization_barrier(
        (arrived, hidden, lengths, stale_rows, stale_steps, stale_back)
    )
    block = lax.axis_index("replica").astype(jnp.int32).reshape(1)
    fresh_rows = pl.pallas_call(
        refresh_kernel,
        name="refresh",
        out_shape=shape((OWN, COLS), BF16),
        grid_spec=pltpu.PrefetchScalarGridSpec(
            num_scalar_prefetch=1,
            grid=(1,),
            in_specs=[
                pl.BlockSpec((PARTS, 6 * CUT, HEAD), lambda i, b: (0, 0, 0)),
                pl.BlockSpec((OWN, 256), lambda i, b: (b[0], 0)),
                pl.BlockSpec((OWN, 128), lambda i, b: (b[0], 0)),
                pl.BlockSpec((OWN, 128), lambda i, b: (b[0], 0)),
                pl.BlockSpec((OWN, 256), lambda i, b: (b[0], 0)),
            ],
            out_specs=pl.BlockSpec((OWN, COLS), lambda i, b: (0, 0)),
            scratch_shapes=[VMEM((2, 6 * CUT, HEAD), F32), VMEM((OWN, COLS), F32)],
        ),
        compiler_params=params(16),
    )(block, arrived, base_query, base_key, base_value, base_output)
    weight = lax.all_gather(fresh_rows, "replica", axis=0, tiled=True)

    mine = hidden.reshape(TOKENS, OWN).T
    spread = jnp.broadcast_to(mine[None], (PARTS, OWN, TOKENS))
    xt = lax.all_to_all(spread, "shard", split_axis=0, concat_axis=0, tiled=False)
    xt = xt.reshape(WIDTH, TOKENS)

    position = (lengths[None, :] + jnp.arange(STEPS)[:, None]).reshape(TOKENS)
    freq = THETA ** (-(jnp.arange(HEAD // 2).astype(F32) * 2.0) / HEAD)
    angle = position.astype(F32)[:, None] * freq
    cos, sin = jnp.cos(angle), jnp.sin(angle)
    cosine = jnp.concatenate([cos, cos], axis=1)
    sine = jnp.concatenate([-sin, sin], axis=1)
    lens = jnp.broadcast_to(lengths[:, None], (ROWS, HEAD))

    rows_s, steps_s, back_s = stale_rows, stale_steps, stale_back
    lens_s = jnp.sum(
        jnp.where(rows_s[0][None, :] == jnp.arange(ROWS)[:, None], lengths[:, None], 0),
        axis=0,
        keepdims=True,
    )
    at = lens_s + steps_s - back_s % (lens_s + steps_s + 1)
    place = jnp.where(
        at >= lens_s, ROWS * CTX + (at - lens_s) * ROWS + rows_s, rows_s * CTX + at
    ).astype(jnp.int32)
    token = (steps_s * ROWS + rows_s).astype(jnp.int32)

    query_gain = query_gain.reshape(1, HEAD)
    key_gain = key_gain.reshape(1, HEAD)
    cache = cache_keys.reshape(ROWS * CTX, HEAD)
    values = cache_values.reshape(ROWS * CTX, HEAD)

    normed, keys, one_q, one_f, old = pl.pallas_call(
        prepare_kernel,
        name="prepare",
        out_shape=(
            shape((TOKENS, WIDTH), BF16),
            shape((TOKENS, HEAD), F32),
            shape((TOKENS, TOKENS), BF16),
            shape((TOKENS, TOKENS), BF16),
            shape((2, TOKENS, HEAD), F32),
        ),
        in_specs=[whole()] * 12,
        out_specs=(whole(),) * 5,
        scratch_shapes=[
            VMEM((1, TOKENS), F32),
            VMEM((2 * TOKENS, HEAD), F32),
            VMEM((2 * TOKENS, HEAD), F32),
        ],
        compiler_params=params(32),
    )(
        xt, norm_gain.reshape(1, WIDTH), query_gain, key_gain, cosine, sine, lens, token, place,
        base_query, base_key, cache,
    )

    parts = pl.pallas_call(
        main_kernel,
        name="attend",
        out_shape=shape((PARTS, OWN + TAIL, TOKENS), BF16),
        in_specs=[whole(), pl.BlockSpec(memory_space=pl.ANY)] + [whole()] * 11,
        out_specs=whole(),
        scratch_shapes=[
            VMEM((WIDTH, COLS), BF16),
            VMEM((2 * TOKENS, HEAD), F32),
            VMEM((2 * TOKENS, HEAD), F32),
            VMEM((2 * TOKENS, HEAD), F32),
            pltpu.SemaphoreType.DMA((CHUNKS,)),
        ],
        compiler_params=params(40),
    )(normed, weight, query_gain, key_gain, cosine, sine, lens, cache, values, keys, one_q, one_f, old)

    landed = lax.all_to_all(parts, "shard", split_axis=0, concat_axis=0, tiled=False)
    out, ratio = pl.pallas_call(
        finish_kernel,
        name="finish",
        out_shape=(shape((TOKENS, OWN), BF16), shape((1, TOKENS), F32)),
        in_specs=[whole()],
        out_specs=(whole(), whole()),
        compiler_params=params(16),
    )(landed)
    return out.reshape(STEPS, ROWS, OWN), ratio


def solution(mesh):
    return jax.shard_map(
        local,
        mesh=mesh,
        in_specs=(
            P(None, "replica", "shard"),
            P(),
            P(),
            P(),
            P(None, "shard"),
            P(None, "shard"),
            P(None, "shard"),
            P(None, "shard"),
            P(("replica", "shard"), None),
            P(("replica", "shard"), None),
            P(("replica", "shard"), None),
            P(("replica", "shard"), None),
            P(("replica", "shard"), None),
            P(("replica", "shard"), None),
            P(("replica", "shard"), None),
            P(("replica", "shard"), None),
            P("replica", None, "shard"),
            P("replica", None, "shard"),
            P("replica"),
            P("replica", None),
            P("replica", None),
            P("replica", None),
        ),
        out_specs=(P(None, "replica", "shard"), P("replica", None)),
        check_vma=False,
    )
```

```python
import jax
import jax.numpy as jnp
from jax import lax
from jax.experimental import pallas as pl
from jax.experimental.pallas import tpu as pltpu
from jax.sharding import PartitionSpec as P

HQ = 32
HEAD = 128
WIDTH = 5120
STEPS = 4
ROWS = 32
TOKENS = STEPS * ROWS
CTX = 64
PARTS = 16
OWN = WIDTH // PARTS
CUT = 20
COLS = 768
GROUP = 8
GROUPS = ROWS // GROUP
TAIL = 16
EPSILON = 1e-06
THETA = 1000000.0
SCALE = HEAD ** (-0.5)
NEG = -1e30
TILES = ((0, 128), (128, 128), (256, 64))
BLOCK = 448
THIRDS = ((0, 112), (112, 112), (224, 96))
F32 = jnp.float32
BF16 = jnp.bfloat16
VMEM = pltpu.VMEM


PIECES = []
PLACES = []
for _dc in range(2):
    for _dx in range(2):
        for _dy in range(4):
            _rows = THIRDS if (_dx, _dy) == (1, 2) else ((0, OWN),)
            PLACES.append(((_dx, _dy, _dc), tuple(range(len(PIECES), len(PIECES) + len(_rows)))))
            PIECES += [((_dx, _dy, _dc), r) for r in _rows]


def fetch(value, dx, dy, dc):
    pairs = []
    for i in range(16):
        x, y, c = i >> 3, (i >> 1) & 3, i & 1
        pairs.append((((x ^ dx) << 3) + (((y + dy) & 3) << 1) + (c ^ dc), i))
    return lax.ppermute(value, "replica", pairs)


def gather_pieces(own):
    held = {(0, 0): [own]}
    over = fetch(own, 1, 0, 0)
    up = fetch(own, 0, 1, 0)
    down = fetch(own, 0, -1, 0)
    held[1, 0], held[0, 1], held[0, 3] = [over], [up], [down]
    far = fetch(up, 0, 1, 0)
    over_up = fetch(up, 1, 0, 0)
    over_down = fetch(over, 0, -1, 0)
    held[0, 2], held[1, 1], held[1, 3] = [far], [over_up], [over_down]
    cuts = [slice(at, at + n) for at, n in THIRDS]
    held[1, 2] = [
        fetch(far[cuts[0]], 1, 0, 0),
        fetch(over_up[cuts[1]], 0, 1, 0),
        fetch(over_down[cuts[2]], 0, -1, 0),
    ]
    same = [v for dx in range(2) for dy in range(4) for v in held[dx, dy]]
    return same + [fetch(v, 0, 0, 1) for v in same]


def factors(codes):
    out = jnp.ones(codes.shape, F32)
    for bit in range(5):
        out = out * jnp.where((codes >> bit) & 1 == 1, F32(2.0 ** -(2**bit)), F32(1.0))
    return out


def pack_kernel(hidden, dq, dk, dv, do, scales, out, buf):
    factor = factors(scales[...])

    def piece(codes, head, column):
        value = codes[:, head * HEAD : (head + 1) * HEAD].astype(F32)
        return value * factor[:, column : column + 1]

    for at, n in TILES:
        buf[at : at + n, :] = hidden[:, at : at + n].astype(F32).T
    mine = buf[0:OWN, :].astype(BF16)
    buf[OWN + 6 * CUT : BLOCK, :] = jnp.zeros((BLOCK - OWN - 6 * CUT, HEAD), F32)
    for dest in range(PARTS):
        half = dest // 2
        pieces = (
            piece(dq, 2 * dest, 2 * dest),
            piece(dq, 2 * dest + 1, 2 * dest + 1),
            piece(dk, half, 32 + half),
            piece(dv, half, 40 + half),
            piece(do, 2 * dest, 48 + 2 * dest),
            piece(do, 2 * dest + 1, 49 + 2 * dest),
        )
        for c, value in enumerate(pieces):
            buf[OWN + CUT * c : OWN + CUT * (c + 1), :] = value
        out[dest, 0:OWN, :] = mine
        out[dest, OWN:BLOCK, :] = buf[OWN:BLOCK, :].astype(BF16)


def refresh_kernel(block, recv, bq, bk, bv, bo, out, buf, delta):
    for src in range(PARTS):
        buf[src % 2] = recv[src, OWN:BLOCK, :].astype(F32)
        for c in range(6):
            delta[CUT * src : CUT * (src + 1), HEAD * c : HEAD * (c + 1)] = buf[
                src % 2, CUT * c : CUT * (c + 1), :
            ]
    out[:, 0:256] = (bq[...].astype(F32) + delta[:, 0:256]).astype(BF16)
    out[:, 256:384] = (bk[...].astype(F32) + delta[:, 256:384]).astype(BF16)
    out[:, 384:512] = (bv[...].astype(F32) + delta[:, 384:512]).astype(BF16)
    out[:, 512:768] = (bo[...].astype(F32) + delta[:, 512:768]).astype(BF16)


def dot_nt(a, b):
    return lax.dot_general(a, b, (((1,), (1,)), ((), ())), preferred_element_type=F32)


def dot(a, b):
    return jnp.dot(a, b, preferred_element_type=F32)


def head_norm_rotate(raw, gain, cosine, sine):
    value = raw * lax.rsqrt(jnp.mean(raw * raw, axis=-1, keepdims=True) + EPSILON) * gain
    swapped = jnp.concatenate([value[:, HEAD // 2 :], value[:, : HEAD // 2]], axis=-1)
    return value * cosine + swapped * sine


def group_scores(group, query, cache, fresh, lens):
    picked = [
        query[h * TOKENS + t * ROWS + group * GROUP : h * TOKENS + t * ROWS + (group + 1) * GROUP, :]
        for h in range(2)
        for t in range(STEPS)
    ]
    q = jnp.concatenate(picked, axis=0).astype(BF16)
    past = dot_nt(q, cache) * SCALE
    new = dot_nt(q, fresh) * SCALE
    n = 2 * STEPS * GROUP
    length = jnp.concatenate([lens[group * GROUP : (group + 1) * GROUP, :]] * (2 * STEPS), axis=0)
    column = lax.broadcasted_iota(jnp.int32, past.shape, 1)
    line = lax.broadcasted_iota(jnp.int32, past.shape, 0)
    past_ok = ((column >> 6) == (line & 7)) & ((column & 63) < length[:, 0:1])
    column = lax.broadcasted_iota(jnp.int32, (n, TOKENS), 1)
    line = lax.broadcasted_iota(jnp.int32, (n, TOKENS), 0)
    new_ok = ((column & 31) == group * GROUP + (line & 7)) & ((column >> 5) <= ((line >> 3) & 3))
    past = jnp.where(past_ok, past, NEG)
    new = jnp.where(new_ok, new, NEG)
    top = jnp.maximum(
        jnp.max(past, axis=-1, keepdims=True), jnp.max(new, axis=-1, keepdims=True)
    )
    past = jnp.exp(past - top)
    new = jnp.exp(new - top)
    total = jnp.sum(past, axis=-1, keepdims=True) + jnp.sum(new, axis=-1, keepdims=True)
    return past, new, total, top + jnp.log(total)


def put_groups(group, ref, value):
    for h in range(2):
        for t in range(STEPS):
            at = h * TOKENS + t * ROWS + group * GROUP
            i = (h * STEPS + t) * GROUP
            ref[at : at + GROUP, :] = value[i : i + GROUP, :]


def sample_logp(query, keys, one_query, lse):
    out = []
    for h in range(2):
        q = dot(one_query, query[h * TOKENS : (h + 1) * TOKENS, :].astype(BF16))
        score = jnp.sum(q * keys, axis=-1, keepdims=True) * SCALE
        line = lse[h * TOKENS : (h + 1) * TOKENS, :].T
        picked = jnp.sum(one_query.astype(F32) * line, axis=-1, keepdims=True)
        out.append(jnp.broadcast_to(score - picked, (TOKENS, HEAD)))
    return out


def prepare_kernel(
    recv, gain, qg, kg, cosine, sine, lens, token, place, base_q, base_k, cache,
    normed, keys_out, one_q_out, one_f_out, old_out,
    query, lse,
):
    total = jnp.zeros((1, TOKENS), F32)
    for src in range(PARTS):
        x = recv[src, 0:OWN, :].astype(F32)
        total = total + jnp.sum(x * x, axis=0, keepdims=True)
    scale = lax.rsqrt(total * (1.0 / WIDTH) + EPSILON)
    for src in range(PARTS):
        for at, n in TILES:
            x = recv[src, at : at + n, :].astype(F32) * scale
            normed[src, :, at : at + n] = (x.T * gain[src : src + 1, at : at + n]).astype(BF16)
    raw = jnp.zeros((TOKENS, 256), F32)
    raw_k = jnp.zeros((TOKENS, HEAD), F32)
    for src in range(PARTS):
        raw = raw + dot(normed[src], base_q[src * OWN : (src + 1) * OWN, :])
        raw_k = raw_k + dot(normed[src], base_k[src * OWN : (src + 1) * OWN, :])
    cos, sin = cosine[...], sine[...]
    for h in range(2):
        query[h * TOKENS : (h + 1) * TOKENS, :] = (
            head_norm_rotate(raw[:, h * HEAD : (h + 1) * HEAD], qg[...], cos, sin)
            .astype(BF16)
            .astype(F32)
        )
    fresh = head_norm_rotate(raw_k, kg[...], cos, sin).astype(BF16)
    for g in range(GROUPS):
        _, _, _, log_sum = group_scores(
            g, query, cache[g * GROUP * CTX : (g + 1) * GROUP * CTX, :], fresh, lens
        )
        put_groups(g, lse, jnp.broadcast_to(log_sum, (log_sum.shape[0], HEAD)))
    tokens = jnp.broadcast_to(token[...], (TOKENS, TOKENS)).T
    places = jnp.broadcast_to(place[...], (TOKENS, TOKENS)).T
    lane = lax.broadcasted_iota(jnp.int32, (TOKENS, TOKENS), 1)
    one_q = jnp.where(tokens == lane, F32(1.0), F32(0.0)).astype(BF16)
    one_f = jnp.where(places == lane + ROWS * CTX, F32(1.0), F32(0.0)).astype(BF16)
    keys = jnp.zeros((TOKENS, HEAD), F32)
    for k in range(ROWS * CTX // HEAD):
        one = jnp.where(places == lane + k * HEAD, F32(1.0), F32(0.0)).astype(BF16)
        keys = keys + dot(one, cache[k * HEAD : (k + 1) * HEAD, :])
    keys_out[...] = keys
    one_q_out[...] = one_q
    one_f_out[...] = one_f
    old = sample_logp(query, keys + dot(one_f, fresh), one_q, lse)
    old_out[0] = old[0]
    old_out[1] = old[1]


def main_kernel(
    here, normed, qg, kg, cosine, sine, lens, cache_hbm, values_hbm, keys, one_q, one_f, old,
    *rest,
):
    pieces = rest[: len(PIECES)]
    out, cache, values, query, lse, mixed, sems = rest[len(PIECES) :]
    copies = (
        pltpu.make_async_copy(cache_hbm, cache, sems.at[0]),
        pltpu.make_async_copy(values_hbm, values, sems.at[1]),
    )
    for copy in copies:
        copy.start()
    me = here[0]

    def owner(place):
        dx, dy, dc = place
        return (((me >> 3) ^ dx) << 3) + ((((me >> 1) + dy) & 3) << 1) + ((me & 1) ^ dc)

    raw = jnp.zeros((TOKENS, 512), F32)
    for place, parts in PLACES:
        block = owner(place)
        if len(parts) == 1:
            raw = raw + dot(normed[block], pieces[parts[0]][:, 0:512])
        else:
            whole_block = jnp.concatenate([pieces[i][:, 0:512] for i in parts], axis=0)
            raw = raw + dot(normed[block], whole_block)
    cos, sin = cosine[...], sine[...]
    for h in range(2):
        query[h * TOKENS : (h + 1) * TOKENS, :] = (
            head_norm_rotate(raw[:, h * HEAD : (h + 1) * HEAD], qg[...], cos, sin)
            .astype(BF16)
            .astype(F32)
        )
    fresh = head_norm_rotate(raw[:, 256:384], kg[...], cos, sin).astype(BF16)
    fresh_v = raw[:, 384:512].astype(BF16)
    for copy in copies:
        copy.wait()
    for g in range(GROUPS):
        at = slice(g * GROUP * CTX, (g + 1) * GROUP * CTX)
        past, new, total, log_sum = group_scores(g, query, cache[at, :], fresh, lens)
        put_groups(g, lse, jnp.broadcast_to(log_sum, (log_sum.shape[0], HEAD)))
        mix = dot((past / total).astype(BF16), values[at, :])
        mix = mix + dot((new / total).astype(BF16), fresh_v)
        put_groups(g, mixed, mix)
    attended = jnp.concatenate([mixed[0:TOKENS, :], mixed[TOKENS:, :]], axis=1).astype(BF16)
    for place, parts in PLACES:
        block = owner(place)
        for i in parts:
            at, n = PIECES[i][1]
            part = dot_nt(pieces[i][:, 512:768], attended)
            out[block, at : at + n, :] = part.astype(BF16)
    now = sample_logp(query, keys[...] + dot(one_f[...], fresh), one_q[...], lse)
    term = (now[0] - old[0]) + (now[1] - old[1])
    line = term.T[0:1, :]
    high = line.astype(BF16).astype(F32)
    middle = (line - high).astype(BF16).astype(F32)
    low = line - high - middle
    tail = jnp.concatenate([high, middle, low, jnp.zeros((TAIL - 3, TOKENS), F32)], axis=0)
    tail = tail.astype(BF16)
    for p in range(PARTS):
        out[p, OWN : OWN + TAIL, :] = tail


def finish_kernel(recv, out, ratio):
    for k, n in ((0, 128), (128, 128), (256, 80)):
        total = recv[0, k : k + n, :].astype(F32)
        for src in range(1, PARTS):
            total = total + recv[src, k : k + n, :].astype(F32)
        if n == 128:
            out[:, k : k + n] = total.T.astype(BF16)
        else:
            tail = total[64:67, :]
            ratio[...] = ((tail[2:3, :] + tail[1:2, :]) + tail[0:1, :]) * (1.0 / HQ)
            out[:, k : k + 64] = total[0:64, :].T.astype(BF16)


def params(mib):
    return pltpu.CompilerParams(vmem_limit_bytes=mib * 1024 * 1024)


def shape(dims, dtype):
    return jax.ShapeDtypeStruct(dims, dtype)


def block(dims):
    return pl.BlockSpec(dims, lambda i: (0,) * len(dims))


def whole():
    return pl.BlockSpec(memory_space=VMEM)


def local(
    hidden,
    norm_gain,
    query_gain,
    key_gain,
    base_query,
    base_key,
    base_value,
    base_output,
    delta_query,
    scale_query,
    key_delta_codes,
    key_scale_codes,
    value_delta_codes,
    value_scale_codes,
    delta_output,
    scale_output,
    cache_keys,
    cache_values,
    lengths,
    stale_rows,
    stale_steps,
    stale_back,
):
    scales = jnp.concatenate([scale_query, key_scale_codes, value_scale_codes, scale_output], axis=1)
    packed = pl.pallas_call(
        pack_kernel,
        name="pack",
        out_shape=shape((PARTS, BLOCK, HEAD), BF16),
        grid=(1,),
        in_specs=[block((TOKENS, OWN)), block((CUT, 4096)), block((CUT, 1024)), block((CUT, 1024)), block((CUT, 4096)), block((CUT, 80))],
        out_specs=whole(),
        scratch_shapes=[VMEM((BLOCK, HEAD), F32)],
        compiler_params=params(8),
    )(hidden.reshape(TOKENS, OWN), delta_query, key_delta_codes, value_delta_codes, delta_output, scales)
    arrived = lax.all_to_all(packed, "shard", split_axis=0, concat_axis=0, tiled=False)
    arrived, lengths, stale_rows, stale_steps, stale_back = lax.optimization_barrier(
        (arrived, lengths, stale_rows, stale_steps, stale_back)
    )
    here = lax.axis_index("replica").astype(jnp.int32).reshape(1)
    fresh_rows = pl.pallas_call(
        refresh_kernel,
        name="refresh",
        out_shape=shape((OWN, COLS), BF16),
        grid_spec=pltpu.PrefetchScalarGridSpec(
            num_scalar_prefetch=1,
            grid=(1,),
            in_specs=[
                whole(),
                pl.BlockSpec((OWN, 256), lambda i, b: (b[0], 0)),
                pl.BlockSpec((OWN, 128), lambda i, b: (b[0], 0)),
                pl.BlockSpec((OWN, 128), lambda i, b: (b[0], 0)),
                pl.BlockSpec((OWN, 256), lambda i, b: (b[0], 0)),
            ],
            out_specs=whole(),
            scratch_shapes=[VMEM((2, BLOCK - OWN, HEAD), F32), VMEM((OWN, COLS), F32)],
        ),
        compiler_params=params(8),
    )(here, arrived, base_query, base_key, base_value, base_output)
    pieces = gather_pieces(fresh_rows)

    position = (lengths[None, :] + jnp.arange(STEPS)[:, None]).reshape(TOKENS)
    freq = THETA ** (-(jnp.arange(HEAD // 2).astype(F32) * 2.0) / HEAD)
    angle = position.astype(F32)[:, None] * freq
    cos, sin = jnp.cos(angle), jnp.sin(angle)
    cosine = jnp.concatenate([cos, cos], axis=1)
    sine = jnp.concatenate([-sin, sin], axis=1)
    lens = jnp.broadcast_to(lengths[:, None], (ROWS, HEAD))

    rows_s, steps_s, back_s = stale_rows, stale_steps, stale_back
    lens_s = jnp.sum(
        jnp.where(rows_s[0][None, :] == jnp.arange(ROWS)[:, None], lengths[:, None], 0),
        axis=0,
        keepdims=True,
    )
    at = lens_s + steps_s - back_s % (lens_s + steps_s + 1)
    place = jnp.where(
        at >= lens_s, ROWS * CTX + (at - lens_s) * ROWS + rows_s, rows_s * CTX + at
    ).astype(jnp.int32)
    token = (steps_s * ROWS + rows_s).astype(jnp.int32)

    query_gain = query_gain.reshape(1, HEAD)
    key_gain = key_gain.reshape(1, HEAD)
    cache = cache_keys.reshape(ROWS * CTX, HEAD)
    values = cache_values.reshape(ROWS * CTX, HEAD)

    normed, keys, one_q, one_f, old = pl.pallas_call(
        prepare_kernel,
        name="prepare",
        out_shape=(
            shape((PARTS, TOKENS, OWN), BF16),
            shape((TOKENS, HEAD), F32),
            shape((TOKENS, TOKENS), BF16),
            shape((TOKENS, TOKENS), BF16),
            shape((2, TOKENS, HEAD), F32),
        ),
        grid=(1,),
        in_specs=[
            whole(),
            block((PARTS, OWN)),
            block((1, HEAD)),
            block((1, HEAD)),
            block((TOKENS, HEAD)),
            block((TOKENS, HEAD)),
            block((ROWS, HEAD)),
            block((1, TOKENS)),
            block((1, TOKENS)),
            block((WIDTH, 256)),
            block((WIDTH, HEAD)),
            block((ROWS * CTX, HEAD)),
        ],
        out_specs=(whole(),) * 5,
        scratch_shapes=[VMEM((2 * TOKENS, HEAD), F32), VMEM((2 * TOKENS, HEAD), F32)],
        compiler_params=params(20),
    )(
        arrived, norm_gain.reshape(PARTS, OWN), query_gain, key_gain, cosine, sine, lens, token, place,
        base_query, base_key, cache,
    )

    anywhere = pl.BlockSpec(memory_space=pl.ANY)
    parts = pl.pallas_call(
        main_kernel,
        name="attend",
        out_shape=shape((PARTS, OWN + TAIL, TOKENS), BF16),
        in_specs=[pl.BlockSpec(memory_space=pltpu.SMEM)]
        + [whole()] * 6
        + [anywhere] * 2
        + [whole()] * (4 + len(PIECES)),
        out_specs=whole(),
        scratch_shapes=[
            VMEM((ROWS * CTX, HEAD), BF16),
            VMEM((ROWS * CTX, HEAD), BF16),
            VMEM((2 * TOKENS, HEAD), F32),
            VMEM((2 * TOKENS, HEAD), F32),
            VMEM((2 * TOKENS, HEAD), F32),
            pltpu.SemaphoreType.DMA((2,)),
        ],
        compiler_params=params(16),
    )(
        here, normed, query_gain, key_gain, cosine, sine, lens, cache, values, keys, one_q, one_f, old,
        *pieces,
    )

    landed = lax.all_to_all(parts, "shard", split_axis=0, concat_axis=0, tiled=False)
    out, ratio = pl.pallas_call(
        finish_kernel,
        name="finish",
        out_shape=(shape((TOKENS, OWN), BF16), shape((1, TOKENS), F32)),
        in_specs=[whole()],
        out_specs=(whole(), whole()),
        compiler_params=params(16),
    )(landed)
    return out.reshape(STEPS, ROWS, OWN), ratio


def solution(mesh):
    return jax.shard_map(
        local,
        mesh=mesh,
        in_specs=(
            P(None, "replica", "shard"),
            P(),
            P(),
            P(),
            P(None, "shard"),
            P(None, "shard"),
            P(None, "shard"),
            P(None, "shard"),
            P(("replica", "shard"), None),
            P(("replica", "shard"), None),
            P(("replica", "shard"), None),
            P(("replica", "shard"), None),
            P(("replica", "shard"), None),
            P(("replica", "shard"), None),
            P(("replica", "shard"), None),
            P(("replica", "shard"), None),
            P("replica", None, "shard"),
            P("replica", None, "shard"),
            P("replica"),
            P("replica", None),
            P("replica", None),
            P("replica", None),
        ),
        out_specs=(P(None, "replica", "shard"), P("replica", None)),
        check_vma=False,
    )
```

```python
import jax
import jax.numpy as jnp
from jax import lax
from jax.experimental import pallas as pl
from jax.experimental.pallas import tpu as pltpu
from jax.sharding import PartitionSpec as P

HQ = 32
HEAD = 128
WIDTH = 5120
STEPS = 4
ROWS = 32
TOKENS = STEPS * ROWS
CTX = 64
PARTS = 16
OWN = WIDTH // PARTS
CUT = 20
COLS = 768
GROUP = 8
GROUPS = ROWS // GROUP
TAIL = 16
EPSILON = 1e-06
THETA = 1000000.0
SCALE = HEAD ** (-0.5)
NEG = -1e30
TILES = ((0, 128), (128, 128), (256, 64))
BLOCK = 128
THIRDS = ((0, 112), (112, 112), (224, 96))
F32 = jnp.float32
BF16 = jnp.bfloat16
VMEM = pltpu.VMEM


PIECES = []
PLACES = []
for _dc in range(2):
    for _dx in range(2):
        for _dy in range(4):
            _rows = THIRDS if (_dx, _dy) == (1, 2) else ((0, OWN),)
            PLACES.append(((_dx, _dy, _dc), tuple(range(len(PIECES), len(PIECES) + len(_rows)))))
            PIECES += [((_dx, _dy, _dc), r) for r in _rows]


def fetch(value, dx, dy, dc):
    pairs = []
    for i in range(16):
        x, y, c = i >> 3, (i >> 1) & 3, i & 1
        pairs.append((((x ^ dx) << 3) + (((y + dy) & 3) << 1) + (c ^ dc), i))
    return lax.ppermute(value, "replica", pairs)


def gather_pieces(own):
    held = {(0, 0): [own]}
    over = fetch(own, 1, 0, 0)
    up = fetch(own, 0, 1, 0)
    down = fetch(own, 0, -1, 0)
    held[1, 0], held[0, 1], held[0, 3] = [over], [up], [down]
    over, up, down = lax.optimization_barrier((over, up, down))
    far = fetch(up, 0, 1, 0)
    over_up = fetch(up, 1, 0, 0)
    over_down = fetch(over, 0, -1, 0)
    far, over_up, over_down = lax.optimization_barrier((far, over_up, over_down))
    held[0, 2], held[1, 1], held[1, 3] = [far], [over_up], [over_down]
    cuts = [slice(at, at + n) for at, n in THIRDS]
    held[1, 2] = [
        fetch(far[cuts[0]], 1, 0, 0),
        fetch(over_up[cuts[1]], 0, 1, 0),
        fetch(over_down[cuts[2]], 0, -1, 0),
    ]
    same = [v for dx in range(2) for dy in range(4) for v in held[dx, dy]]
    return same + [fetch(v, 0, 0, 1) for v in same]


def along_shard(value, dx, dz):
    pairs = [((((i >> 3) ^ dx) << 3) + ((i + dz) & 7), i) for i in range(16)]
    return lax.ppermute(value, "shard", pairs)


def gather_pairs(own):
    pair = jnp.concatenate([own, along_shard(own, 1, 0)], axis=0)
    held = {0: pair}
    up, down = pair, pair
    for k in range(1, 5):
        up = along_shard(up, 0, 1)
        held[k] = up
        if k < 4:
            down = along_shard(down, 0, -1)
            held[8 - k] = down
    return [held[k] for k in range(8)]


def factors(codes):
    out = jnp.ones(codes.shape, F32)
    for bit in range(5):
        out = out * jnp.where((codes >> bit) & 1 == 1, F32(2.0 ** -(2**bit)), F32(1.0))
    return out


def pack_kernel(hidden, dq, dk, dv, do, scales, out, turned, buf):
    factor = factors(scales[...])

    def piece(codes, head, column):
        value = codes[:, head * HEAD : (head + 1) * HEAD].astype(F32)
        return value * factor[:, column : column + 1]

    for at, n in TILES:
        turned[at : at + n, :] = hidden[:, at : at + n].astype(F32).T.astype(BF16)
    buf[6 * CUT : BLOCK, :] = jnp.zeros((BLOCK - 6 * CUT, HEAD), F32)
    for dest in range(PARTS):
        half = dest // 2
        pieces = (
            piece(dq, 2 * dest, 2 * dest),
            piece(dq, 2 * dest + 1, 2 * dest + 1),
            piece(dk, half, 32 + half),
            piece(dv, half, 40 + half),
            piece(do, 2 * dest, 48 + 2 * dest),
            piece(do, 2 * dest + 1, 49 + 2 * dest),
        )
        for c, value in enumerate(pieces):
            buf[CUT * c : CUT * (c + 1), :] = value
        out[dest] = buf[...].astype(BF16)


def refresh_kernel(block, recv, bq, bk, bv, bo, out, buf, delta):
    for src in range(PARTS):
        buf[src % 2] = recv[src].astype(F32)
        for c in range(6):
            delta[CUT * src : CUT * (src + 1), HEAD * c : HEAD * (c + 1)] = buf[
                src % 2, CUT * c : CUT * (c + 1), :
            ]
    out[:, 0:256] = (bq[...].astype(F32) + delta[:, 0:256]).astype(BF16)
    out[:, 256:384] = (bk[...].astype(F32) + delta[:, 256:384]).astype(BF16)
    out[:, 384:512] = (bv[...].astype(F32) + delta[:, 384:512]).astype(BF16)
    out[:, 512:768] = (bo[...].astype(F32) + delta[:, 512:768]).astype(BF16)


def dot_nt(a, b):
    return lax.dot_general(a, b, (((1,), (1,)), ((), ())), preferred_element_type=F32)


def dot(a, b):
    return jnp.dot(a, b, preferred_element_type=F32)


def head_norm_rotate(raw, gain, cosine, sine):
    value = raw * lax.rsqrt(jnp.mean(raw * raw, axis=-1, keepdims=True) + EPSILON) * gain
    swapped = jnp.concatenate([value[:, HEAD // 2 :], value[:, : HEAD // 2]], axis=-1)
    return value * cosine + swapped * sine


def group_scores(group, query, cache, fresh, lens):
    picked = [
        query[h * TOKENS + t * ROWS + group * GROUP : h * TOKENS + t * ROWS + (group + 1) * GROUP, :]
        for h in range(2)
        for t in range(STEPS)
    ]
    q = jnp.concatenate(picked, axis=0).astype(BF16)
    past = dot_nt(q, cache) * SCALE
    new = dot_nt(q, fresh) * SCALE
    n = 2 * STEPS * GROUP
    length = jnp.concatenate([lens[group * GROUP : (group + 1) * GROUP, :]] * (2 * STEPS), axis=0)
    column = lax.broadcasted_iota(jnp.int32, past.shape, 1)
    line = lax.broadcasted_iota(jnp.int32, past.shape, 0)
    past_ok = ((column >> 6) == (line & 7)) & ((column & 63) < length[:, 0:1])
    column = lax.broadcasted_iota(jnp.int32, (n, TOKENS), 1)
    line = lax.broadcasted_iota(jnp.int32, (n, TOKENS), 0)
    new_ok = ((column & 31) == group * GROUP + (line & 7)) & ((column >> 5) <= ((line >> 3) & 3))
    past = jnp.where(past_ok, past, NEG)
    new = jnp.where(new_ok, new, NEG)
    top = jnp.maximum(
        jnp.max(past, axis=-1, keepdims=True), jnp.max(new, axis=-1, keepdims=True)
    )
    past = jnp.exp(past - top)
    new = jnp.exp(new - top)
    total = jnp.sum(past, axis=-1, keepdims=True) + jnp.sum(new, axis=-1, keepdims=True)
    return past, new, total, top + jnp.log(total)


def put_groups(group, ref, value):
    for h in range(2):
        for t in range(STEPS):
            at = h * TOKENS + t * ROWS + group * GROUP
            i = (h * STEPS + t) * GROUP
            ref[at : at + GROUP, :] = value[i : i + GROUP, :]


def sample_logp(query, keys, one_query, lse):
    out = []
    for h in range(2):
        q = dot(one_query, query[h * TOKENS : (h + 1) * TOKENS, :].astype(BF16))
        score = jnp.sum(q * keys, axis=-1, keepdims=True) * SCALE
        line = lse[h * TOKENS : (h + 1) * TOKENS, :].T
        picked = jnp.sum(one_query.astype(F32) * line, axis=-1, keepdims=True)
        out.append(jnp.broadcast_to(score - picked, (TOKENS, HEAD)))
    return out


def prepare_kernel(
    seat, gain, qg, kg, cosine, sine, lens, token, place, base_q, base_k, cache,
    p0, p1, p2, p3, p4, p5, p6, p7, normed, keys_out, one_q_out, one_f_out, old_out,
    query, lse,
):
    total = jnp.zeros((1, TOKENS), F32)
    pairs = (p0, p1, p2, p3, p4, p5, p6, p7)
    for pair in pairs:
        x = pair[...].astype(F32)
        total = total + jnp.sum(x * x, axis=0, keepdims=True)
    scale = lax.rsqrt(total * (1.0 / WIDTH) + EPSILON)
    me = seat[0]
    for step, pair in enumerate(pairs):
        for half in range(2):
            src = (((me >> 3) ^ half) << 3) + ((me + step) & 7)
            for at, n in TILES:
                x = pair[half * OWN + at : half * OWN + at + n, :].astype(F32) * scale
                normed[src, :, at : at + n] = (x.T * gain[src, :, at : at + n]).astype(BF16)
    raw = jnp.zeros((TOKENS, 256), F32)
    raw_k = jnp.zeros((TOKENS, HEAD), F32)
    for src in range(PARTS):
        raw = raw + dot(normed[src], base_q[src * OWN : (src + 1) * OWN, :])
        raw_k = raw_k + dot(normed[src], base_k[src * OWN : (src + 1) * OWN, :])
    cos, sin = cosine[...], sine[...]
    for h in range(2):
        query[h * TOKENS : (h + 1) * TOKENS, :] = (
            head_norm_rotate(raw[:, h * HEAD : (h + 1) * HEAD], qg[...], cos, sin)
            .astype(BF16)
            .astype(F32)
        )
    fresh = head_norm_rotate(raw_k, kg[...], cos, sin).astype(BF16)
    for g in range(GROUPS):
        _, _, _, log_sum = group_scores(
            g, query, cache[g * GROUP * CTX : (g + 1) * GROUP * CTX, :], fresh, lens
        )
        put_groups(g, lse, jnp.broadcast_to(log_sum, (log_sum.shape[0], HEAD)))
    tokens = jnp.broadcast_to(token[...], (TOKENS, TOKENS)).T
    places = jnp.broadcast_to(place[...], (TOKENS, TOKENS)).T
    lane = lax.broadcasted_iota(jnp.int32, (TOKENS, TOKENS), 1)
    one_q = jnp.where(tokens == lane, F32(1.0), F32(0.0)).astype(BF16)
    one_f = jnp.where(places == lane + ROWS * CTX, F32(1.0), F32(0.0)).astype(BF16)
    keys = jnp.zeros((TOKENS, HEAD), F32)
    for k in range(ROWS * CTX // HEAD):
        one = jnp.where(places == lane + k * HEAD, F32(1.0), F32(0.0)).astype(BF16)
        keys = keys + dot(one, cache[k * HEAD : (k + 1) * HEAD, :])
    keys_out[...] = keys
    one_q_out[...] = one_q
    one_f_out[...] = one_f
    old = sample_logp(query, keys + dot(one_f, fresh), one_q, lse)
    old_out[0] = old[0]
    old_out[1] = old[1]


def main_kernel(
    here, normed, qg, kg, cosine, sine, lens, cache_hbm, values_hbm, keys, one_q, one_f, old,
    *rest,
):
    pieces = rest[: len(PIECES)]
    out, cache, values, query, lse, mixed, sems = rest[len(PIECES) :]
    copies = (
        pltpu.make_async_copy(cache_hbm, cache, sems.at[0]),
        pltpu.make_async_copy(values_hbm, values, sems.at[1]),
    )
    for copy in copies:
        copy.start()
    me = here[0]

    def owner(place):
        dx, dy, dc = place
        return (((me >> 3) ^ dx) << 3) + ((((me >> 1) + dy) & 3) << 1) + ((me & 1) ^ dc)

    raw = jnp.zeros((TOKENS, 512), F32)
    for place, parts in PLACES:
        block = owner(place)
        if len(parts) == 1:
            raw = raw + dot(normed[block], pieces[parts[0]][:, 0:512])
        else:
            whole_block = jnp.concatenate([pieces[i][:, 0:512] for i in parts], axis=0)
            raw = raw + dot(normed[block], whole_block)
    cos, sin = cosine[...], sine[...]
    for h in range(2):
        query[h * TOKENS : (h + 1) * TOKENS, :] = (
            head_norm_rotate(raw[:, h * HEAD : (h + 1) * HEAD], qg[...], cos, sin)
            .astype(BF16)
            .astype(F32)
        )
    fresh = head_norm_rotate(raw[:, 256:384], kg[...], cos, sin).astype(BF16)
    fresh_v = raw[:, 384:512].astype(BF16)
    for copy in copies:
        copy.wait()
    for g in range(GROUPS):
        at = slice(g * GROUP * CTX, (g + 1) * GROUP * CTX)
        past, new, total, log_sum = group_scores(g, query, cache[at, :], fresh, lens)
        put_groups(g, lse, jnp.broadcast_to(log_sum, (log_sum.shape[0], HEAD)))
        mix = dot((past / total).astype(BF16), values[at, :])
        mix = mix + dot((new / total).astype(BF16), fresh_v)
        put_groups(g, mixed, mix)
    attended = jnp.concatenate([mixed[0:TOKENS, :], mixed[TOKENS:, :]], axis=1).astype(BF16)
    for place, parts in PLACES:
        block = owner(place)
        for i in parts:
            at, n = PIECES[i][1]
            part = dot_nt(pieces[i][:, 512:768], attended)
            out[block, at : at + n, :] = part.astype(BF16)
    now = sample_logp(query, keys[...] + dot(one_f[...], fresh), one_q[...], lse)
    term = (now[0] - old[0]) + (now[1] - old[1])
    line = term.T[0:1, :]
    high = line.astype(BF16).astype(F32)
    middle = (line - high).astype(BF16).astype(F32)
    low = line - high - middle
    tail = jnp.concatenate([high, middle, low, jnp.zeros((TAIL - 3, TOKENS), F32)], axis=0)
    tail = tail.astype(BF16)
    for p in range(PARTS):
        out[p, OWN : OWN + TAIL, :] = tail


def finish_kernel(recv, out, ratio):
    for k, n in ((0, 128), (128, 128), (256, 80)):
        total = recv[0, k : k + n, :].astype(F32)
        for src in range(1, PARTS):
            total = total + recv[src, k : k + n, :].astype(F32)
        if n == 128:
            out[:, k : k + n] = total.T.astype(BF16)
        else:
            tail = total[64:67, :]
            ratio[...] = ((tail[2:3, :] + tail[1:2, :]) + tail[0:1, :]) * (1.0 / HQ)
            out[:, k : k + 64] = total[0:64, :].T.astype(BF16)


def params(mib):
    return pltpu.CompilerParams(vmem_limit_bytes=mib * 1024 * 1024)


def shape(dims, dtype):
    return jax.ShapeDtypeStruct(dims, dtype)


def block(dims):
    return pl.BlockSpec(dims, lambda i: (0,) * len(dims))


def whole():
    return pl.BlockSpec(memory_space=VMEM)


def local(
    hidden,
    norm_gain,
    query_gain,
    key_gain,
    base_query,
    base_key,
    base_value,
    base_output,
    delta_query,
    scale_query,
    key_delta_codes,
    key_scale_codes,
    value_delta_codes,
    value_scale_codes,
    delta_output,
    scale_output,
    cache_keys,
    cache_values,
    lengths,
    stale_rows,
    stale_steps,
    stale_back,
):
    scales = jnp.concatenate([scale_query, key_scale_codes, value_scale_codes, scale_output], axis=1)
    packed, turned = pl.pallas_call(
        pack_kernel,
        name="pack",
        out_shape=(shape((PARTS, BLOCK, HEAD), BF16), shape((OWN, TOKENS), BF16)),
        grid=(1,),
        in_specs=[block((TOKENS, OWN)), block((CUT, 4096)), block((CUT, 1024)), block((CUT, 1024)), block((CUT, 4096)), block((CUT, 80))],
        out_specs=(whole(), whole()),
        scratch_shapes=[VMEM((BLOCK, HEAD), F32)],
        compiler_params=params(8),
    )(hidden.reshape(TOKENS, OWN), delta_query, key_delta_codes, value_delta_codes, delta_output, scales)
    arrived = lax.all_to_all(packed, "shard", split_axis=0, concat_axis=0, tiled=False)
    arrived, turned, lengths, stale_rows, stale_steps, stale_back = lax.optimization_barrier(
        (arrived, turned, lengths, stale_rows, stale_steps, stale_back)
    )
    here = lax.axis_index("replica").astype(jnp.int32).reshape(1)
    fresh_rows = pl.pallas_call(
        refresh_kernel,
        name="refresh",
        out_shape=shape((OWN, COLS), BF16),
        grid_spec=pltpu.PrefetchScalarGridSpec(
            num_scalar_prefetch=1,
            grid=(1,),
            in_specs=[
                whole(),
                pl.BlockSpec((OWN, 256), lambda i, b: (b[0], 0)),
                pl.BlockSpec((OWN, 128), lambda i, b: (b[0], 0)),
                pl.BlockSpec((OWN, 128), lambda i, b: (b[0], 0)),
                pl.BlockSpec((OWN, 256), lambda i, b: (b[0], 0)),
            ],
            out_specs=whole(),
            scratch_shapes=[VMEM((2, BLOCK, HEAD), F32), VMEM((OWN, COLS), F32)],
        ),
        compiler_params=params(8),
    )(here, arrived, base_query, base_key, base_value, base_output)
    pieces = gather_pieces(fresh_rows)
    features = gather_pairs(turned)
    seat = lax.axis_index("shard").astype(jnp.int32).reshape(1)

    position = (lengths[None, :] + jnp.arange(STEPS)[:, None]).reshape(TOKENS)
    freq = THETA ** (-(jnp.arange(HEAD // 2).astype(F32) * 2.0) / HEAD)
    angle = position.astype(F32)[:, None] * freq
    cos, sin = jnp.cos(angle), jnp.sin(angle)
    cosine = jnp.concatenate([cos, cos], axis=1)
    sine = jnp.concatenate([-sin, sin], axis=1)
    lens = jnp.broadcast_to(lengths[:, None], (ROWS, HEAD))

    rows_s, steps_s, back_s = stale_rows, stale_steps, stale_back
    lens_s = jnp.sum(
        jnp.where(rows_s[0][None, :] == jnp.arange(ROWS)[:, None], lengths[:, None], 0),
        axis=0,
        keepdims=True,
    )
    at = lens_s + steps_s - back_s % (lens_s + steps_s + 1)
    place = jnp.where(
        at >= lens_s, ROWS * CTX + (at - lens_s) * ROWS + rows_s, rows_s * CTX + at
    ).astype(jnp.int32)
    token = (steps_s * ROWS + rows_s).astype(jnp.int32)

    query_gain = query_gain.reshape(1, HEAD)
    key_gain = key_gain.reshape(1, HEAD)
    cache = cache_keys.reshape(ROWS * CTX, HEAD)
    values = cache_values.reshape(ROWS * CTX, HEAD)

    normed, keys, one_q, one_f, old = pl.pallas_call(
        prepare_kernel,
        name="prepare",
        out_shape=(
            shape((PARTS, TOKENS, OWN), BF16),
            shape((TOKENS, HEAD), F32),
            shape((TOKENS, TOKENS), BF16),
            shape((TOKENS, TOKENS), BF16),
            shape((2, TOKENS, HEAD), F32),
        ),
        grid=(1,),
        in_specs=[
            pl.BlockSpec(memory_space=pltpu.SMEM),
            block((PARTS, 1, OWN)),
            block((1, HEAD)),
            block((1, HEAD)),
            block((TOKENS, HEAD)),
            block((TOKENS, HEAD)),
            block((ROWS, HEAD)),
            block((1, TOKENS)),
            block((1, TOKENS)),
            block((WIDTH, 256)),
            block((WIDTH, HEAD)),
            block((ROWS * CTX, HEAD)),
        ]
        + [whole()] * 8,
        out_specs=(whole(),) * 5,
        scratch_shapes=[VMEM((2 * TOKENS, HEAD), F32), VMEM((2 * TOKENS, HEAD), F32)],
        compiler_params=params(20),
    )(
        seat, norm_gain.reshape(PARTS, 1, OWN), query_gain, key_gain, cosine, sine, lens, token, place,
        base_query, base_key, cache, *features,
    )

    anywhere = pl.BlockSpec(memory_space=pl.ANY)
    parts = pl.pallas_call(
        main_kernel,
        name="attend",
        out_shape=shape((PARTS, OWN + TAIL, TOKENS), BF16),
        in_specs=[pl.BlockSpec(memory_space=pltpu.SMEM)]
        + [whole()] * 6
        + [anywhere] * 2
        + [whole()] * (4 + len(PIECES)),
        out_specs=whole(),
        scratch_shapes=[
            VMEM((ROWS * CTX, HEAD), BF16),
            VMEM((ROWS * CTX, HEAD), BF16),
            VMEM((2 * TOKENS, HEAD), F32),
            VMEM((2 * TOKENS, HEAD), F32),
            VMEM((2 * TOKENS, HEAD), F32),
            pltpu.SemaphoreType.DMA((2,)),
        ],
        compiler_params=params(16),
    )(
        here, normed, query_gain, key_gain, cosine, sine, lens, cache, values, keys, one_q, one_f, old,
        *pieces,
    )

    landed = lax.all_to_all(parts, "shard", split_axis=0, concat_axis=0, tiled=False)
    out, ratio = pl.pallas_call(
        finish_kernel,
        name="finish",
        out_shape=(shape((TOKENS, OWN), BF16), shape((1, TOKENS), F32)),
        in_specs=[whole()],
        out_specs=(whole(), whole()),
        compiler_params=params(16),
    )(landed)
    return out.reshape(STEPS, ROWS, OWN), ratio


def solution(mesh):
    return jax.shard_map(
        local,
        mesh=mesh,
        in_specs=(
            P(None, "replica", "shard"),
            P(),
            P(),
            P(),
            P(None, "shard"),
            P(None, "shard"),
            P(None, "shard"),
            P(None, "shard"),
            P(("replica", "shard"), None),
            P(("replica", "shard"), None),
            P(("replica", "shard"), None),
            P(("replica", "shard"), None),
            P(("replica", "shard"), None),
            P(("replica", "shard"), None),
            P(("replica", "shard"), None),
            P(("replica", "shard"), None),
            P("replica", None, "shard"),
            P("replica", None, "shard"),
            P("replica"),
            P("replica", None),
            P("replica", None),
            P("replica", None),
        ),
        out_specs=(P(None, "replica", "shard"), P("replica", None)),
        check_vma=False,
    )
```

```python
import jax
import jax.numpy as jnp
from jax import lax
from jax.experimental import pallas as pl
from jax.experimental.pallas import tpu as pltpu
from jax.sharding import PartitionSpec as P

HQ = 32
KV = 8
HEAD = 128
WIDTH = 5120
STEPS = 4
ROWS = 32
TOKENS = STEPS * ROWS
CTX = 64
PARTS = 16
OWN = WIDTH // PARTS
CUT = 20
GROUP = 8
GROUPS = ROWS // GROUP
TAIL = 16
EPSILON = 1e-06
THETA = 1000000.0
SCALE = HEAD ** (-0.5)
NEG = -1e30
TILES = ((0, 128), (128, 128), (256, 64))
BLOCK = 128
HALF = PARTS // 2
LIFT = 32
SENT = 2 * TOKENS + TAIL
THIRDS = ((0, 112), (112, 112), (224, 96))
F32 = jnp.float32
BF16 = jnp.bfloat16
VMEM = pltpu.VMEM


PLACES = tuple((dx, dy) for dx in range(2) for dy in range(4))


def fetch(value, dx, dy, dc):
    pairs = []
    for i in range(16):
        x, y, c = i >> 3, (i >> 1) & 3, i & 1
        pairs.append((((x ^ dx) << 3) + (((y + dy) & 3) << 1) + (c ^ dc), i))
    return lax.ppermute(value, "replica", pairs)


def along_shard(value, dx, dz):
    pairs = [((((i >> 3) ^ dx) << 3) + ((i + dz) & 7), i) for i in range(16)]
    return lax.ppermute(value, "shard", pairs)


def owner(here, place):
    return (((here >> 3) ^ place[0]) << 2) + (((here >> 1) + place[1]) & 3)


def factors(codes):
    out = jnp.ones(codes.shape, F32)
    for bit in range(5):
        out = out * jnp.where((codes >> bit) & 1 == 1, F32(2.0 ** -(2**bit)), F32(1.0))
    return out


def start_all(copies):
    for copy in copies:
        copy.start()


def pack_kernel(
    here, hidden, dq, dk, dv, do, sq, so, skt, svt, base,
    out, turned, moved,
    vh, vq, vk, vv, vo, vsq, vso, vsk, vsv, rows, buf, sems,
):
    shift = CUT * here[0]
    first = (shift >> 4) << 4
    pairs = [(hidden, vh), (sq, vsq), (so, vso), (skt, vsk), (svt, vsv)]
    pairs += [(dq, vq), (dk, vk), (dv, vv), (do, vo)]
    copies = [pltpu.make_async_copy(a, b, sems.at[i]) for i, (a, b) in enumerate(pairs)]
    for dest in range(PARTS):
        at = pl.multiple_of(OWN * dest + first, 16)
        copies.append(
            pltpu.make_async_copy(
                base.at[pl.ds(at, LIFT), :], rows.at[dest], sems.at[len(pairs) + dest]
            )
        )
    start_all(copies)
    for copy in copies[:5]:
        copy.wait()
    for at, n in TILES:
        turned[at : at + n, :] = vh[:, at : at + n].astype(F32).T.astype(BF16)
    fq, fo, fk, fv = factors(vsq[...]), factors(vso[...]), factors(vsk[...]), factors(vsv[...])
    line = lax.broadcasted_iota(jnp.int32, (CUT, CUT), 0)
    lane = lax.broadcasted_iota(jnp.int32, (CUT, CUT), 1)

    def column(factor, head):
        spread = jnp.where(line == lane, factor[head : head + 1, :], 0.0)
        return jnp.sum(spread, axis=1, keepdims=True)

    def piece(codes, head, factor):
        return codes[:, head * HEAD : (head + 1) * HEAD].astype(F32) * factor

    for copy in copies[5:]:
        copy.wait()
    for head in range(HQ):
        moved[:, head * HEAD : (head + 1) * HEAD] = piece(vo, head, fo[:, head : head + 1]).astype(BF16)
    buf[6 * CUT : BLOCK, :] = jnp.zeros((BLOCK - 6 * CUT, HEAD), F32)
    turn = (LIFT - (shift - first)) & (LIFT - 1)
    for half in range(PARTS // 2):
        key, value = piece(vk, half, column(fk, half)), piece(vv, half, column(fv, half))
        for dest in (2 * half, 2 * half + 1):
            mine = pltpu.roll(rows[dest].astype(F32), turn, 0)[0:CUT, :]
            pieces = (
                piece(vq, 2 * dest, fq[:, 2 * dest : 2 * dest + 1]),
                piece(vq, 2 * dest + 1, fq[:, 2 * dest + 1 : 2 * dest + 2]),
                key,
                value,
                mine[:, 0:HEAD],
                mine[:, HEAD:],
            )
            for c, item in enumerate(pieces):
                buf[CUT * c : CUT * (c + 1), :] = item
            out[dest] = buf[...].astype(BF16)


def refresh_kernel(here, recv, bq, bk, bv, out, vq, vk, vv, buf, delta, sems):
    at = pl.ds(pl.multiple_of(OWN * here[0], 64), OWN)
    copies = [
        pltpu.make_async_copy(a.at[at, :], b, sems.at[i])
        for i, (a, b) in enumerate(((bq, vq), (bk, vk), (bv, vv)))
    ]
    start_all(copies)
    for src in range(PARTS):
        buf[src % 2] = recv[src].astype(F32)
        for c in range(4):
            delta[CUT * src : CUT * (src + 1), HEAD * c : HEAD * (c + 1)] = buf[
                src % 2, CUT * c : CUT * (c + 1), :
            ]
    for copy in copies:
        copy.wait()
    out[:, 0:256] = (vq[...].astype(F32) + delta[:, 0:256]).astype(BF16)
    out[:, 256:384] = (vk[...].astype(F32) + delta[:, 256:384]).astype(BF16)
    out[:, 384:512] = (vv[...].astype(F32) + delta[:, 384:512]).astype(BF16)


def refresh_out_kernel(recv, moved, out, buf):
    for src in range(PARTS):
        buf[src % 2] = recv[src].astype(F32)
        for h in range(2):
            at = (2 * src + h) * HEAD
            base = buf[src % 2, CUT * (4 + h) : CUT * (5 + h), :]
            out[:, at : at + HEAD] = (base + moved[:, at : at + HEAD].astype(F32)).astype(BF16)


def dot_nt(a, b):
    return lax.dot_general(a, b, (((1,), (1,)), ((), ())), preferred_element_type=F32)


def dot(a, b):
    return jnp.dot(a, b, preferred_element_type=F32)


def head_norm_rotate(raw, gain, cosine, sine):
    value = raw * lax.rsqrt(jnp.mean(raw * raw, axis=-1, keepdims=True) + EPSILON) * gain
    swapped = jnp.concatenate([value[:, HEAD // 2 :], value[:, : HEAD // 2]], axis=-1)
    return value * cosine + swapped * sine


def group_scores(group, query, cache, fresh, lens):
    picked = [
        query[h * TOKENS + t * ROWS + group * GROUP : h * TOKENS + t * ROWS + (group + 1) * GROUP, :]
        for h in range(2)
        for t in range(STEPS)
    ]
    q = jnp.concatenate(picked, axis=0).astype(BF16)
    past = dot_nt(q, cache) * SCALE
    new = dot_nt(q, fresh) * SCALE
    n = 2 * STEPS * GROUP
    length = jnp.concatenate([lens[group * GROUP : (group + 1) * GROUP, :]] * (2 * STEPS), axis=0)
    column = lax.broadcasted_iota(jnp.int32, past.shape, 1)
    line = lax.broadcasted_iota(jnp.int32, past.shape, 0)
    past_ok = ((column >> 6) == (line & 7)) & ((column & 63) < length[:, 0:1])
    column = lax.broadcasted_iota(jnp.int32, (n, TOKENS), 1)
    line = lax.broadcasted_iota(jnp.int32, (n, TOKENS), 0)
    new_ok = ((column & 31) == group * GROUP + (line & 7)) & ((column >> 5) <= ((line >> 3) & 3))
    past = jnp.where(past_ok, past, NEG)
    new = jnp.where(new_ok, new, NEG)
    top = jnp.maximum(
        jnp.max(past, axis=-1, keepdims=True), jnp.max(new, axis=-1, keepdims=True)
    )
    past = jnp.exp(past - top)
    new = jnp.exp(new - top)
    total = jnp.sum(past, axis=-1, keepdims=True) + jnp.sum(new, axis=-1, keepdims=True)
    return past, new, total, top + jnp.log(total)


def put_groups(group, ref, value):
    for h in range(2):
        for t in range(STEPS):
            at = h * TOKENS + t * ROWS + group * GROUP
            i = (h * STEPS + t) * GROUP
            ref[at : at + GROUP, :] = value[i : i + GROUP, :]


def sample_logp(query, keys, one_query, lse):
    out = []
    for h in range(2):
        q = dot(one_query, query[h * TOKENS : (h + 1) * TOKENS, :].astype(BF16))
        score = jnp.sum(q * keys, axis=-1, keepdims=True) * SCALE
        line = lse[h * TOKENS : (h + 1) * TOKENS, :].T
        picked = jnp.sum(one_query.astype(F32) * line, axis=-1, keepdims=True)
        out.append(jnp.broadcast_to(score - picked, (TOKENS, HEAD)))
    return out


def normalise_kernel(
    here, seat, gain, p0, p1, p2, p3, p4, p5, p6, p7, normed, keep, give,
):
    total = jnp.zeros((1, TOKENS), F32)
    pairs = (p0, p1, p2, p3, p4, p5, p6, p7)
    for pair in pairs:
        x = pair[...].astype(F32)
        total = total + jnp.sum(x * x, axis=0, keepdims=True)
    scale = lax.rsqrt(total * (1.0 / WIDTH) + EPSILON)
    me = seat[0]
    for step, pair in enumerate(pairs):
        for half in range(2):
            src = (((me >> 3) ^ half) << 3) + ((me + step) & 7)
            for at, n in TILES:
                x = pair[half * OWN + at : half * OWN + at + n, :].astype(F32) * scale
                normed[src, :, at : at + n] = (x.T * gain[src, :, at : at + n]).astype(BF16)
    core = here[0] & 1
    for j in range(HALF):
        keep[j] = normed[2 * j + core]
        give[j] = normed[2 * j + 1 - core]


def old_kernel(
    normed, table, marks, base_q, base_k, cache_hbm,
    keys_out, one_q_out, one_f_out, old_out,
    wq, wk, cache, query, lse, sems,
):
    copies = [
        pltpu.make_async_copy(a, b, sems.at[i])
        for i, (a, b) in enumerate(((base_q, wq), (base_k, wk), (cache_hbm, cache)))
    ]
    start_all(copies)
    for copy in copies:
        copy.wait()
    raw = jnp.zeros((TOKENS, 256), F32)
    raw_k = jnp.zeros((TOKENS, HEAD), F32)
    for src in range(PARTS):
        raw = raw + dot(normed[src], wq[src * OWN : (src + 1) * OWN, :])
        raw_k = raw_k + dot(normed[src], wk[src * OWN : (src + 1) * OWN, :])
    cos, sin = table[0:TOKENS, :], table[TOKENS : 2 * TOKENS, :]
    qg, kg = table[2 * TOKENS : 2 * TOKENS + 1, :], table[2 * TOKENS + 1 : 2 * TOKENS + 2, :]
    lens = marks
    for h in range(2):
        query[h * TOKENS : (h + 1) * TOKENS, :] = (
            head_norm_rotate(raw[:, h * HEAD : (h + 1) * HEAD], qg, cos, sin)
            .astype(BF16)
            .astype(F32)
        )
    fresh = head_norm_rotate(raw_k, kg, cos, sin).astype(BF16)
    for g in range(GROUPS):
        _, _, _, log_sum = group_scores(
            g, query, cache[g * GROUP * CTX : (g + 1) * GROUP * CTX, :], fresh, lens
        )
        put_groups(g, lse, jnp.broadcast_to(log_sum, (log_sum.shape[0], HEAD)))
    tokens = jnp.broadcast_to(marks[ROWS : ROWS + 1, :], (TOKENS, TOKENS)).T
    places = jnp.broadcast_to(marks[ROWS + 1 : ROWS + 2, :], (TOKENS, TOKENS)).T
    lane = lax.broadcasted_iota(jnp.int32, (TOKENS, TOKENS), 1)
    one_q = jnp.where(tokens == lane, F32(1.0), F32(0.0)).astype(BF16)
    one_f = jnp.where(places == lane + ROWS * CTX, F32(1.0), F32(0.0)).astype(BF16)
    keys = jnp.zeros((TOKENS, HEAD), F32)
    for k in range(ROWS * CTX // HEAD):
        one = jnp.where(places == lane + k * HEAD, F32(1.0), F32(0.0)).astype(BF16)
        keys = keys + dot(one, cache[k * HEAD : (k + 1) * HEAD, :])
    keys_out[...] = keys
    one_q_out[...] = one_q
    one_f_out[...] = one_f
    old = sample_logp(query, keys + dot(one_f, fresh), one_q, lse)
    old_out[0] = old[0]
    old_out[1] = old[1]


def project_kernel(here, keep, given, w00, w01, w02, w03, w10, w11, wa, wb, wc, w13, own, other):
    raw = jnp.zeros((2 * TOKENS, 512), F32)
    weights = (w00, w01, w02, w03, w10, w11, (wa, wb, wc), w13)
    for place, weight in zip(PLACES, weights):
        j = owner(here[0], place)
        lines = jnp.concatenate([keep[j], given[j]], axis=0)
        if isinstance(weight, tuple):
            value = jnp.concatenate([w[...] for w in weight], axis=0)
        else:
            value = weight[...]
        raw = raw + dot(lines, value)
    own[...] = raw[0:TOKENS, :]
    other[...] = raw[TOKENS:, :]


def attend_kernel(
    own, other, table, marks, cache_hbm, values_hbm, keys, one_q, one_f, old,
    out,
    cache, values, query, lse, mixed, sems,
):
    copies = (
        pltpu.make_async_copy(cache_hbm, cache, sems.at[0]),
        pltpu.make_async_copy(values_hbm, values, sems.at[1]),
    )
    start_all(copies)
    raw = own[...] + other[...]
    cos, sin = table[0:TOKENS, :], table[TOKENS : 2 * TOKENS, :]
    qg, kg = table[2 * TOKENS : 2 * TOKENS + 1, :], table[2 * TOKENS + 1 : 2 * TOKENS + 2, :]
    lens = marks
    for h in range(2):
        query[h * TOKENS : (h + 1) * TOKENS, :] = (
            head_norm_rotate(raw[:, h * HEAD : (h + 1) * HEAD], qg, cos, sin)
            .astype(BF16)
            .astype(F32)
        )
    fresh = head_norm_rotate(raw[:, 256:384], kg, cos, sin).astype(BF16)
    fresh_v = raw[:, 384:512].astype(BF16)
    for copy in copies:
        copy.wait()
    for g in range(GROUPS):
        at = slice(g * GROUP * CTX, (g + 1) * GROUP * CTX)
        past, new, total, log_sum = group_scores(g, query, cache[at, :], fresh, lens)
        put_groups(g, lse, jnp.broadcast_to(log_sum, (log_sum.shape[0], HEAD)))
        mix = dot((past / total).astype(BF16), values[at, :])
        mix = mix + dot((new / total).astype(BF16), fresh_v)
        put_groups(g, mixed, mix)
    attended = mixed[...].astype(BF16)
    now = sample_logp(query, keys[...] + dot(one_f[...], fresh), one_q[...], lse)
    term = (now[0] - old[0]) + (now[1] - old[1])
    line = term.T[0:1, :]
    high = line.astype(BF16).astype(F32)
    middle = (line - high).astype(BF16).astype(F32)
    low = line - high - middle
    tail = jnp.concatenate([high, middle, low, jnp.zeros((TAIL - 3, TOKENS), F32)], axis=0)
    tail = tail.astype(BF16)
    for p in range(PARTS):
        out[p, 0 : 2 * TOKENS, :] = attended
        out[p, 2 * TOKENS : SENT, :] = tail


def collect_kernel(here, w0, w1, w2, w3, w4, w5, w6, w7, out, buf):
    buf[...] = jnp.zeros_like(buf)
    for place, weight in zip(PLACES, (w0, w1, w2, w3, w4, w5, w6, w7)):
        buf[0:CUT, :] = weight[...].astype(F32)
        out[owner(here[0], place)] = buf[...].astype(BF16)


def finish_kernel(here, recv, mine, theirs, out, ratio, lines, blocks, features):
    tail = jnp.zeros((TAIL, TOKENS), F32)
    for src in range(PARTS):
        for h in range(2):
            at = (2 * src + h) * HEAD
            lines[:, at : at + HEAD] = recv[src, h * TOKENS : (h + 1) * TOKENS, :]
        tail = tail + recv[src, 2 * TOKENS : SENT, :].astype(F32)
    ratio[...] = ((tail[2:3, :] + tail[1:2, :]) + tail[0:1, :]) * (1.0 / HQ)
    core = here[0] & 1
    for weight, parity in ((mine, core), (theirs, 1 - core)):
        result = dot_nt(weight[...].reshape(HALF * LIFT, 2 * PARTS * HEAD), lines[...])
        for j in range(HALF):
            blocks[2 * j + parity] = result[LIFT * j : LIFT * (j + 1), :]
    for b in range(PARTS):
        features[CUT * b : CUT * (b + 1), :] = blocks[b, 0:CUT, :]
    for at, n in TILES:
        out[:, at : at + n] = features[at : at + n, :].T.astype(BF16)


def params(mib):
    return pltpu.CompilerParams(vmem_limit_bytes=mib * 1024 * 1024)


def shape(dims, dtype):
    return jax.ShapeDtypeStruct(dims, dtype)


def whole(n=1):
    return [pl.BlockSpec(memory_space=VMEM)] * n


def scalars(n=1):
    return [pl.BlockSpec(memory_space=pltpu.SMEM)] * n


def far_away(n=1):
    return [pl.BlockSpec(memory_space=pltpu.HBM)] * n


def call(kernel, name, out_shape, in_specs, scratch, mib):
    several = isinstance(out_shape, tuple)
    return pl.pallas_call(
        kernel,
        name=name,
        out_shape=out_shape,
        in_specs=in_specs,
        out_specs=tuple(whole(len(out_shape))) if several else whole()[0],
        scratch_shapes=scratch,
        compiler_params=params(mib),
    )


def local(
    hidden,
    norm_gain,
    query_gain,
    key_gain,
    base_query,
    base_key,
    base_value,
    base_output,
    delta_query,
    scale_query,
    key_delta_codes,
    key_scale_codes,
    value_delta_codes,
    value_scale_codes,
    delta_output,
    scale_output,
    cache_keys,
    cache_values,
    lengths,
    stale_rows,
    stale_steps,
    stale_back,
):
    here = lax.axis_index("replica").astype(jnp.int32).reshape(1)
    seat = lax.axis_index("shard").astype(jnp.int32).reshape(1)
    dma = pltpu.SemaphoreType.DMA
    packed, turned, moved = call(
        pack_kernel,
        "pack",
        (
            shape((PARTS, BLOCK, HEAD), BF16),
            shape((OWN, TOKENS), BF16),
            shape((CUT, HQ * HEAD), BF16),
        ),
        scalars() + far_away(10),
        [
            VMEM((TOKENS, OWN), BF16),
            VMEM((CUT, HQ * HEAD), BF16),
            VMEM((CUT, KV * HEAD), BF16),
            VMEM((CUT, KV * HEAD), BF16),
            VMEM((CUT, HQ * HEAD), BF16),
            VMEM((CUT, HQ), jnp.int32),
            VMEM((CUT, HQ), jnp.int32),
            VMEM((KV, CUT), jnp.int32),
            VMEM((KV, CUT), jnp.int32),
            VMEM((PARTS, LIFT, 2 * HEAD), BF16),
            VMEM((BLOCK, HEAD), F32),
            dma((9 + PARTS,)),
        ],
        16,
    )(
        here, hidden.reshape(TOKENS, OWN), delta_query, key_delta_codes, value_delta_codes, delta_output,
        scale_query, scale_output, key_scale_codes.T, value_scale_codes.T, base_output,
    )
    mirrored = [(r * PARTS + s, s * PARTS + r) for r in range(PARTS) for s in range(PARTS)]
    moved = lax.ppermute(moved, ("replica", "shard"), mirrored)
    across = along_shard(turned, 1, 0)
    arrived = lax.all_to_all(packed, "shard", split_axis=0, concat_axis=0, tiled=False)
    arrived, moved, across, turned, lengths, stale_rows, stale_steps, stale_back = (
        lax.optimization_barrier(
            (arrived, moved, across, turned, lengths, stale_rows, stale_steps, stale_back)
        )
    )
    fresh_rows = call(
        refresh_kernel,
        "refresh",
        shape((OWN, 512), BF16),
        scalars() + whole() + far_away(3),
        [
            VMEM((OWN, 256), BF16),
            VMEM((OWN, 128), BF16),
            VMEM((OWN, 128), BF16),
            VMEM((2, BLOCK, HEAD), F32),
            VMEM((OWN, 512), F32),
            dma((3,)),
        ],
        8,
    )(here, arrived, base_query, base_key, base_value)
    pair = jnp.concatenate([turned, across], axis=0)
    fresh_out = call(
        refresh_out_kernel,
        "refresh_out",
        shape((CUT, HQ * HEAD), BF16),
        whole(2),
        [VMEM((2, BLOCK, HEAD), F32)],
        8,
    )(arrived, moved)

    over = fetch(fresh_rows, 1, 0, 0)
    up = fetch(fresh_rows, 0, 1, 0)
    down = fetch(fresh_rows, 0, -1, 0)
    z1, z7 = along_shard(pair, 0, 1), along_shard(pair, 0, -1)
    z2, z6 = along_shard(pair, 0, 2), along_shard(pair, 0, -2)
    over, up, down, z1, z7, z2, z6 = lax.optimization_barrier((over, up, down, z1, z7, z2, z6))
    over_up = fetch(up, 1, 0, 0)
    far = fetch(up, 0, 1, 0)
    over_down = fetch(over, 0, -1, 0)
    z3, z5 = along_shard(z2, 0, 1), along_shard(z6, 0, -1)
    z4 = along_shard(z2, 0, 2)
    over_up, far, over_down, z3, z4, z5, fresh_out = lax.optimization_barrier(
        (over_up, far, over_down, z3, z4, z5, fresh_out)
    )
    cuts = [slice(at, at + n) for at, n in THIRDS]
    far_over = [
        fetch(far[cuts[0]], 1, 0, 0),
        fetch(over_up[cuts[1]], 0, 1, 0),
        fetch(over_down[cuts[2]], 0, -1, 0),
    ]

    normed, keep, give = call(
        normalise_kernel,
        "normalise",
        (
            shape((PARTS, TOKENS, OWN), BF16),
            shape((HALF, TOKENS, OWN), BF16),
            shape((HALF, TOKENS, OWN), BF16),
        ),
        scalars(2) + whole(9),
        [],
        8,
    )(here, seat, norm_gain.reshape(PARTS, 1, OWN), pair, z1, z2, z3, z4, z5, z6, z7)
    given = fetch(give, 0, 0, 1)

    position = (lengths[None, :] + jnp.arange(STEPS)[:, None]).reshape(TOKENS)
    freq = THETA ** (-(jnp.arange(HEAD // 2).astype(F32) * 2.0) / HEAD)
    angle = position.astype(F32)[:, None] * freq
    cos, sin = jnp.cos(angle), jnp.sin(angle)
    table = jnp.concatenate(
        [
            jnp.concatenate([cos, cos], axis=1),
            jnp.concatenate([-sin, sin], axis=1),
            query_gain.reshape(1, HEAD),
            key_gain.reshape(1, HEAD),
            jnp.zeros((6, HEAD), F32),
        ],
        axis=0,
    )
    rows_s, steps_s, back_s = stale_rows, stale_steps, stale_back
    lens_s = jnp.sum(
        jnp.where(rows_s[0][None, :] == jnp.arange(ROWS)[:, None], lengths[:, None], 0),
        axis=0,
        keepdims=True,
    )
    at = lens_s + steps_s - back_s % (lens_s + steps_s + 1)
    place = jnp.where(
        at >= lens_s, ROWS * CTX + (at - lens_s) * ROWS + rows_s, rows_s * CTX + at
    ).astype(jnp.int32)
    token = (steps_s * ROWS + rows_s).astype(jnp.int32)
    marks = jnp.concatenate(
        [
            jnp.broadcast_to(lengths[:, None], (ROWS, HEAD)),
            token,
            place,
            jnp.zeros((6, HEAD), jnp.int32),
        ],
        axis=0,
    )
    cache = cache_keys.reshape(ROWS * CTX, HEAD)
    values = cache_values.reshape(ROWS * CTX, HEAD)

    keys, one_q, one_f, old = call(
        old_kernel,
        "old",
        (
            shape((TOKENS, HEAD), F32),
            shape((TOKENS, TOKENS), BF16),
            shape((TOKENS, TOKENS), BF16),
            shape((2, TOKENS, HEAD), F32),
        ),
        whole(3) + far_away(3),
        [
            VMEM((WIDTH, 256), BF16),
            VMEM((WIDTH, HEAD), BF16),
            VMEM((ROWS * CTX, HEAD), BF16),
            VMEM((2 * TOKENS, HEAD), F32),
            VMEM((2 * TOKENS, HEAD), F32),
            dma((3,)),
        ],
        16,
    )(normed, table, marks, base_query, base_key, cache)

    own, other = call(
        project_kernel,
        "project",
        (shape((TOKENS, 512), F32), shape((TOKENS, 512), F32)),
        scalars() + whole(12),
        [],
        12,
    )(here, keep, given, fresh_rows, up, far, down, over, over_up, *far_over, over_down)
    other = fetch(other, 0, 0, 1)

    out_over = fetch(fresh_out, 1, 0, 0)
    out_up = fetch(fresh_out, 0, 1, 0)
    out_down = fetch(fresh_out, 0, -1, 0)
    out_over_up = fetch(out_up, 1, 0, 0)
    out_far = fetch(out_up, 0, 1, 0)
    out_over_down = fetch(out_over, 0, -1, 0)
    out_far_over = fetch(out_far, 1, 0, 0)
    mine = call(
        collect_kernel,
        "collect",
        shape((HALF, LIFT, HQ * HEAD), BF16),
        scalars() + whole(8),
        [VMEM((LIFT, HQ * HEAD), F32)],
        8,
    )(here, fresh_out, out_up, out_far, out_down, out_over, out_over_up, out_far_over, out_over_down)
    theirs = fetch(mine, 0, 0, 1)

    sent = call(
        attend_kernel,
        "attend",
        shape((PARTS, SENT, HEAD), BF16),
        whole(4) + far_away(2) + whole(4),
        [
            VMEM((ROWS * CTX, HEAD), BF16),
            VMEM((ROWS * CTX, HEAD), BF16),
            VMEM((2 * TOKENS, HEAD), F32),
            VMEM((2 * TOKENS, HEAD), F32),
            VMEM((2 * TOKENS, HEAD), F32),
            dma((2,)),
        ],
        12,
    )(own, other, table, marks, cache, values, keys, one_q, one_f, old)
    landed = lax.all_to_all(sent, "shard", split_axis=0, concat_axis=0, tiled=False)
    out, ratio = call(
        finish_kernel,
        "finish",
        (shape((TOKENS, OWN), BF16), shape((1, TOKENS), F32)),
        scalars() + whole(3),
        [
            VMEM((TOKENS, HQ * HEAD), BF16),
            VMEM((PARTS, LIFT, TOKENS), F32),
            VMEM((OWN, TOKENS), F32),
        ],
        12,
    )(here, landed, mine, theirs)
    return out.reshape(STEPS, ROWS, OWN), ratio


def solution(mesh):
    return jax.shard_map(
        local,
        mesh=mesh,
        in_specs=(
            P(None, "replica", "shard"),
            P(),
            P(),
            P(),
            P(None, "shard"),
            P(None, "shard"),
            P(None, "shard"),
            P(None, "shard"),
            P(("replica", "shard"), None),
            P(("replica", "shard"), None),
            P(("replica", "shard"), None),
            P(("replica", "shard"), None),
            P(("replica", "shard"), None),
            P(("replica", "shard"), None),
            P(("replica", "shard"), None),
            P(("replica", "shard"), None),
            P("replica", None, "shard"),
            P("replica", None, "shard"),
            P("replica"),
            P("replica", None),
            P("replica", None),
            P("replica", None),
        ),
        out_specs=(P(None, "replica", "shard"), P("replica", None)),
        check_vma=False,
    )
```

```python
import jax
import jax.numpy as jnp
from jax import lax
from jax.experimental import pallas as pl
from jax.experimental.pallas import tpu as pltpu
from jax.sharding import PartitionSpec as P

HQ = 32
KV = 8
HEAD = 128
WIDTH = 5120
STEPS = 4
ROWS = 32
TOKENS = STEPS * ROWS
CTX = 64
PARTS = 16
OWN = WIDTH // PARTS
CUT = 20
GROUP = 8
GROUPS = ROWS // GROUP
TAIL = 16
EPSILON = 1e-06
THETA = 1000000.0
SCALE = HEAD ** (-0.5)
NEG = -1e30
TILES = ((0, 128), (128, 128), (256, 64))
BLOCK = 128
HALF = PARTS // 2
FOLD = OWN // 2
TALL = OWN + FOLD
WIDE = 384
SENT = OWN + TAIL
F32 = jnp.float32
BF16 = jnp.bfloat16
VMEM = pltpu.VMEM


def fetch(value, dx, dy, dc):
    pairs = []
    for i in range(16):
        x, y, c = i >> 3, (i >> 1) & 3, i & 1
        pairs.append((((x ^ dx) << 3) + (((y + dy) & 3) << 1) + (c ^ dc), i))
    return lax.ppermute(value, "replica", pairs)


def along_shard(value, dx, dz):
    pairs = [((((i >> 3) ^ dx) << 3) + ((i + dz) & 7), i) for i in range(16)]
    return lax.ppermute(value, "shard", pairs)


def factors(codes):
    out = jnp.ones(codes.shape, F32)
    for bit in range(5):
        out = out * jnp.where((codes >> bit) & 1 == 1, F32(2.0 ** -(2**bit)), F32(1.0))
    return out


def start_all(copies):
    for copy in copies:
        copy.start()


def pack_kernel(
    hidden, dq, dk, dv, do, sq, so, skt, svt,
    out, turned,
    vh, vq, vk, vv, vo, vsq, vso, vsk, vsv, buf, sems,
):
    pairs = [(hidden, vh), (sq, vsq), (so, vso), (skt, vsk), (svt, vsv)]
    pairs += [(dq, vq), (dk, vk), (dv, vv), (do, vo)]
    copies = [pltpu.make_async_copy(a, b, sems.at[i]) for i, (a, b) in enumerate(pairs)]
    start_all(copies)
    for copy in copies[:5]:
        copy.wait()
    for at, n in TILES:
        turned[at : at + n, :] = vh[:, at : at + n].astype(F32).T.astype(BF16)
    fq, fo, fk, fv = factors(vsq[...]), factors(vso[...]), factors(vsk[...]), factors(vsv[...])
    line = lax.broadcasted_iota(jnp.int32, (CUT, CUT), 0)
    lane = lax.broadcasted_iota(jnp.int32, (CUT, CUT), 1)

    def column(factor, head):
        spread = jnp.where(line == lane, factor[head : head + 1, :], 0.0)
        return jnp.sum(spread, axis=1, keepdims=True)

    def piece(codes, head, factor):
        return codes[:, head * HEAD : (head + 1) * HEAD].astype(F32) * factor

    for copy in copies[5:]:
        copy.wait()
    buf[6 * CUT : BLOCK, :] = jnp.zeros((BLOCK - 6 * CUT, HEAD), F32)
    for half in range(PARTS // 2):
        key, value = piece(vk, half, column(fk, half)), piece(vv, half, column(fv, half))
        for dest in (2 * half, 2 * half + 1):
            pieces = (
                piece(vq, 2 * dest, fq[:, 2 * dest : 2 * dest + 1]),
                piece(vq, 2 * dest + 1, fq[:, 2 * dest + 1 : 2 * dest + 2]),
                key,
                value,
                piece(vo, 2 * dest, fo[:, 2 * dest : 2 * dest + 1]),
                piece(vo, 2 * dest + 1, fo[:, 2 * dest + 1 : 2 * dest + 2]),
            )
            for c, item in enumerate(pieces):
                buf[CUT * c : CUT * (c + 1), :] = item
            out[dest] = buf[...].astype(BF16)


def refresh_kernel(
    here, recv, bq, bk, bv, bo, out, vq, vk, vv, vo, buf, delta, fresh, sems,
):
    at = pl.ds(pl.multiple_of(OWN * here[0], 64), OWN)
    bases = ((bq, vq), (bk, vk), (bv, vv), (bo, vo))
    copies = [
        pltpu.make_async_copy(a.at[at, :], b, sems.at[i]) for i, (a, b) in enumerate(bases)
    ]
    start_all(copies)
    for src in range(PARTS):
        buf[src % 2] = recv[src].astype(F32)
        for c in range(6):
            delta[CUT * src : CUT * (src + 1), HEAD * c : HEAD * (c + 1)] = buf[
                src % 2, CUT * c : CUT * (c + 1), :
            ]
    for copy in copies:
        copy.wait()
    for at, n, base in ((0, 256, vq), (256, 128, vk), (384, 128, vv)):
        fresh[0:OWN, at : at + n] = (base[...].astype(F32) + delta[:, at : at + n]).astype(BF16)
    for half in range(2):
        at = slice(half * FOLD, (half + 1) * FOLD)
        value = vo[at, :].astype(F32) + delta[at, 512:768]
        fresh[OWN:, half * 256 : (half + 1) * 256] = value.astype(BF16)
    copies = [pltpu.make_async_copy(fresh, out.at[j], sems.at[4 + j]) for j in range(HALF)]
    start_all(copies)
    for copy in copies:
        copy.wait()


def dot_nt(a, b):
    return lax.dot_general(a, b, (((1,), (1,)), ((), ())), preferred_element_type=F32)


def dot(a, b):
    return jnp.dot(a, b, preferred_element_type=F32)


def head_norm_rotate(raw, gain, cosine, sine):
    value = raw * lax.rsqrt(jnp.mean(raw * raw, axis=-1, keepdims=True) + EPSILON) * gain
    swapped = jnp.concatenate([value[:, HEAD // 2 :], value[:, : HEAD // 2]], axis=-1)
    return value * cosine + swapped * sine


def group_scores(group, query, cache, fresh, lens):
    picked = [
        query[h * TOKENS + t * ROWS + group * GROUP : h * TOKENS + t * ROWS + (group + 1) * GROUP, :]
        for h in range(2)
        for t in range(STEPS)
    ]
    q = jnp.concatenate(picked, axis=0).astype(BF16)
    past = dot_nt(q, cache) * SCALE
    new = dot_nt(q, fresh) * SCALE
    n = 2 * STEPS * GROUP
    length = jnp.concatenate([lens[group * GROUP : (group + 1) * GROUP, :]] * (2 * STEPS), axis=0)
    column = lax.broadcasted_iota(jnp.int32, past.shape, 1)
    line = lax.broadcasted_iota(jnp.int32, past.shape, 0)
    past_ok = ((column >> 6) == (line & 7)) & ((column & 63) < length[:, 0:1])
    column = lax.broadcasted_iota(jnp.int32, (n, TOKENS), 1)
    line = lax.broadcasted_iota(jnp.int32, (n, TOKENS), 0)
    new_ok = ((column & 31) == group * GROUP + (line & 7)) & ((column >> 5) <= ((line >> 3) & 3))
    past = jnp.where(past_ok, past, NEG)
    new = jnp.where(new_ok, new, NEG)
    top = jnp.maximum(
        jnp.max(past, axis=-1, keepdims=True), jnp.max(new, axis=-1, keepdims=True)
    )
    past = jnp.exp(past - top)
    new = jnp.exp(new - top)
    total = jnp.sum(past, axis=-1, keepdims=True) + jnp.sum(new, axis=-1, keepdims=True)
    return past, new, total, top + jnp.log(total)


def put_groups(group, ref, value):
    for h in range(2):
        for t in range(STEPS):
            at = h * TOKENS + t * ROWS + group * GROUP
            i = (h * STEPS + t) * GROUP
            ref[at : at + GROUP, :] = value[i : i + GROUP, :]


def sample_logp(query, keys, one_query, lse):
    out = []
    for h in range(2):
        q = dot(one_query, query[h * TOKENS : (h + 1) * TOKENS, :].astype(BF16))
        score = jnp.sum(q * keys, axis=-1, keepdims=True) * SCALE
        line = lse[h * TOKENS : (h + 1) * TOKENS, :].T
        picked = jnp.sum(one_query.astype(F32) * line, axis=-1, keepdims=True)
        out.append(jnp.broadcast_to(score - picked, (TOKENS, HEAD)))
    return out


def normalise_kernel(here, seat, gain, p0, p1, p2, p3, p4, p5, p6, p7, keep, give):
    total = jnp.zeros((1, TOKENS), F32)
    pairs = (p0, p1, p2, p3, p4, p5, p6, p7)
    for pair in pairs:
        x = pair[...].astype(F32)
        total = total + jnp.sum(x * x, axis=0, keepdims=True)
    scale = lax.rsqrt(total * (1.0 / WIDTH) + EPSILON)
    me, core = seat[0], here[0] & 1

    def put(step, pair, target):
        for half in range(2):
            src = (((me >> 3) ^ half) << 3) + ((me + step) & 7)
            for at, n in TILES:
                x = pair[half * OWN + at : half * OWN + at + n, :].astype(F32) * scale
                value = (x.T * gain[src, :, at : at + n]).astype(BF16)
                target[src >> 1, :, at : at + n] = value
            target[src >> 1, :, OWN:] = jnp.zeros((TOKENS, WIDE - OWN), BF16)

    for step, pair in enumerate(pairs):
        same = ((me + step) & 1) == core
        pl.when(same)(lambda step=step, pair=pair: put(step, pair, keep))
        pl.when(jnp.logical_not(same))(lambda step=step, pair=pair: put(step, pair, give))


def select_kernel(marks, cache_hbm, keys_out, one_q_out, one_f_out, cache, sems):
    copy = pltpu.make_async_copy(cache_hbm, cache, sems.at[0])
    copy.start()
    tokens = jnp.broadcast_to(marks[ROWS : ROWS + 1, :], (TOKENS, TOKENS)).T
    places = jnp.broadcast_to(marks[ROWS + 1 : ROWS + 2, :], (TOKENS, TOKENS)).T
    lane = lax.broadcasted_iota(jnp.int32, (TOKENS, TOKENS), 1)
    one_q = jnp.where(tokens == lane, F32(1.0), F32(0.0)).astype(BF16)
    one_f = jnp.where(places == lane + ROWS * CTX, F32(1.0), F32(0.0)).astype(BF16)
    copy.wait()
    keys = jnp.zeros((TOKENS, HEAD), F32)
    for k in range(ROWS * CTX // HEAD):
        one = jnp.where(places == lane + k * HEAD, F32(1.0), F32(0.0)).astype(BF16)
        keys = keys + dot(one, cache[k * HEAD : (k + 1) * HEAD, :])
    keys_out[...] = keys
    one_q_out[...] = one_q
    one_f_out[...] = one_f


def old_kernel(
    here, keep, give, table, marks, keys, one_q, one_f, base_q, base_k, cache_hbm,
    old_out,
    wq, wk, cache, query, lse, sems,
):
    quarter = WIDTH // 4
    copies = []
    for i in range(4):
        at = pl.ds(i * quarter, quarter)
        copies += [
            pltpu.make_async_copy(base_q.at[at, :], wq.at[at, :], sems.at[2 * i]),
            pltpu.make_async_copy(base_k.at[at, :], wk.at[at, :], sems.at[2 * i + 1]),
        ]
    copies.append(pltpu.make_async_copy(cache_hbm, cache, sems.at[8]))
    start_all(copies)
    core = here[0] & 1
    raw = jnp.zeros((TOKENS, 256), F32)
    raw_k = jnp.zeros((TOKENS, HEAD), F32)
    for j in range(HALF):
        if j % 2 == 0:
            copies[j].wait()
            copies[j + 1].wait()
        for lines, src in ((keep, 2 * j + core), (give, 2 * j + 1 - core)):
            at = pl.ds(pl.multiple_of(OWN * src, 64), OWN)
            raw = raw + dot(lines[j, :, 0:OWN], wq[at, :])
            raw_k = raw_k + dot(lines[j, :, 0:OWN], wk[at, :])
    copies[8].wait()
    cos, sin = table[0:TOKENS, :], table[TOKENS : 2 * TOKENS, :]
    qg, kg = table[2 * TOKENS : 2 * TOKENS + 1, :], table[2 * TOKENS + 1 : 2 * TOKENS + 2, :]
    lens = marks
    for h in range(2):
        query[h * TOKENS : (h + 1) * TOKENS, :] = (
            head_norm_rotate(raw[:, h * HEAD : (h + 1) * HEAD], qg, cos, sin)
            .astype(BF16)
            .astype(F32)
        )
    fresh = head_norm_rotate(raw_k, kg, cos, sin).astype(BF16)
    for g in range(GROUPS):
        _, _, _, log_sum = group_scores(
            g, query, cache[g * GROUP * CTX : (g + 1) * GROUP * CTX, :], fresh, lens
        )
        put_groups(g, lse, jnp.broadcast_to(log_sum, (log_sum.shape[0], HEAD)))
    old = sample_logp(query, keys[...] + dot(one_f[...], fresh), one_q[...], lse)
    old_out[0] = old[0]
    old_out[1] = old[1]


def project_kernel(keep, given, weight, own, other, below):
    raw = jnp.zeros((2 * TOKENS, 512), F32)
    for j in range(HALF):
        lines = jnp.concatenate([keep[j, :, 0:OWN], given[j, :, 0:OWN]], axis=0)
        raw = raw + dot(lines, weight[j, 0:OWN, :])
        below[j] = weight[j, OWN:, :]
    own[...] = raw[0:TOKENS, :]
    other[...] = raw[TOKENS:, :]


def attend_kernel(
    here, own, other, table, marks, cache_hbm, values_hbm, keys, one_q, one_f, old, mine, theirs,
    out,
    cache, values, query, lse, mixed, sems,
):
    copies = (
        pltpu.make_async_copy(cache_hbm, cache, sems.at[0]),
        pltpu.make_async_copy(values_hbm, values, sems.at[1]),
    )
    start_all(copies)
    raw = own[...] + other[...]
    cos, sin = table[0:TOKENS, :], table[TOKENS : 2 * TOKENS, :]
    qg, kg = table[2 * TOKENS : 2 * TOKENS + 1, :], table[2 * TOKENS + 1 : 2 * TOKENS + 2, :]
    lens = marks
    for h in range(2):
        query[h * TOKENS : (h + 1) * TOKENS, :] = (
            head_norm_rotate(raw[:, h * HEAD : (h + 1) * HEAD], qg, cos, sin)
            .astype(BF16)
            .astype(F32)
        )
    fresh = head_norm_rotate(raw[:, 256:384], kg, cos, sin).astype(BF16)
    fresh_v = raw[:, 384:512].astype(BF16)
    for copy in copies:
        copy.wait()
    for g in range(GROUPS):
        at = slice(g * GROUP * CTX, (g + 1) * GROUP * CTX)
        past, new, total, log_sum = group_scores(g, query, cache[at, :], fresh, lens)
        put_groups(g, lse, jnp.broadcast_to(log_sum, (log_sum.shape[0], HEAD)))
        mix = dot((past / total).astype(BF16), values[at, :])
        mix = mix + dot((new / total).astype(BF16), fresh_v)
        put_groups(g, mixed, mix)
    attended = jnp.concatenate([mixed[0:TOKENS, :], mixed[TOKENS:, :]], axis=1).astype(BF16)
    core = here[0] & 1
    for rows, parity in ((mine, core), (theirs, 1 - core)):
        for j in range(HALF):
            for half in range(2):
                part = dot_nt(rows[j, :, half * 256 : (half + 1) * 256], attended)
                at = slice(half * FOLD, (half + 1) * FOLD)
                out[2 * j + parity, at, :] = part.astype(BF16)
    now = sample_logp(query, keys[...] + dot(one_f[...], fresh), one_q[...], lse)
    term = (now[0] - old[0]) + (now[1] - old[1])
    line = term.T[0:1, :]
    high = line.astype(BF16).astype(F32)
    middle = (line - high).astype(BF16).astype(F32)
    low = line - high - middle
    tail = jnp.concatenate([high, middle, low, jnp.zeros((TAIL - 3, TOKENS), F32)], axis=0)
    tail = tail.astype(BF16)
    for p in range(PARTS):
        out[p, OWN:SENT, :] = tail


def finish_kernel(recv, out, ratio):
    for k, n in ((0, 128), (128, 128), (256, 80)):
        total = recv[0, k : k + n, :].astype(F32)
        for src in range(1, PARTS):
            total = total + recv[src, k : k + n, :].astype(F32)
        if n == 128:
            out[:, k : k + n] = total.T.astype(BF16)
        else:
            tail = total[64:67, :]
            ratio[...] = ((tail[2:3, :] + tail[1:2, :]) + tail[0:1, :]) * (1.0 / HQ)
            out[:, k : k + 64] = total[0:64, :].T.astype(BF16)


def params(mib):
    return pltpu.CompilerParams(vmem_limit_bytes=mib * 1024 * 1024)


def shape(dims, dtype):
    return jax.ShapeDtypeStruct(dims, dtype)


def whole(*dims):
    return pl.BlockSpec(dims, lambda i: (0,) * len(dims))


def scalars(n=1):
    return [pl.BlockSpec(memory_space=pltpu.SMEM)] * n


def far_away(n=1):
    return [pl.BlockSpec(memory_space=pltpu.HBM)] * n


def spec_of(out):
    return whole(*out.shape)


def call(kernel, name, outs, in_specs, scratch, far=False, mib=56):
    several = isinstance(outs, tuple)
    return pl.pallas_call(
        kernel,
        name=name,
        grid=(1,),
        out_shape=outs,
        in_specs=in_specs,
        out_specs=far_away()[0] if far else tuple(map(spec_of, outs)) if several else spec_of(outs),
        scratch_shapes=scratch,
        compiler_params=params(mib),
    )


def local(
    hidden,
    norm_gain,
    query_gain,
    key_gain,
    base_query,
    base_key,
    base_value,
    base_output,
    delta_query,
    scale_query,
    key_delta_codes,
    key_scale_codes,
    value_delta_codes,
    value_scale_codes,
    delta_output,
    scale_output,
    cache_keys,
    cache_values,
    lengths,
    stale_rows,
    stale_steps,
    stale_back,
):
    here = lax.axis_index("replica").astype(jnp.int32).reshape(1)
    seat = lax.axis_index("shard").astype(jnp.int32).reshape(1)
    dma = pltpu.SemaphoreType.DMA
    packed, turned = call(
        pack_kernel,
        "pack",
        (shape((PARTS, BLOCK, HEAD), BF16), shape((OWN, TOKENS), BF16)),
        far_away(9),
        [
            VMEM((TOKENS, OWN), BF16),
            VMEM((CUT, HQ * HEAD), BF16),
            VMEM((CUT, KV * HEAD), BF16),
            VMEM((CUT, KV * HEAD), BF16),
            VMEM((CUT, HQ * HEAD), BF16),
            VMEM((CUT, HQ), jnp.int32),
            VMEM((CUT, HQ), jnp.int32),
            VMEM((KV, CUT), jnp.int32),
            VMEM((KV, CUT), jnp.int32),
            VMEM((BLOCK, HEAD), F32),
            dma((9,)),
        ],
        mib=56,
    )(
        hidden.reshape(TOKENS, OWN), delta_query, key_delta_codes, value_delta_codes, delta_output,
        scale_query, scale_output, key_scale_codes.T, value_scale_codes.T,
    )
    across = along_shard(turned, 1, 0)
    arrived = lax.all_to_all(packed, "shard", split_axis=0, concat_axis=0, tiled=False)
    arrived, across, lengths, stale_rows, stale_steps, stale_back = lax.optimization_barrier(
        (arrived, across, lengths, stale_rows, stale_steps, stale_back)
    )
    copies = call(
        refresh_kernel,
        "refresh",
        shape((HALF, TALL, 512), BF16),
        scalars() + [whole(PARTS, BLOCK, HEAD)] + far_away(4),
        [
            VMEM((OWN, 256), BF16),
            VMEM((OWN, 128), BF16),
            VMEM((OWN, 128), BF16),
            VMEM((OWN, 256), BF16),
            VMEM((2, BLOCK, HEAD), F32),
            VMEM((OWN, 768), F32),
            VMEM((TALL, 512), BF16),
            dma((4 + HALF,)),
        ],
        True,
        mib=56,
    )(here, arrived, base_query, base_key, base_value, base_output)
    groups = [[2 * j + core for j in range(HALF)] for core in range(2)]
    pair = jnp.concatenate([turned, across], axis=0)
    copies, pair = lax.optimization_barrier((copies, pair))
    weight = lax.all_to_all(
        copies, "replica", split_axis=0, concat_axis=0, tiled=False, axis_index_groups=groups
    )
    position = (lengths[None, :] + jnp.arange(STEPS)[:, None]).reshape(TOKENS)
    freq = THETA ** (-(jnp.arange(HEAD // 2).astype(F32) * 2.0) / HEAD)
    angle = position.astype(F32)[:, None] * freq
    cos, sin = jnp.cos(angle), jnp.sin(angle)
    table = jnp.concatenate(
        [
            jnp.concatenate([cos, cos], axis=1),
            jnp.concatenate([-sin, sin], axis=1),
            query_gain.reshape(1, HEAD),
            key_gain.reshape(1, HEAD),
            jnp.zeros((6, HEAD), F32),
        ],
        axis=0,
    )
    rows_s, steps_s, back_s = stale_rows, stale_steps, stale_back
    lens_s = jnp.sum(
        jnp.where(rows_s[0][None, :] == jnp.arange(ROWS)[:, None], lengths[:, None], 0),
        axis=0,
        keepdims=True,
    )
    at = lens_s + steps_s - back_s % (lens_s + steps_s + 1)
    place = jnp.where(
        at >= lens_s, ROWS * CTX + (at - lens_s) * ROWS + rows_s, rows_s * CTX + at
    ).astype(jnp.int32)
    token = (steps_s * ROWS + rows_s).astype(jnp.int32)
    marks = jnp.concatenate(
        [
            jnp.broadcast_to(lengths[:, None], (ROWS, HEAD)),
            token,
            place,
            jnp.zeros((6, HEAD), jnp.int32),
        ],
        axis=0,
    )
    cache = cache_keys.reshape(ROWS * CTX, HEAD)
    values = cache_values.reshape(ROWS * CTX, HEAD)

    keys, one_q, one_f = call(
        select_kernel,
        "select",
        (
            shape((TOKENS, HEAD), F32),
            shape((TOKENS, TOKENS), BF16),
            shape((TOKENS, TOKENS), BF16),
        ),
        [whole(ROWS + 8, HEAD)] + far_away(),
        [VMEM((ROWS * CTX, HEAD), BF16), dma((1,))],
    )(marks, cache)
    z1, z7 = along_shard(pair, 0, 1), along_shard(pair, 0, -1)
    z2, z6 = along_shard(pair, 0, 2), along_shard(pair, 0, -2)
    z2, z6, keys, one_q, one_f, table = lax.optimization_barrier(
        (z2, z6, keys, one_q, one_f, table)
    )
    z3, z5 = along_shard(z2, 0, 1), along_shard(z6, 0, -1)
    z4 = along_shard(z2, 0, 2)

    keep, give = call(
        normalise_kernel,
        "normalise",
        (
            shape((HALF, TOKENS, WIDE), BF16),
            shape((HALF, TOKENS, WIDE), BF16),
        ),
        scalars(2) + [whole(PARTS, 1, OWN)] + [whole(2 * OWN, TOKENS)] * 8,
        [],
    )(here, seat, norm_gain.reshape(PARTS, 1, OWN), pair, z1, z2, z3, z4, z5, z6, z7)
    given = fetch(give, 0, 0, 1)

    old = call(
        old_kernel,
        "old",
        shape((2, TOKENS, HEAD), F32),
        scalars()
        + [whole(HALF, TOKENS, WIDE)] * 2
        + [whole(2 * TOKENS + 8, HEAD), whole(ROWS + 8, HEAD)]
        + [whole(TOKENS, HEAD)] * 3
        + far_away(3),
        [
            VMEM((WIDTH, 256), BF16),
            VMEM((WIDTH, HEAD), BF16),
            VMEM((ROWS * CTX, HEAD), BF16),
            VMEM((2 * TOKENS, HEAD), F32),
            VMEM((2 * TOKENS, HEAD), F32),
            dma((9,)),
        ],
    )(here, keep, give, table, marks, keys, one_q, one_f, base_query, base_key, cache)

    weight, keep, given, old = lax.optimization_barrier((weight, keep, given, old))
    own, other, mine = call(
        project_kernel,
        "project",
        (
            shape((TOKENS, 512), F32),
            shape((TOKENS, 512), F32),
            shape((HALF, FOLD, 512), BF16),
        ),
        [whole(HALF, TOKENS, WIDE)] * 2 + [whole(HALF, TALL, 512)],
        [],
        mib=20,
    )(keep, given, weight)
    other = fetch(other, 0, 0, 1)
    theirs = fetch(mine, 0, 0, 1)

    sent = call(
        attend_kernel,
        "attend",
        shape((PARTS, SENT, HEAD), BF16),
        scalars()
        + [whole(TOKENS, 512)] * 2
        + [whole(2 * TOKENS + 8, HEAD), whole(ROWS + 8, HEAD)]
        + far_away(2)
        + [whole(TOKENS, HEAD)] * 3
        + [whole(2, TOKENS, HEAD)]
        + [whole(HALF, FOLD, 512)] * 2,
        [
            VMEM((ROWS * CTX, HEAD), BF16),
            VMEM((ROWS * CTX, HEAD), BF16),
            VMEM((2 * TOKENS, HEAD), F32),
            VMEM((2 * TOKENS, HEAD), F32),
            VMEM((2 * TOKENS, HEAD), F32),
            dma((2,)),
        ],
        mib=24,
    )(here, own, other, table, marks, cache, values, keys, one_q, one_f, old, mine, theirs)
    landed = lax.all_to_all(sent, "shard", split_axis=0, concat_axis=0, tiled=False)
    out, ratio = call(
        finish_kernel,
        "finish",
        (shape((TOKENS, OWN), BF16), shape((1, TOKENS), F32)),
        [whole(PARTS, SENT, HEAD)],
        [],
        mib=20,
    )(landed)
    return out.reshape(STEPS, ROWS, OWN), ratio


def solution(mesh):
    return jax.shard_map(
        local,
        mesh=mesh,
        in_specs=(
            P(None, "replica", "shard"),
            P(),
            P(),
            P(),
            P(None, "shard"),
            P(None, "shard"),
            P(None, "shard"),
            P(None, "shard"),
            P(("replica", "shard"), None),
            P(("replica", "shard"), None),
            P(("replica", "shard"), None),
            P(("replica", "shard"), None),
            P(("replica", "shard"), None),
            P(("replica", "shard"), None),
            P(("replica", "shard"), None),
            P(("replica", "shard"), None),
            P("replica", None, "shard"),
            P("replica", None, "shard"),
            P("replica"),
            P("replica", None),
            P("replica", None),
            P("replica", None),
        ),
        out_specs=(P(None, "replica", "shard"), P("replica", None)),
        check_vma=False,
    )
```

```python
import jax
import jax.numpy as jnp
from jax import lax
from jax.experimental import pallas as pl
from jax.experimental.pallas import tpu as pltpu
from jax.sharding import PartitionSpec as P

HQ = 32
KV = 8
HEAD = 128
WIDTH = 5120
STEPS = 4
ROWS = 32
TOKENS = STEPS * ROWS
CTX = 64
PARTS = 16
OWN = WIDTH // PARTS
CUT = 20
GROUP = 8
GROUPS = ROWS // GROUP
TAIL = 16
EPSILON = 1e-06
THETA = 1000000.0
SCALE = HEAD ** (-0.5)
NEG = -1e30
TILES = ((0, 128), (128, 128), (256, 64))
BLOCK = 128
HALF = PARTS // 2
FOLD = OWN // 2
UPPER = 256
LOWER = OWN - UPPER + FOLD
WIDE = 384
SENT = OWN + TAIL
F32 = jnp.float32
BF16 = jnp.bfloat16
VMEM = pltpu.VMEM


def fetch(value, dx, dy, dc):
    pairs = []
    for i in range(16):
        x, y, c = i >> 3, (i >> 1) & 3, i & 1
        pairs.append((((x ^ dx) << 3) + (((y + dy) & 3) << 1) + (c ^ dc), i))
    return lax.ppermute(value, "replica", pairs)


PLACES = tuple((dx, dy) for dx in range(2) for dy in range(4))


def owner(here, place):
    return (((here >> 3) ^ place[0]) << 2) + (((here >> 1) + place[1]) & 3)


def gather_blocks(own, turn):
    over, first, back = fetch(own, 1, 0, 0), fetch(own, 0, turn, 0), fetch(own, 0, -turn, 0)
    over_first, far, over_back = fetch(first, 1, 0, 0), fetch(first, 0, turn, 0), fetch(over, 0, -turn, 0)
    held = {(0, 0): own, (1, 0): over, (0, turn & 3): first, (0, -turn & 3): back}
    held.update({(1, turn & 3): over_first, (0, 2): far, (1, -turn & 3): over_back})
    if turn == 1:
        held[1, 2] = fetch(far, 1, 0, 0)
    else:
        held[1, 2] = fetch(over_back, 0, 1, 0)
    return [held[place] for place in PLACES]


def along_shard(value, dx, dz):
    pairs = [((((i >> 3) ^ dx) << 3) + ((i + dz) & 7), i) for i in range(16)]
    return lax.ppermute(value, "shard", pairs)


def factors(codes):
    out = jnp.ones(codes.shape, F32)
    for bit in range(5):
        out = out * jnp.where((codes >> bit) & 1 == 1, F32(2.0 ** -(2**bit)), F32(1.0))
    return out


def start_all(copies):
    for copy in copies:
        copy.start()


def pack_kernel(
    hidden, dq, dk, dv, do, sq, so, skt, svt,
    out, turned,
    vh, vq, vk, vv, vo, vsq, vso, vsk, vsv, buf, sems,
):
    pairs = [(hidden, vh), (sq, vsq), (so, vso), (skt, vsk), (svt, vsv)]
    pairs += [(dq, vq), (dk, vk), (dv, vv), (do, vo)]
    copies = [pltpu.make_async_copy(a, b, sems.at[i]) for i, (a, b) in enumerate(pairs)]
    start_all(copies)
    for copy in copies[:5]:
        copy.wait()
    for at, n in TILES:
        turned[at : at + n, :] = vh[:, at : at + n].astype(F32).T.astype(BF16)
    fq, fo, fk, fv = factors(vsq[...]), factors(vso[...]), factors(vsk[...]), factors(vsv[...])
    line = lax.broadcasted_iota(jnp.int32, (CUT, CUT), 0)
    lane = lax.broadcasted_iota(jnp.int32, (CUT, CUT), 1)

    def column(factor, head):
        spread = jnp.where(line == lane, factor[head : head + 1, :], 0.0)
        return jnp.sum(spread, axis=1, keepdims=True)

    def piece(codes, head, factor):
        return codes[:, head * HEAD : (head + 1) * HEAD].astype(F32) * factor

    for copy in copies[5:]:
        copy.wait()
    buf[6 * CUT : BLOCK, :] = jnp.zeros((BLOCK - 6 * CUT, HEAD), F32)
    for half in range(PARTS // 2):
        key, value = piece(vk, half, column(fk, half)), piece(vv, half, column(fv, half))
        for dest in (2 * half, 2 * half + 1):
            pieces = (
                piece(vq, 2 * dest, fq[:, 2 * dest : 2 * dest + 1]),
                piece(vq, 2 * dest + 1, fq[:, 2 * dest + 1 : 2 * dest + 2]),
                key,
                value,
                piece(vo, 2 * dest, fo[:, 2 * dest : 2 * dest + 1]),
                piece(vo, 2 * dest + 1, fo[:, 2 * dest + 1 : 2 * dest + 2]),
            )
            for c, item in enumerate(pieces):
                buf[CUT * c : CUT * (c + 1), :] = item
            out[dest] = buf[...].astype(BF16)


def refresh_kernel(
    here, recv, bq, bk, bv, bo, upper, lower, vq, vk, vv, vo, buf, delta, sems,
):
    at = pl.ds(pl.multiple_of(OWN * here[0], 64), OWN)
    bases = ((bq, vq), (bk, vk), (bv, vv), (bo, vo))
    copies = [
        pltpu.make_async_copy(a.at[at, :], b, sems.at[i]) for i, (a, b) in enumerate(bases)
    ]
    start_all(copies)
    for src in range(PARTS):
        buf[src % 2] = recv[src].astype(F32)
        for c in range(6):
            delta[CUT * src : CUT * (src + 1), HEAD * c : HEAD * (c + 1)] = buf[
                src % 2, CUT * c : CUT * (c + 1), :
            ]
    for copy in copies:
        copy.wait()
    for at, n, base in ((0, 256, vq), (256, 128, vk), (384, 128, vv)):
        value = (base[...].astype(F32) + delta[:, at : at + n]).astype(BF16)
        upper[:, at : at + n] = value[0:UPPER]
        lower[0 : OWN - UPPER, at : at + n] = value[UPPER:]
    for half in range(2):
        at = slice(half * FOLD, (half + 1) * FOLD)
        value = vo[at, :].astype(F32) + delta[at, 512:768]
        lower[OWN - UPPER :, half * 256 : (half + 1) * 256] = value.astype(BF16)


def dot_nt(a, b):
    return lax.dot_general(a, b, (((1,), (1,)), ((), ())), preferred_element_type=F32)


def dot(a, b):
    return jnp.dot(a, b, preferred_element_type=F32)


def head_norm_rotate(raw, gain, cosine, sine):
    value = raw * lax.rsqrt(jnp.mean(raw * raw, axis=-1, keepdims=True) + EPSILON) * gain
    swapped = jnp.concatenate([value[:, HEAD // 2 :], value[:, : HEAD // 2]], axis=-1)
    return value * cosine + swapped * sine


def group_scores(group, query, cache, fresh, lens):
    picked = [
        query[h * TOKENS + t * ROWS + group * GROUP : h * TOKENS + t * ROWS + (group + 1) * GROUP, :]
        for h in range(2)
        for t in range(STEPS)
    ]
    q = jnp.concatenate(picked, axis=0).astype(BF16)
    past = dot_nt(q, cache) * SCALE
    new = dot_nt(q, fresh) * SCALE
    n = 2 * STEPS * GROUP
    length = jnp.concatenate([lens[group * GROUP : (group + 1) * GROUP, :]] * (2 * STEPS), axis=0)
    column = lax.broadcasted_iota(jnp.int32, past.shape, 1)
    line = lax.broadcasted_iota(jnp.int32, past.shape, 0)
    past_ok = ((column >> 6) == (line & 7)) & ((column & 63) < length[:, 0:1])
    column = lax.broadcasted_iota(jnp.int32, (n, TOKENS), 1)
    line = lax.broadcasted_iota(jnp.int32, (n, TOKENS), 0)
    new_ok = ((column & 31) == group * GROUP + (line & 7)) & ((column >> 5) <= ((line >> 3) & 3))
    past = jnp.where(past_ok, past, NEG)
    new = jnp.where(new_ok, new, NEG)
    top = jnp.maximum(
        jnp.max(past, axis=-1, keepdims=True), jnp.max(new, axis=-1, keepdims=True)
    )
    past = jnp.exp(past - top)
    new = jnp.exp(new - top)
    total = jnp.sum(past, axis=-1, keepdims=True) + jnp.sum(new, axis=-1, keepdims=True)
    return past, new, total, top + jnp.log(total)


def put_groups(group, ref, value):
    for h in range(2):
        for t in range(STEPS):
            at = h * TOKENS + t * ROWS + group * GROUP
            i = (h * STEPS + t) * GROUP
            ref[at : at + GROUP, :] = value[i : i + GROUP, :]


def sample_logp(query, keys, one_query, lse):
    out = []
    for h in range(2):
        q = dot(one_query, query[h * TOKENS : (h + 1) * TOKENS, :].astype(BF16))
        score = jnp.sum(q * keys, axis=-1, keepdims=True) * SCALE
        line = lse[h * TOKENS : (h + 1) * TOKENS, :].T
        picked = jnp.sum(one_query.astype(F32) * line, axis=-1, keepdims=True)
        out.append(jnp.broadcast_to(score - picked, (TOKENS, HEAD)))
    return out


def normalise_kernel(here, seat, gain, pairs, keep, give):
    total = jnp.zeros((1, TOKENS), F32)
    for z in range(8):
        x = pairs[z].astype(F32)
        total = total + jnp.sum(x * x, axis=0, keepdims=True)
    scale = lax.rsqrt(total * (1.0 / WIDTH) + EPSILON)
    me, core = seat[0], here[0] & 1

    def put(z, target):
        for half in range(2):
            src = (((me >> 3) ^ half) << 3) + z
            for at, n in TILES:
                x = pairs[z, half * OWN + at : half * OWN + at + n, :].astype(F32) * scale
                value = (x.T * gain[src, :, at : at + n]).astype(BF16)
                target[src >> 1, :, at : at + n] = value
            target[src >> 1, :, OWN:] = jnp.zeros((TOKENS, WIDE - OWN), BF16)

    for z in range(8):
        pl.when(core == z & 1)(lambda z=z: put(z, keep))
        pl.when(core != z & 1)(lambda z=z: put(z, give))


def select_kernel(marks, cache_hbm, keys_out, one_q_out, one_f_out, cache, sems):
    copy = pltpu.make_async_copy(cache_hbm, cache, sems.at[0])
    copy.start()
    tokens = jnp.broadcast_to(marks[ROWS : ROWS + 1, :], (TOKENS, TOKENS)).T
    places = jnp.broadcast_to(marks[ROWS + 1 : ROWS + 2, :], (TOKENS, TOKENS)).T
    lane = lax.broadcasted_iota(jnp.int32, (TOKENS, TOKENS), 1)
    one_q = jnp.where(tokens == lane, F32(1.0), F32(0.0)).astype(BF16)
    one_f = jnp.where(places == lane + ROWS * CTX, F32(1.0), F32(0.0)).astype(BF16)
    copy.wait()
    keys = jnp.zeros((TOKENS, HEAD), F32)
    for k in range(ROWS * CTX // HEAD):
        one = jnp.where(places == lane + k * HEAD, F32(1.0), F32(0.0)).astype(BF16)
        keys = keys + dot(one, cache[k * HEAD : (k + 1) * HEAD, :])
    keys_out[...] = keys
    one_q_out[...] = one_q
    one_f_out[...] = one_f


def old_kernel(
    here, keep, give, table, marks, keys, one_q, one_f, base_q, base_k, cache_hbm,
    old_out,
    wq, wk, cache, query, lse, sems,
):
    quarter = WIDTH // 4
    copies = []
    for i in range(4):
        at = pl.ds(i * quarter, quarter)
        copies += [
            pltpu.make_async_copy(base_q.at[at, :], wq.at[at, :], sems.at[2 * i]),
            pltpu.make_async_copy(base_k.at[at, :], wk.at[at, :], sems.at[2 * i + 1]),
        ]
    copies.append(pltpu.make_async_copy(cache_hbm, cache, sems.at[8]))
    start_all(copies)
    core = here[0] & 1
    raw = jnp.zeros((TOKENS, 256), F32)
    raw_k = jnp.zeros((TOKENS, HEAD), F32)
    for j in range(HALF):
        if j % 2 == 0:
            copies[j].wait()
            copies[j + 1].wait()
        for lines, src in ((keep, 2 * j + core), (give, 2 * j + 1 - core)):
            at = pl.ds(pl.multiple_of(OWN * src, 64), OWN)
            raw = raw + dot(lines[j, :, 0:OWN], wq[at, :])
            raw_k = raw_k + dot(lines[j, :, 0:OWN], wk[at, :])
    copies[8].wait()
    cos, sin = table[0:TOKENS, :], table[TOKENS : 2 * TOKENS, :]
    qg, kg = table[2 * TOKENS : 2 * TOKENS + 1, :], table[2 * TOKENS + 1 : 2 * TOKENS + 2, :]
    lens = marks
    for h in range(2):
        query[h * TOKENS : (h + 1) * TOKENS, :] = (
            head_norm_rotate(raw[:, h * HEAD : (h + 1) * HEAD], qg, cos, sin)
            .astype(BF16)
            .astype(F32)
        )
    fresh = head_norm_rotate(raw_k, kg, cos, sin).astype(BF16)
    for g in range(GROUPS):
        _, _, _, log_sum = group_scores(
            g, query, cache[g * GROUP * CTX : (g + 1) * GROUP * CTX, :], fresh, lens
        )
        put_groups(g, lse, jnp.broadcast_to(log_sum, (log_sum.shape[0], HEAD)))
    old = sample_logp(query, keys[...] + dot(one_f[...], fresh), one_q[...], lse)
    old_out[0] = old[0]
    old_out[1] = old[1]


def project_kernel(here, keep, given, *rest):
    uppers, lowers, (own, other, below) = rest[0:8], rest[8:16], rest[16:]
    raw = jnp.zeros((2 * TOKENS, 512), F32)
    for place, upper, lower in zip(PLACES, uppers, lowers):
        j = owner(here[0], place)
        for at, n, weight in ((0, UPPER, upper), (UPPER, OWN - UPPER, lower)):
            lines = jnp.concatenate([keep[j, :, at : at + n], given[j, :, at : at + n]], axis=0)
            raw = raw + dot(lines, weight[0:n, :])
        below[j] = lower[OWN - UPPER :, :]
    own[...] = raw[0:TOKENS, :]
    other[...] = raw[TOKENS:, :]


def attend_kernel(
    here, own, other, table, marks, cache_hbm, values_hbm, keys, one_q, one_f, old, mine, theirs,
    out,
    cache, values, query, lse, mixed, sems,
):
    copies = (
        pltpu.make_async_copy(cache_hbm, cache, sems.at[0]),
        pltpu.make_async_copy(values_hbm, values, sems.at[1]),
    )
    start_all(copies)
    raw = own[...] + other[...]
    cos, sin = table[0:TOKENS, :], table[TOKENS : 2 * TOKENS, :]
    qg, kg = table[2 * TOKENS : 2 * TOKENS + 1, :], table[2 * TOKENS + 1 : 2 * TOKENS + 2, :]
    lens = marks
    for h in range(2):
        query[h * TOKENS : (h + 1) * TOKENS, :] = (
            head_norm_rotate(raw[:, h * HEAD : (h + 1) * HEAD], qg, cos, sin)
            .astype(BF16)
            .astype(F32)
        )
    fresh = head_norm_rotate(raw[:, 256:384], kg, cos, sin).astype(BF16)
    fresh_v = raw[:, 384:512].astype(BF16)
    for copy in copies:
        copy.wait()
    for g in range(GROUPS):
        at = slice(g * GROUP * CTX, (g + 1) * GROUP * CTX)
        past, new, total, log_sum = group_scores(g, query, cache[at, :], fresh, lens)
        put_groups(g, lse, jnp.broadcast_to(log_sum, (log_sum.shape[0], HEAD)))
        mix = dot((past / total).astype(BF16), values[at, :])
        mix = mix + dot((new / total).astype(BF16), fresh_v)
        put_groups(g, mixed, mix)
    attended = jnp.concatenate([mixed[0:TOKENS, :], mixed[TOKENS:, :]], axis=1).astype(BF16)
    core = here[0] & 1
    for rows, parity in ((mine, core), (theirs, 1 - core)):
        for j in range(HALF):
            for half in range(2):
                part = dot_nt(rows[j, :, half * 256 : (half + 1) * 256], attended)
                at = slice(half * FOLD, (half + 1) * FOLD)
                out[2 * j + parity, at, :] = part.astype(BF16)
    now = sample_logp(query, keys[...] + dot(one_f[...], fresh), one_q[...], lse)
    term = (now[0] - old[0]) + (now[1] - old[1])
    line = term.T[0:1, :]
    high = line.astype(BF16).astype(F32)
    middle = (line - high).astype(BF16).astype(F32)
    low = line - high - middle
    tail = jnp.concatenate([high, middle, low, jnp.zeros((TAIL - 3, TOKENS), F32)], axis=0)
    tail = tail.astype(BF16)
    for p in range(PARTS):
        out[p, OWN:SENT, :] = tail


def finish_kernel(recv, out, ratio):
    for k, n in ((0, 128), (128, 128), (256, 80)):
        total = recv[0, k : k + n, :].astype(F32)
        for src in range(1, PARTS):
            total = total + recv[src, k : k + n, :].astype(F32)
        if n == 128:
            out[:, k : k + n] = total.T.astype(BF16)
        else:
            tail = total[64:67, :]
            ratio[...] = ((tail[2:3, :] + tail[1:2, :]) + tail[0:1, :]) * (1.0 / HQ)
            out[:, k : k + 64] = total[0:64, :].T.astype(BF16)


def params(mib):
    return pltpu.CompilerParams(vmem_limit_bytes=mib * 1024 * 1024)


def shape(dims, dtype):
    return jax.ShapeDtypeStruct(dims, dtype)


def whole(*dims):
    return pl.BlockSpec(dims, lambda i: (0,) * len(dims))


def scalars(n=1):
    return [pl.BlockSpec(memory_space=pltpu.SMEM)] * n


def far_away(n=1):
    return [pl.BlockSpec(memory_space=pltpu.HBM)] * n


def spec_of(out):
    return whole(*out.shape)


def call(kernel, name, outs, in_specs, scratch, far=False, mib=56):
    several = isinstance(outs, tuple)
    return pl.pallas_call(
        kernel,
        name=name,
        grid=(1,),
        out_shape=outs,
        in_specs=in_specs,
        out_specs=far_away()[0] if far else tuple(map(spec_of, outs)) if several else spec_of(outs),
        scratch_shapes=scratch,
        compiler_params=params(mib),
    )


def local(
    hidden,
    norm_gain,
    query_gain,
    key_gain,
    base_query,
    base_key,
    base_value,
    base_output,
    delta_query,
    scale_query,
    key_delta_codes,
    key_scale_codes,
    value_delta_codes,
    value_scale_codes,
    delta_output,
    scale_output,
    cache_keys,
    cache_values,
    lengths,
    stale_rows,
    stale_steps,
    stale_back,
):
    here = lax.axis_index("replica").astype(jnp.int32).reshape(1)
    seat = lax.axis_index("shard").astype(jnp.int32).reshape(1)
    dma = pltpu.SemaphoreType.DMA
    packed, turned = call(
        pack_kernel,
        "pack",
        (shape((PARTS, BLOCK, HEAD), BF16), shape((OWN, TOKENS), BF16)),
        far_away(9),
        [
            VMEM((TOKENS, OWN), BF16),
            VMEM((CUT, HQ * HEAD), BF16),
            VMEM((CUT, KV * HEAD), BF16),
            VMEM((CUT, KV * HEAD), BF16),
            VMEM((CUT, HQ * HEAD), BF16),
            VMEM((CUT, HQ), jnp.int32),
            VMEM((CUT, HQ), jnp.int32),
            VMEM((KV, CUT), jnp.int32),
            VMEM((KV, CUT), jnp.int32),
            VMEM((BLOCK, HEAD), F32),
            dma((9,)),
        ],
        mib=56,
    )(
        hidden.reshape(TOKENS, OWN), delta_query, key_delta_codes, value_delta_codes, delta_output,
        scale_query, scale_output, key_scale_codes.T, value_scale_codes.T,
    )
    across = along_shard(turned, 1, 0)
    arrived = lax.all_to_all(packed, "shard", split_axis=0, concat_axis=0, tiled=False)
    spread = jnp.concatenate([turned, across], axis=0)
    spread = jnp.broadcast_to(spread[None], (8, 2 * OWN, TOKENS))
    arrived, spread, lengths, stale_rows, stale_steps, stale_back = lax.optimization_barrier(
        (arrived, spread, lengths, stale_rows, stale_steps, stale_back)
    )
    upper, lower = call(
        refresh_kernel,
        "refresh",
        (shape((UPPER, 512), BF16), shape((LOWER, 512), BF16)),
        scalars() + [whole(PARTS, BLOCK, HEAD)] + far_away(4),
        [
            VMEM((OWN, 256), BF16),
            VMEM((OWN, 128), BF16),
            VMEM((OWN, 128), BF16),
            VMEM((OWN, 256), BF16),
            VMEM((2, BLOCK, HEAD), F32),
            VMEM((OWN, 768), F32),
            dma((4,)),
        ],
        mib=56,
    )(here, arrived, base_query, base_key, base_value, base_output)
    upper, lower, spread = lax.optimization_barrier((upper, lower, spread))
    uppers, lowers = gather_blocks(upper, 1), gather_blocks(lower, -1)
    rings = [[8 * x + z for z in range(8)] for x in range(2)]
    hidden_t = lax.all_to_all(
        spread,
        "shard",
        split_axis=0,
        concat_axis=0,
        tiled=False,
        axis_index_groups=rings,
    )

    position = (lengths[None, :] + jnp.arange(STEPS)[:, None]).reshape(TOKENS)
    freq = THETA ** (-(jnp.arange(HEAD // 2).astype(F32) * 2.0) / HEAD)
    angle = position.astype(F32)[:, None] * freq
    cos, sin = jnp.cos(angle), jnp.sin(angle)
    table = jnp.concatenate(
        [
            jnp.concatenate([cos, cos], axis=1),
            jnp.concatenate([-sin, sin], axis=1),
            query_gain.reshape(1, HEAD),
            key_gain.reshape(1, HEAD),
            jnp.zeros((6, HEAD), F32),
        ],
        axis=0,
    )
    rows_s, steps_s, back_s = stale_rows, stale_steps, stale_back
    lens_s = jnp.sum(
        jnp.where(rows_s[0][None, :] == jnp.arange(ROWS)[:, None], lengths[:, None], 0),
        axis=0,
        keepdims=True,
    )
    at = lens_s + steps_s - back_s % (lens_s + steps_s + 1)
    place = jnp.where(
        at >= lens_s, ROWS * CTX + (at - lens_s) * ROWS + rows_s, rows_s * CTX + at
    ).astype(jnp.int32)
    token = (steps_s * ROWS + rows_s).astype(jnp.int32)
    marks = jnp.concatenate(
        [
            jnp.broadcast_to(lengths[:, None], (ROWS, HEAD)),
            token,
            place,
            jnp.zeros((6, HEAD), jnp.int32),
        ],
        axis=0,
    )
    cache = cache_keys.reshape(ROWS * CTX, HEAD)
    values = cache_values.reshape(ROWS * CTX, HEAD)

    keys, one_q, one_f = call(
        select_kernel,
        "select",
        (
            shape((TOKENS, HEAD), F32),
            shape((TOKENS, TOKENS), BF16),
            shape((TOKENS, TOKENS), BF16),
        ),
        [whole(ROWS + 8, HEAD)] + far_away(),
        [VMEM((ROWS * CTX, HEAD), BF16), dma((1,))],
        mib=8,
    )(marks, cache)
    later = uppers + lowers
    hidden_t, keys, one_q, one_f, table, _ = lax.optimization_barrier(
        (hidden_t, keys, one_q, one_f, table, later)
    )
    keep, give = call(
        normalise_kernel,
        "normalise",
        (
            shape((HALF, TOKENS, WIDE), BF16),
            shape((HALF, TOKENS, WIDE), BF16),
        ),
        scalars(2) + [whole(PARTS, 1, OWN)] + [whole(8, 2 * OWN, TOKENS)],
        [],
        mib=16,
    )(here, seat, norm_gain.reshape(PARTS, 1, OWN), hidden_t)
    given = fetch(give, 0, 0, 1)

    old = call(
        old_kernel,
        "old",
        shape((2, TOKENS, HEAD), F32),
        scalars()
        + [whole(HALF, TOKENS, WIDE)] * 2
        + [whole(2 * TOKENS + 8, HEAD), whole(ROWS + 8, HEAD)]
        + [whole(TOKENS, HEAD)] * 3
        + far_away(3),
        [
            VMEM((WIDTH, 256), BF16),
            VMEM((WIDTH, HEAD), BF16),
            VMEM((ROWS * CTX, HEAD), BF16),
            VMEM((2 * TOKENS, HEAD), F32),
            VMEM((2 * TOKENS, HEAD), F32),
            dma((9,)),
        ],
        mib=24,
    )(here, keep, give, table, marks, keys, one_q, one_f, base_query, base_key, cache)

    own, other, mine = call(
        project_kernel,
        "project",
        (
            shape((TOKENS, 512), F32),
            shape((TOKENS, 512), F32),
            shape((HALF, FOLD, 512), BF16),
        ),
        scalars()
        + [whole(HALF, TOKENS, WIDE)] * 2
        + [whole(UPPER, 512)] * 8
        + [whole(LOWER, 512)] * 8,
        [],
        mib=24,
    )(here, keep, given, *uppers, *lowers)
    other = fetch(other, 0, 0, 1)
    theirs = fetch(mine, 0, 0, 1)

    sent = call(
        attend_kernel,
        "attend",
        shape((PARTS, SENT, HEAD), BF16),
        scalars()
        + [whole(TOKENS, 512)] * 2
        + [whole(2 * TOKENS + 8, HEAD), whole(ROWS + 8, HEAD)]
        + far_away(2)
        + [whole(TOKENS, HEAD)] * 3
        + [whole(2, TOKENS, HEAD)]
        + [whole(HALF, FOLD, 512)] * 2,
        [
            VMEM((ROWS * CTX, HEAD), BF16),
            VMEM((ROWS * CTX, HEAD), BF16),
            VMEM((2 * TOKENS, HEAD), F32),
            VMEM((2 * TOKENS, HEAD), F32),
            VMEM((2 * TOKENS, HEAD), F32),
            dma((2,)),
        ],
        mib=24,
    )(here, own, other, table, marks, cache, values, keys, one_q, one_f, old, mine, theirs)
    landed = lax.all_to_all(sent, "shard", split_axis=0, concat_axis=0, tiled=False)
    out, ratio = call(
        finish_kernel,
        "finish",
        (shape((TOKENS, OWN), BF16), shape((1, TOKENS), F32)),
        [whole(PARTS, SENT, HEAD)],
        [],
        mib=20,
    )(landed)
    return out.reshape(STEPS, ROWS, OWN), ratio


def solution(mesh):
    return jax.shard_map(
        local,
        mesh=mesh,
        in_specs=(
            P(None, "replica", "shard"),
            P(),
            P(),
            P(),
            P(None, "shard"),
            P(None, "shard"),
            P(None, "shard"),
            P(None, "shard"),
            P(("replica", "shard"), None),
            P(("replica", "shard"), None),
            P(("replica", "shard"), None),
            P(("replica", "shard"), None),
            P(("replica", "shard"), None),
            P(("replica", "shard"), None),
            P(("replica", "shard"), None),
            P(("replica", "shard"), None),
            P("replica", None, "shard"),
            P("replica", None, "shard"),
            P("replica"),
            P("replica", None),
            P("replica", None),
            P("replica", None),
        ),
        out_specs=(P(None, "replica", "shard"), P("replica", None)),
        check_vma=False,
    )
```

```python
import jax
import jax.numpy as jnp
from jax import lax
from jax.experimental import pallas as pl
from jax.experimental.pallas import tpu as pltpu
from jax.sharding import PartitionSpec as P

HQ = 32
KV = 8
HEAD = 128
WIDTH = 5120
STEPS = 4
ROWS = 32
TOKENS = STEPS * ROWS
CTX = 64
PARTS = 16
OWN = WIDTH // PARTS
CUT = 20
GROUP = 8
GROUPS = ROWS // GROUP
TAIL = 16
EPSILON = 1e-06
THETA = 1000000.0
SCALE = HEAD ** (-0.5)
NEG = -1e30
TILES = ((0, 128), (128, 128), (256, 64))
BLOCK = 128
HALF = PARTS // 2
FOLD = OWN // 2
UPPER = 256
LOWER = OWN - UPPER + FOLD
WIDE = 384
SENT = OWN + TAIL
TRIPS = ((3, -3), (4, 2), (-2, 1), (-1, 0))
F32 = jnp.float32
BF16 = jnp.bfloat16
VMEM = pltpu.VMEM


def fetch(value, dx, dy, dc):
    pairs = []
    for i in range(16):
        x, y, c = i >> 3, (i >> 1) & 3, i & 1
        pairs.append((((x ^ dx) << 3) + (((y + dy) & 3) << 1) + (c ^ dc), i))
    return lax.ppermute(value, "replica", pairs)


PLACES = tuple((dx, dy) for dx in range(2) for dy in range(4))


def owner(here, place):
    return (((here >> 3) ^ place[0]) << 2) + (((here >> 1) + place[1]) & 3)


def gather_blocks(own, turn):
    over, first, back = fetch(own, 1, 0, 0), fetch(own, 0, turn, 0), fetch(own, 0, -turn, 0)
    over_first, far, over_back = fetch(first, 1, 0, 0), fetch(first, 0, turn, 0), fetch(over, 0, -turn, 0)
    held = {(0, 0): own, (1, 0): over, (0, turn & 3): first, (0, -turn & 3): back}
    held.update({(1, turn & 3): over_first, (0, 2): far, (1, -turn & 3): over_back})
    if turn == 1:
        held[1, 2] = fetch(far, 1, 0, 0)
    else:
        held[1, 2] = fetch(over_back, 0, 1, 0)
    return [held[place] for place in PLACES]


def along_shard(value, dx, dz):
    pairs = [((((i >> 3) ^ dx) << 3) + ((i + dz) & 7), i) for i in range(16)]
    return lax.ppermute(value, "shard", pairs)


def factors(codes):
    out = jnp.ones(codes.shape, F32)
    for bit in range(5):
        out = out * jnp.where((codes >> bit) & 1 == 1, F32(2.0 ** -(2**bit)), F32(1.0))
    return out


def start_all(copies):
    for copy in copies:
        copy.start()


def pack_kernel(
    hidden, dq, dk, dv, do, sq, so, skt, svt,
    out, turned,
    vh, vq, vk, vv, vo, vsq, vso, vsk, vsv, buf, sems,
):
    pairs = [(hidden, vh), (sq, vsq), (so, vso), (skt, vsk), (svt, vsv)]
    pairs += [(dq, vq), (dk, vk), (dv, vv), (do, vo)]
    copies = [pltpu.make_async_copy(a, b, sems.at[i]) for i, (a, b) in enumerate(pairs)]
    start_all(copies)
    for copy in copies[:5]:
        copy.wait()
    for at, n in TILES:
        turned[at : at + n, :] = vh[:, at : at + n].astype(F32).T.astype(BF16)
    fq, fo, fk, fv = factors(vsq[...]), factors(vso[...]), factors(vsk[...]), factors(vsv[...])
    line = lax.broadcasted_iota(jnp.int32, (CUT, CUT), 0)
    lane = lax.broadcasted_iota(jnp.int32, (CUT, CUT), 1)

    def column(factor, head):
        spread = jnp.where(line == lane, factor[head : head + 1, :], 0.0)
        return jnp.sum(spread, axis=1, keepdims=True)

    def piece(codes, head, factor):
        return codes[:, head * HEAD : (head + 1) * HEAD].astype(F32) * factor

    for copy in copies[5:]:
        copy.wait()
    buf[6 * CUT : BLOCK, :] = jnp.zeros((BLOCK - 6 * CUT, HEAD), F32)
    for half in range(PARTS // 2):
        key, value = piece(vk, half, column(fk, half)), piece(vv, half, column(fv, half))
        for dest in (2 * half, 2 * half + 1):
            pieces = (
                piece(vq, 2 * dest, fq[:, 2 * dest : 2 * dest + 1]),
                piece(vq, 2 * dest + 1, fq[:, 2 * dest + 1 : 2 * dest + 2]),
                key,
                value,
                piece(vo, 2 * dest, fo[:, 2 * dest : 2 * dest + 1]),
                piece(vo, 2 * dest + 1, fo[:, 2 * dest + 1 : 2 * dest + 2]),
            )
            for c, item in enumerate(pieces):
                buf[CUT * c : CUT * (c + 1), :] = item
            out[dest] = buf[...].astype(BF16)


def refresh_kernel(
    here, recv, bq, bk, bv, bo, upper, lower, vq, vk, vv, vo, buf, delta, sems,
):
    at = pl.ds(pl.multiple_of(OWN * here[0], 64), OWN)
    bases = ((bq, vq), (bk, vk), (bv, vv), (bo, vo))
    copies = [
        pltpu.make_async_copy(a.at[at, :], b, sems.at[i]) for i, (a, b) in enumerate(bases)
    ]
    start_all(copies)
    for src in range(PARTS):
        buf[src % 2] = recv[src].astype(F32)
        for c in range(6):
            delta[CUT * src : CUT * (src + 1), HEAD * c : HEAD * (c + 1)] = buf[
                src % 2, CUT * c : CUT * (c + 1), :
            ]
    for copy in copies:
        copy.wait()
    for at, n, base in ((0, 256, vq), (256, 128, vk), (384, 128, vv)):
        value = (base[...].astype(F32) + delta[:, at : at + n]).astype(BF16)
        upper[:, at : at + n] = value[0:UPPER]
        lower[0 : OWN - UPPER, at : at + n] = value[UPPER:]
    for half in range(2):
        at = slice(half * FOLD, (half + 1) * FOLD)
        value = vo[at, :].astype(F32) + delta[at, 512:768]
        lower[OWN - UPPER :, half * 256 : (half + 1) * 256] = value.astype(BF16)


def dot_nt(a, b):
    return lax.dot_general(a, b, (((1,), (1,)), ((), ())), preferred_element_type=F32)


def dot(a, b):
    return jnp.dot(a, b, preferred_element_type=F32)


def head_norm_rotate(raw, gain, cosine, sine):
    value = raw * lax.rsqrt(jnp.mean(raw * raw, axis=-1, keepdims=True) + EPSILON) * gain
    swapped = jnp.concatenate([value[:, HEAD // 2 :], value[:, : HEAD // 2]], axis=-1)
    return value * cosine + swapped * sine


def group_scores(group, query, cache, fresh, lens):
    picked = [
        query[h * TOKENS + t * ROWS + group * GROUP : h * TOKENS + t * ROWS + (group + 1) * GROUP, :]
        for h in range(2)
        for t in range(STEPS)
    ]
    q = jnp.concatenate(picked, axis=0).astype(BF16)
    past = dot_nt(q, cache) * SCALE
    new = dot_nt(q, fresh) * SCALE
    n = 2 * STEPS * GROUP
    length = jnp.concatenate([lens[group * GROUP : (group + 1) * GROUP, :]] * (2 * STEPS), axis=0)
    column = lax.broadcasted_iota(jnp.int32, past.shape, 1)
    line = lax.broadcasted_iota(jnp.int32, past.shape, 0)
    past_ok = ((column >> 6) == (line & 7)) & ((column & 63) < length[:, 0:1])
    column = lax.broadcasted_iota(jnp.int32, (n, TOKENS), 1)
    line = lax.broadcasted_iota(jnp.int32, (n, TOKENS), 0)
    new_ok = ((column & 31) == group * GROUP + (line & 7)) & ((column >> 5) <= ((line >> 3) & 3))
    past = jnp.where(past_ok, past, NEG)
    new = jnp.where(new_ok, new, NEG)
    top = jnp.maximum(
        jnp.max(past, axis=-1, keepdims=True), jnp.max(new, axis=-1, keepdims=True)
    )
    past = jnp.exp(past - top)
    new = jnp.exp(new - top)
    total = jnp.sum(past, axis=-1, keepdims=True) + jnp.sum(new, axis=-1, keepdims=True)
    return past, new, total, top + jnp.log(total)


def put_groups(group, ref, value):
    for h in range(2):
        for t in range(STEPS):
            at = h * TOKENS + t * ROWS + group * GROUP
            i = (h * STEPS + t) * GROUP
            ref[at : at + GROUP, :] = value[i : i + GROUP, :]


def sample_logp(query, keys, one_query, lse):
    out = []
    for h in range(2):
        q = dot(one_query, query[h * TOKENS : (h + 1) * TOKENS, :].astype(BF16))
        score = jnp.sum(q * keys, axis=-1, keepdims=True) * SCALE
        line = lse[h * TOKENS : (h + 1) * TOKENS, :].T
        picked = jnp.sum(one_query.astype(F32) * line, axis=-1, keepdims=True)
        out.append(jnp.broadcast_to(score - picked, (TOKENS, HEAD)))
    return out


def normalise_kernel(here, seat, gain, pairs, keep, give):
    total = jnp.zeros((1, TOKENS), F32)
    for z in range(8):
        x = pairs[z].astype(F32)
        total = total + jnp.sum(x * x, axis=0, keepdims=True)
    scale = lax.rsqrt(total * (1.0 / WIDTH) + EPSILON)
    me, core = seat[0], here[0] & 1

    def put(z, target):
        for half in range(2):
            src = (((me >> 3) ^ half) << 3) + z
            for at, n in TILES:
                x = pairs[z, half * OWN + at : half * OWN + at + n, :].astype(F32) * scale
                value = (x.T * gain[src, :, at : at + n]).astype(BF16)
                target[src >> 1, :, at : at + n] = value
            target[src >> 1, :, OWN:] = jnp.zeros((TOKENS, WIDE - OWN), BF16)

    for z in range(8):
        pl.when(core == z & 1)(lambda z=z: put(z, keep))
        pl.when(core != z & 1)(lambda z=z: put(z, give))


def select_kernel(marks, cache_hbm, keys_out, one_q_out, one_f_out, cache, sems):
    copy = pltpu.make_async_copy(cache_hbm, cache, sems.at[0])
    copy.start()
    tokens = jnp.broadcast_to(marks[ROWS : ROWS + 1, :], (TOKENS, TOKENS)).T
    places = jnp.broadcast_to(marks[ROWS + 1 : ROWS + 2, :], (TOKENS, TOKENS)).T
    lane = lax.broadcasted_iota(jnp.int32, (TOKENS, TOKENS), 1)
    one_q = jnp.where(tokens == lane, F32(1.0), F32(0.0)).astype(BF16)
    one_f = jnp.where(places == lane + ROWS * CTX, F32(1.0), F32(0.0)).astype(BF16)
    copy.wait()
    keys = jnp.zeros((TOKENS, HEAD), F32)
    for k in range(ROWS * CTX // HEAD):
        one = jnp.where(places == lane + k * HEAD, F32(1.0), F32(0.0)).astype(BF16)
        keys = keys + dot(one, cache[k * HEAD : (k + 1) * HEAD, :])
    keys_out[...] = keys
    one_q_out[...] = one_q
    one_f_out[...] = one_f


def old_kernel(
    here, keep, give, table, marks, keys, one_q, one_f, base_q, base_k, cache_hbm,
    old_out,
    wq, wk, cache, query, lse, sems,
):
    quarter = WIDTH // 4
    copies = []
    for i in range(4):
        at = pl.ds(i * quarter, quarter)
        copies += [
            pltpu.make_async_copy(base_q.at[at, :], wq.at[at, :], sems.at[2 * i]),
            pltpu.make_async_copy(base_k.at[at, :], wk.at[at, :], sems.at[2 * i + 1]),
        ]
    copies.append(pltpu.make_async_copy(cache_hbm, cache, sems.at[8]))
    start_all(copies)
    core = here[0] & 1
    raw = jnp.zeros((TOKENS, 256), F32)
    raw_k = jnp.zeros((TOKENS, HEAD), F32)
    for j in range(HALF):
        if j % 2 == 0:
            copies[j].wait()
            copies[j + 1].wait()
        for lines, src in ((keep, 2 * j + core), (give, 2 * j + 1 - core)):
            at = pl.ds(pl.multiple_of(OWN * src, 64), OWN)
            raw = raw + dot(lines[j, :, 0:OWN], wq[at, :])
            raw_k = raw_k + dot(lines[j, :, 0:OWN], wk[at, :])
    copies[8].wait()
    cos, sin = table[0:TOKENS, :], table[TOKENS : 2 * TOKENS, :]
    qg, kg = table[2 * TOKENS : 2 * TOKENS + 1, :], table[2 * TOKENS + 1 : 2 * TOKENS + 2, :]
    lens = marks
    for h in range(2):
        query[h * TOKENS : (h + 1) * TOKENS, :] = (
            head_norm_rotate(raw[:, h * HEAD : (h + 1) * HEAD], qg, cos, sin)
            .astype(BF16)
            .astype(F32)
        )
    fresh = head_norm_rotate(raw_k, kg, cos, sin).astype(BF16)
    for g in range(GROUPS):
        _, _, _, log_sum = group_scores(
            g, query, cache[g * GROUP * CTX : (g + 1) * GROUP * CTX, :], fresh, lens
        )
        put_groups(g, lse, jnp.broadcast_to(log_sum, (log_sum.shape[0], HEAD)))
    old = sample_logp(query, keys[...] + dot(one_f[...], fresh), one_q[...], lse)
    old_out[0] = old[0]
    old_out[1] = old[1]


def project_kernel(here, keep, given, *rest):
    uppers, lowers, (own, other, below) = rest[0:8], rest[8:16], rest[16:]
    raw = jnp.zeros((2 * TOKENS, 512), F32)
    for place, upper, lower in zip(PLACES, uppers, lowers):
        j = owner(here[0], place)
        for at, n, weight in ((0, UPPER, upper), (UPPER, OWN - UPPER, lower)):
            lines = jnp.concatenate([keep[j, :, at : at + n], given[j, :, at : at + n]], axis=0)
            raw = raw + dot(lines, weight[0:n, :])
        below[j] = lower[OWN - UPPER :, :]
    own[...] = raw[0:TOKENS, :]
    other[...] = raw[TOKENS:, :]


def attend_kernel(
    here, seat, own, other, table, marks, cache_hbm, values_hbm, keys, one_q, one_f, old, mine, theirs,
    give0, give1, give2, give3, keep0, keep1, keep2, keep3,
    cache, values, query, lse, mixed, sems,
):
    copies = (
        pltpu.make_async_copy(cache_hbm, cache, sems.at[0]),
        pltpu.make_async_copy(values_hbm, values, sems.at[1]),
    )
    start_all(copies)
    raw = own[...] + other[...]
    cos, sin = table[0:TOKENS, :], table[TOKENS : 2 * TOKENS, :]
    qg, kg = table[2 * TOKENS : 2 * TOKENS + 1, :], table[2 * TOKENS + 1 : 2 * TOKENS + 2, :]
    lens = marks
    for h in range(2):
        query[h * TOKENS : (h + 1) * TOKENS, :] = (
            head_norm_rotate(raw[:, h * HEAD : (h + 1) * HEAD], qg, cos, sin)
            .astype(BF16)
            .astype(F32)
        )
    fresh = head_norm_rotate(raw[:, 256:384], kg, cos, sin).astype(BF16)
    fresh_v = raw[:, 384:512].astype(BF16)
    for copy in copies:
        copy.wait()
    for g in range(GROUPS):
        at = slice(g * GROUP * CTX, (g + 1) * GROUP * CTX)
        past, new, total, log_sum = group_scores(g, query, cache[at, :], fresh, lens)
        put_groups(g, lse, jnp.broadcast_to(log_sum, (log_sum.shape[0], HEAD)))
        mix = dot((past / total).astype(BF16), values[at, :])
        mix = mix + dot((new / total).astype(BF16), fresh_v)
        put_groups(g, mixed, mix)
    attended = jnp.concatenate([mixed[0:TOKENS, :], mixed[TOKENS:, :]], axis=1).astype(BF16)
    gives, keeps = (give0, give1, give2, give3), (keep0, keep1, keep2, keep3)
    me = seat[0]

    def place_parts(even, odd):
        for c, trips in enumerate(TRIPS):
            for i, dz in enumerate(trips):
                rows = odd if dz & 1 else even
                for dx, target in ((1, gives[c]), (0, keeps[c])):
                    j = (((me >> 3) ^ dx) << 2) + (((me + dz) & 7) >> 1)
                    for half in range(2):
                        part = dot_nt(rows[j, :, half * 256 : (half + 1) * 256], attended)
                        at = slice(half * FOLD, (half + 1) * FOLD)
                        target[i, at, :] = part.astype(target.dtype)

    same = ((here[0] ^ me) & 1) == 0
    pl.when(same)(lambda: place_parts(mine, theirs))
    pl.when(jnp.logical_not(same))(lambda: place_parts(theirs, mine))
    now = sample_logp(query, keys[...] + dot(one_f[...], fresh), one_q[...], lse)
    term = (now[0] - old[0]) + (now[1] - old[1])
    tail = split_line(term.T[0:1, :])
    for target in gives + keeps:
        for i in range(2):
            target[i, OWN:SENT, :] = tail.astype(target.dtype)


def split_line(line):
    high = line.astype(BF16).astype(F32)
    middle = (line - high).astype(BF16).astype(F32)
    low = line - high - middle
    return jnp.concatenate([high, middle, low, jnp.zeros((TAIL - 3, TOKENS), F32)], axis=0)


def merge_kernel(keep, recv, first, second):
    for i, out in enumerate((first, second)):
        total = keep[i] + recv[i].astype(F32)
        out[0:OWN, :] = total[0:OWN, :].astype(out.dtype)
        line = (total[OWN + 2 : OWN + 3, :] + total[OWN + 1 : OWN + 2, :]) + total[OWN : OWN + 1, :]
        out[OWN:SENT, :] = split_line(line).astype(out.dtype)


def finish_kernel(own, r1, r2, r3, r4, r5, r6, r7, out, ratio):
    for k, n in ((0, 128), (128, 128), (256, 80)):
        total = own[k : k + n, :]
        for part in (r1, r2, r3, r4, r5, r6, r7):
            total = total + part[k : k + n, :].astype(F32)
        if n == 128:
            out[:, k : k + n] = total.T.astype(BF16)
        else:
            tail = total[64:67, :]
            ratio[...] = ((tail[2:3, :] + tail[1:2, :]) + tail[0:1, :]) * (1.0 / HQ)
            out[:, k : k + 64] = total[0:64, :].T.astype(BF16)


def params(mib):
    return pltpu.CompilerParams(vmem_limit_bytes=mib * 1024 * 1024)


def shape(dims, dtype):
    return jax.ShapeDtypeStruct(dims, dtype)


def whole(*dims):
    return pl.BlockSpec(dims, lambda i: (0,) * len(dims))


def scalars(n=1):
    return [pl.BlockSpec(memory_space=pltpu.SMEM)] * n


def far_away(n=1):
    return [pl.BlockSpec(memory_space=pltpu.HBM)] * n


def spec_of(out):
    return whole(*out.shape)


def call(kernel, name, outs, in_specs, scratch, far=False, mib=56):
    several = isinstance(outs, tuple)
    return pl.pallas_call(
        kernel,
        name=name,
        grid=(1,),
        out_shape=outs,
        in_specs=in_specs,
        out_specs=far_away()[0] if far else tuple(map(spec_of, outs)) if several else spec_of(outs),
        scratch_shapes=scratch,
        compiler_params=params(mib),
    )


def local(
    hidden,
    norm_gain,
    query_gain,
    key_gain,
    base_query,
    base_key,
    base_value,
    base_output,
    delta_query,
    scale_query,
    key_delta_codes,
    key_scale_codes,
    value_delta_codes,
    value_scale_codes,
    delta_output,
    scale_output,
    cache_keys,
    cache_values,
    lengths,
    stale_rows,
    stale_steps,
    stale_back,
):
    here = lax.axis_index("replica").astype(jnp.int32).reshape(1)
    seat = lax.axis_index("shard").astype(jnp.int32).reshape(1)
    dma = pltpu.SemaphoreType.DMA
    packed, turned = call(
        pack_kernel,
        "pack",
        (shape((PARTS, BLOCK, HEAD), BF16), shape((OWN, TOKENS), BF16)),
        far_away(9),
        [
            VMEM((TOKENS, OWN), BF16),
            VMEM((CUT, HQ * HEAD), BF16),
            VMEM((CUT, KV * HEAD), BF16),
            VMEM((CUT, KV * HEAD), BF16),
            VMEM((CUT, HQ * HEAD), BF16),
            VMEM((CUT, HQ), jnp.int32),
            VMEM((CUT, HQ), jnp.int32),
            VMEM((KV, CUT), jnp.int32),
            VMEM((KV, CUT), jnp.int32),
            VMEM((BLOCK, HEAD), F32),
            dma((9,)),
        ],
        mib=56,
    )(
        hidden.reshape(TOKENS, OWN), delta_query, key_delta_codes, value_delta_codes, delta_output,
        scale_query, scale_output, key_scale_codes.T, value_scale_codes.T,
    )
    across = along_shard(turned, 1, 0)
    arrived = lax.all_to_all(packed, "shard", split_axis=0, concat_axis=0, tiled=False)
    spread = jnp.concatenate([turned, across], axis=0)
    spread = jnp.broadcast_to(spread[None], (8, 2 * OWN, TOKENS))
    arrived, spread, lengths, stale_rows, stale_steps, stale_back = lax.optimization_barrier(
        (arrived, spread, lengths, stale_rows, stale_steps, stale_back)
    )
    upper, lower = call(
        refresh_kernel,
        "refresh",
        (shape((UPPER, 512), BF16), shape((LOWER, 512), BF16)),
        scalars() + [whole(PARTS, BLOCK, HEAD)] + far_away(4),
        [
            VMEM((OWN, 256), BF16),
            VMEM((OWN, 128), BF16),
            VMEM((OWN, 128), BF16),
            VMEM((OWN, 256), BF16),
            VMEM((2, BLOCK, HEAD), F32),
            VMEM((OWN, 768), F32),
            dma((4,)),
        ],
        mib=56,
    )(here, arrived, base_query, base_key, base_value, base_output)
    upper, lower, spread = lax.optimization_barrier((upper, lower, spread))
    uppers, lowers = gather_blocks(upper, 1), gather_blocks(lower, -1)
    rings = [[8 * x + z for z in range(8)] for x in range(2)]
    hidden_t = lax.all_to_all(
        spread,
        "shard",
        split_axis=0,
        concat_axis=0,
        tiled=False,
        axis_index_groups=rings,
    )

    position = (lengths[None, :] + jnp.arange(STEPS)[:, None]).reshape(TOKENS)
    freq = THETA ** (-(jnp.arange(HEAD // 2).astype(F32) * 2.0) / HEAD)
    angle = position.astype(F32)[:, None] * freq
    cos, sin = jnp.cos(angle), jnp.sin(angle)
    table = jnp.concatenate(
        [
            jnp.concatenate([cos, cos], axis=1),
            jnp.concatenate([-sin, sin], axis=1),
            query_gain.reshape(1, HEAD),
            key_gain.reshape(1, HEAD),
            jnp.zeros((6, HEAD), F32),
        ],
        axis=0,
    )
    rows_s, steps_s, back_s = stale_rows, stale_steps, stale_back
    lens_s = jnp.sum(
        jnp.where(rows_s[0][None, :] == jnp.arange(ROWS)[:, None], lengths[:, None], 0),
        axis=0,
        keepdims=True,
    )
    at = lens_s + steps_s - back_s % (lens_s + steps_s + 1)
    place = jnp.where(
        at >= lens_s, ROWS * CTX + (at - lens_s) * ROWS + rows_s, rows_s * CTX + at
    ).astype(jnp.int32)
    token = (steps_s * ROWS + rows_s).astype(jnp.int32)
    marks = jnp.concatenate(
        [
            jnp.broadcast_to(lengths[:, None], (ROWS, HEAD)),
            token,
            place,
            jnp.zeros((6, HEAD), jnp.int32),
        ],
        axis=0,
    )
    cache = cache_keys.reshape(ROWS * CTX, HEAD)
    values = cache_values.reshape(ROWS * CTX, HEAD)

    keys, one_q, one_f = call(
        select_kernel,
        "select",
        (
            shape((TOKENS, HEAD), F32),
            shape((TOKENS, TOKENS), BF16),
            shape((TOKENS, TOKENS), BF16),
        ),
        [whole(ROWS + 8, HEAD)] + far_away(),
        [VMEM((ROWS * CTX, HEAD), BF16), dma((1,))],
        mib=8,
    )(marks, cache)
    later = uppers + lowers
    hidden_t, keys, one_q, one_f, table, _ = lax.optimization_barrier(
        (hidden_t, keys, one_q, one_f, table, later)
    )
    keep, give = call(
        normalise_kernel,
        "normalise",
        (
            shape((HALF, TOKENS, WIDE), BF16),
            shape((HALF, TOKENS, WIDE), BF16),
        ),
        scalars(2) + [whole(PARTS, 1, OWN)] + [whole(8, 2 * OWN, TOKENS)],
        [],
        mib=16,
    )(here, seat, norm_gain.reshape(PARTS, 1, OWN), hidden_t)
    given = fetch(give, 0, 0, 1)

    old = call(
        old_kernel,
        "old",
        shape((2, TOKENS, HEAD), F32),
        scalars()
        + [whole(HALF, TOKENS, WIDE)] * 2
        + [whole(2 * TOKENS + 8, HEAD), whole(ROWS + 8, HEAD)]
        + [whole(TOKENS, HEAD)] * 3
        + far_away(3),
        [
            VMEM((WIDTH, 256), BF16),
            VMEM((WIDTH, HEAD), BF16),
            VMEM((ROWS * CTX, HEAD), BF16),
            VMEM((2 * TOKENS, HEAD), F32),
            VMEM((2 * TOKENS, HEAD), F32),
            dma((9,)),
        ],
        mib=24,
    )(here, keep, give, table, marks, keys, one_q, one_f, base_query, base_key, cache)

    own, other, mine = call(
        project_kernel,
        "project",
        (
            shape((TOKENS, 512), F32),
            shape((TOKENS, 512), F32),
            shape((HALF, FOLD, 512), BF16),
        ),
        scalars()
        + [whole(HALF, TOKENS, WIDE)] * 2
        + [whole(UPPER, 512)] * 8
        + [whole(LOWER, 512)] * 8,
        [],
        mib=24,
    )(here, keep, given, *uppers, *lowers)
    other = fetch(other, 0, 0, 1)
    theirs = fetch(mine, 0, 0, 1)

    parts = call(
        attend_kernel,
        "attend",
        (shape((2, SENT, HEAD), BF16),) * 4 + (shape((2, SENT, HEAD), F32),) * 4,
        scalars(2)
        + [whole(TOKENS, 512)] * 2
        + [whole(2 * TOKENS + 8, HEAD), whole(ROWS + 8, HEAD)]
        + far_away(2)
        + [whole(TOKENS, HEAD)] * 3
        + [whole(2, TOKENS, HEAD)]
        + [whole(HALF, FOLD, 512)] * 2,
        [
            VMEM((ROWS * CTX, HEAD), BF16),
            VMEM((ROWS * CTX, HEAD), BF16),
            VMEM((2 * TOKENS, HEAD), F32),
            VMEM((2 * TOKENS, HEAD), F32),
            VMEM((2 * TOKENS, HEAD), F32),
            dma((2,)),
        ],
        mib=24,
    )(here, seat, own, other, table, marks, cache, values, keys, one_q, one_f, old, mine, theirs)
    crossed = [along_shard(give, 1, 0) for give in parts[:4]]
    landed = []
    for trips, keep_part, recv in zip(TRIPS, parts[4:], crossed):
        kinds = tuple(shape((SENT, HEAD), BF16 if dz else F32) for dz in trips)
        sums = call(
            merge_kernel, "merge", kinds, [whole(2, SENT, HEAD)] * 2, [], mib=8
        )(keep_part, recv)
        landed += [along_shard(part, 0, -dz) if dz else part for dz, part in zip(trips, sums)]
    out, ratio = call(
        finish_kernel,
        "finish",
        (shape((TOKENS, OWN), BF16), shape((1, TOKENS), F32)),
        [whole(SENT, HEAD)] * 8,
        [],
        mib=16,
    )(landed[-1], *landed[:-1])
    return out.reshape(STEPS, ROWS, OWN), ratio


def solution(mesh):
    return jax.shard_map(
        local,
        mesh=mesh,
        in_specs=(
            P(None, "replica", "shard"),
            P(),
            P(),
            P(),
            P(None, "shard"),
            P(None, "shard"),
            P(None, "shard"),
            P(None, "shard"),
            P(("replica", "shard"), None),
            P(("replica", "shard"), None),
            P(("replica", "shard"), None),
            P(("replica", "shard"), None),
            P(("replica", "shard"), None),
            P(("replica", "shard"), None),
            P(("replica", "shard"), None),
            P(("replica", "shard"), None),
            P("replica", None, "shard"),
            P("replica", None, "shard"),
            P("replica"),
            P("replica", None),
            P("replica", None),
            P("replica", None),
        ),
        out_specs=(P(None, "replica", "shard"), P("replica", None)),
        check_vma=False,
    )
```

```python
import jax
import jax.numpy as jnp
from jax import lax
from jax.experimental import pallas as pl
from jax.experimental.pallas import tpu as pltpu
from jax.sharding import PartitionSpec as P

HQ = 32
KV = 8
HEAD = 128
WIDTH = 5120
STEPS = 4
ROWS = 32
TOKENS = STEPS * ROWS
CTX = 64
PARTS = 16
OWN = WIDTH // PARTS
CUT = 20
GROUP = 8
GROUPS = ROWS // GROUP
TAIL = 16
EPSILON = 1e-06
THETA = 1000000.0
SCALE = HEAD ** (-0.5)
NEG = -1e30
TILES = ((0, 128), (128, 128), (256, 64))
BLOCK = 128
HALF = PARTS // 2
FOLD = OWN // 2
UPPER = 256
LOWER = OWN - UPPER + FOLD
WIDE = 384
SENT = OWN + TAIL
TRIPS = ((3, -3), (4, 2), (-2, 1), (-1, 0))
F32 = jnp.float32
BF16 = jnp.bfloat16
VMEM = pltpu.VMEM


def fetch(value, dx, dy, dc):
    pairs = []
    for i in range(16):
        x, y, c = i >> 3, (i >> 1) & 3, i & 1
        pairs.append((((x ^ dx) << 3) + (((y + dy) & 3) << 1) + (c ^ dc), i))
    return lax.ppermute(value, "replica", pairs)


PLACES = tuple((dx, dy) for dx in range(2) for dy in range(4))


def owner(here, place):
    return (((here >> 3) ^ place[0]) << 2) + (((here >> 1) + place[1]) & 3)


def gather_blocks(own, turn):
    over, first, back = fetch(own, 1, 0, 0), fetch(own, 0, turn, 0), fetch(own, 0, -turn, 0)
    over_first, far, over_back = fetch(first, 1, 0, 0), fetch(first, 0, turn, 0), fetch(over, 0, -turn, 0)
    held = {(0, 0): own, (1, 0): over, (0, turn & 3): first, (0, -turn & 3): back}
    held.update({(1, turn & 3): over_first, (0, 2): far, (1, -turn & 3): over_back})
    if turn == 1:
        held[1, 2] = fetch(far, 1, 0, 0)
    else:
        held[1, 2] = fetch(over_back, 0, 1, 0)
    return [held[place] for place in PLACES]


def along_shard(value, dx, dz):
    pairs = [((((i >> 3) ^ dx) << 3) + ((i + dz) & 7), i) for i in range(16)]
    return lax.ppermute(value, "shard", pairs)


def factors(codes):
    out = jnp.ones(codes.shape, F32)
    for bit in range(5):
        out = out * jnp.where((codes >> bit) & 1 == 1, F32(2.0 ** -(2**bit)), F32(1.0))
    return out


def start_all(copies):
    for copy in copies:
        copy.start()


def pack_kernel(
    hidden, dq, dk, dv, do, sq, so, skt, svt,
    out, turned,
    vh, vq, vk, vv, vo, vsq, vso, vsk, vsv, buf, sems,
):
    pairs = [(hidden, vh), (sq, vsq), (so, vso), (skt, vsk), (svt, vsv)]
    pairs += [(dq, vq), (dk, vk), (dv, vv), (do, vo)]
    copies = [pltpu.make_async_copy(a, b, sems.at[i]) for i, (a, b) in enumerate(pairs)]
    start_all(copies)
    for copy in copies[:5]:
        copy.wait()
    for at, n in TILES:
        turned[at : at + n, :] = vh[:, at : at + n].astype(F32).T.astype(BF16)
    fq, fo, fk, fv = factors(vsq[...]), factors(vso[...]), factors(vsk[...]), factors(vsv[...])
    line = lax.broadcasted_iota(jnp.int32, (CUT, CUT), 0)
    lane = lax.broadcasted_iota(jnp.int32, (CUT, CUT), 1)

    def column(factor, head):
        spread = jnp.where(line == lane, factor[head : head + 1, :], 0.0)
        return jnp.sum(spread, axis=1, keepdims=True)

    def piece(codes, head, factor):
        return codes[:, head * HEAD : (head + 1) * HEAD].astype(F32) * factor

    for copy in copies[5:]:
        copy.wait()
    buf[6 * CUT : BLOCK, :] = jnp.zeros((BLOCK - 6 * CUT, HEAD), F32)
    for half in range(PARTS // 2):
        key, value = piece(vk, half, column(fk, half)), piece(vv, half, column(fv, half))
        for dest in (2 * half, 2 * half + 1):
            pieces = (
                piece(vq, 2 * dest, fq[:, 2 * dest : 2 * dest + 1]),
                piece(vq, 2 * dest + 1, fq[:, 2 * dest + 1 : 2 * dest + 2]),
                key,
                value,
                piece(vo, 2 * dest, fo[:, 2 * dest : 2 * dest + 1]),
                piece(vo, 2 * dest + 1, fo[:, 2 * dest + 1 : 2 * dest + 2]),
            )
            for c, item in enumerate(pieces):
                buf[CUT * c : CUT * (c + 1), :] = item
            out[dest] = buf[...].astype(BF16)


def spread_kernel(turned, across, out, pair, sems):
    pair[0:OWN, :] = turned[...]
    pair[OWN:, :] = across[...]
    copies = [pltpu.make_async_copy(pair, out.at[z], sems.at[z]) for z in range(8)]
    start_all(copies)
    for copy in copies:
        copy.wait()


def refresh_kernel(
    here, recv, bq, bk, bv, bo, upper, lower, vq, vk, vv, vo, buf, delta, sems,
):
    at = pl.ds(pl.multiple_of(OWN * here[0], 64), OWN)
    bases = ((bq, vq), (bk, vk), (bv, vv), (bo, vo))
    copies = [
        pltpu.make_async_copy(a.at[at, :], b, sems.at[i]) for i, (a, b) in enumerate(bases)
    ]
    start_all(copies)
    for src in range(PARTS):
        buf[src % 2] = recv[src].astype(F32)
        for c in range(6):
            delta[CUT * src : CUT * (src + 1), HEAD * c : HEAD * (c + 1)] = buf[
                src % 2, CUT * c : CUT * (c + 1), :
            ]
    for copy in copies:
        copy.wait()
    for at, n, base in ((0, 256, vq), (256, 128, vk), (384, 128, vv)):
        value = (base[...].astype(F32) + delta[:, at : at + n]).astype(BF16)
        upper[:, at : at + n] = value[0:UPPER]
        lower[0 : OWN - UPPER, at : at + n] = value[UPPER:]
    for half in range(2):
        at = slice(half * FOLD, (half + 1) * FOLD)
        value = vo[at, :].astype(F32) + delta[at, 512:768]
        lower[OWN - UPPER :, half * 256 : (half + 1) * 256] = value.astype(BF16)


def dot_nt(a, b):
    return lax.dot_general(a, b, (((1,), (1,)), ((), ())), preferred_element_type=F32)


def dot(a, b):
    return jnp.dot(a, b, preferred_element_type=F32)


def head_norm_rotate(raw, gain, cosine, sine):
    value = raw * lax.rsqrt(jnp.mean(raw * raw, axis=-1, keepdims=True) + EPSILON) * gain
    swapped = jnp.concatenate([value[:, HEAD // 2 :], value[:, : HEAD // 2]], axis=-1)
    return value * cosine + swapped * sine


def group_scores(group, query, cache, fresh, lens):
    picked = [
        query[h * TOKENS + t * ROWS + group * GROUP : h * TOKENS + t * ROWS + (group + 1) * GROUP, :]
        for h in range(2)
        for t in range(STEPS)
    ]
    q = jnp.concatenate(picked, axis=0).astype(BF16)
    past = dot_nt(q, cache) * SCALE
    new = dot_nt(q, fresh) * SCALE
    n = 2 * STEPS * GROUP
    length = jnp.concatenate([lens[group * GROUP : (group + 1) * GROUP, :]] * (2 * STEPS), axis=0)
    column = lax.broadcasted_iota(jnp.int32, past.shape, 1)
    line = lax.broadcasted_iota(jnp.int32, past.shape, 0)
    past_ok = ((column >> 6) == (line & 7)) & ((column & 63) < length[:, 0:1])
    column = lax.broadcasted_iota(jnp.int32, (n, TOKENS), 1)
    line = lax.broadcasted_iota(jnp.int32, (n, TOKENS), 0)
    new_ok = ((column & 31) == group * GROUP + (line & 7)) & ((column >> 5) <= ((line >> 3) & 3))
    past = jnp.where(past_ok, past, NEG)
    new = jnp.where(new_ok, new, NEG)
    top = jnp.maximum(
        jnp.max(past, axis=-1, keepdims=True), jnp.max(new, axis=-1, keepdims=True)
    )
    past = jnp.exp(past - top)
    new = jnp.exp(new - top)
    total = jnp.sum(past, axis=-1, keepdims=True) + jnp.sum(new, axis=-1, keepdims=True)
    return past, new, total, top + jnp.log(total)


def put_groups(group, ref, value):
    for h in range(2):
        for t in range(STEPS):
            at = h * TOKENS + t * ROWS + group * GROUP
            i = (h * STEPS + t) * GROUP
            ref[at : at + GROUP, :] = value[i : i + GROUP, :]


def sample_logp(query, keys, one_query, lse):
    out = []
    for h in range(2):
        q = dot(one_query, query[h * TOKENS : (h + 1) * TOKENS, :].astype(BF16))
        score = jnp.sum(q * keys, axis=-1, keepdims=True) * SCALE
        line = lse[h * TOKENS : (h + 1) * TOKENS, :].T
        picked = jnp.sum(one_query.astype(F32) * line, axis=-1, keepdims=True)
        out.append(jnp.broadcast_to(score - picked, (TOKENS, HEAD)))
    return out


def normalise_kernel(here, seat, gain, pairs, keep, give):
    total = jnp.zeros((1, TOKENS), F32)
    for z in range(8):
        x = pairs[z].astype(F32)
        total = total + jnp.sum(x * x, axis=0, keepdims=True)
    scale = lax.rsqrt(total * (1.0 / WIDTH) + EPSILON)
    me, core = seat[0], here[0] & 1

    def put(z, target):
        for half in range(2):
            src = (((me >> 3) ^ half) << 3) + z
            for at, n in TILES:
                x = pairs[z, half * OWN + at : half * OWN + at + n, :].astype(F32) * scale
                value = (x.T * gain[src, :, at : at + n]).astype(BF16)
                target[src >> 1, :, at : at + n] = value
            target[src >> 1, :, OWN:] = jnp.zeros((TOKENS, WIDE - OWN), BF16)

    for z in range(8):
        pl.when(core == z & 1)(lambda z=z: put(z, keep))
        pl.when(core != z & 1)(lambda z=z: put(z, give))


def select_kernel(marks, cache_hbm, keys_out, one_q_out, one_f_out, cache, sems):
    copy = pltpu.make_async_copy(cache_hbm, cache, sems.at[0])
    copy.start()
    tokens = jnp.broadcast_to(marks[ROWS : ROWS + 1, :], (TOKENS, TOKENS)).T
    places = jnp.broadcast_to(marks[ROWS + 1 : ROWS + 2, :], (TOKENS, TOKENS)).T
    lane = lax.broadcasted_iota(jnp.int32, (TOKENS, TOKENS), 1)
    one_q = jnp.where(tokens == lane, F32(1.0), F32(0.0)).astype(BF16)
    one_f = jnp.where(places == lane + ROWS * CTX, F32(1.0), F32(0.0)).astype(BF16)
    copy.wait()
    keys = jnp.zeros((TOKENS, HEAD), F32)
    for k in range(ROWS * CTX // HEAD):
        one = jnp.where(places == lane + k * HEAD, F32(1.0), F32(0.0)).astype(BF16)
        keys = keys + dot(one, cache[k * HEAD : (k + 1) * HEAD, :])
    keys_out[...] = keys
    one_q_out[...] = one_q
    one_f_out[...] = one_f


def old_kernel(
    here, keep, give, table, marks, keys, one_q, one_f, base_q, base_k, cache_hbm,
    old_out,
    wq, wk, cache, query, lse, sems,
):
    quarter = WIDTH // 4
    copies = []
    for i in range(4):
        at = pl.ds(i * quarter, quarter)
        copies += [
            pltpu.make_async_copy(base_q.at[at, :], wq.at[at, :], sems.at[2 * i]),
            pltpu.make_async_copy(base_k.at[at, :], wk.at[at, :], sems.at[2 * i + 1]),
        ]
    copies.append(pltpu.make_async_copy(cache_hbm, cache, sems.at[8]))
    start_all(copies)
    core = here[0] & 1
    raw = jnp.zeros((TOKENS, 256), F32)
    raw_k = jnp.zeros((TOKENS, HEAD), F32)
    for j in range(HALF):
        if j % 2 == 0:
            copies[j].wait()
            copies[j + 1].wait()
        for lines, src in ((keep, 2 * j + core), (give, 2 * j + 1 - core)):
            at = pl.ds(pl.multiple_of(OWN * src, 64), OWN)
            raw = raw + dot(lines[j, :, 0:OWN], wq[at, :])
            raw_k = raw_k + dot(lines[j, :, 0:OWN], wk[at, :])
    copies[8].wait()
    cos, sin = table[0:TOKENS, :], table[TOKENS : 2 * TOKENS, :]
    qg, kg = table[2 * TOKENS : 2 * TOKENS + 1, :], table[2 * TOKENS + 1 : 2 * TOKENS + 2, :]
    lens = marks
    for h in range(2):
        query[h * TOKENS : (h + 1) * TOKENS, :] = (
            head_norm_rotate(raw[:, h * HEAD : (h + 1) * HEAD], qg, cos, sin)
            .astype(BF16)
            .astype(F32)
        )
    fresh = head_norm_rotate(raw_k, kg, cos, sin).astype(BF16)
    for g in range(GROUPS):
        _, _, _, log_sum = group_scores(
            g, query, cache[g * GROUP * CTX : (g + 1) * GROUP * CTX, :], fresh, lens
        )
        put_groups(g, lse, jnp.broadcast_to(log_sum, (log_sum.shape[0], HEAD)))
    old = sample_logp(query, keys[...] + dot(one_f[...], fresh), one_q[...], lse)
    old_out[0] = old[0]
    old_out[1] = old[1]


def project_kernel(here, keep, given, *rest):
    uppers, lowers, (own, other, below) = rest[0:8], rest[8:16], rest[16:]
    raw = jnp.zeros((2 * TOKENS, 512), F32)
    for place, upper, lower in zip(PLACES, uppers, lowers):
        j = owner(here[0], place)
        for at, n, weight in ((0, UPPER, upper), (UPPER, OWN - UPPER, lower)):
            lines = jnp.concatenate([keep[j, :, at : at + n], given[j, :, at : at + n]], axis=0)
            raw = raw + dot(lines, weight[0:n, :])
        below[j] = lower[OWN - UPPER :, :]
    own[...] = raw[0:TOKENS, :]
    other[...] = raw[TOKENS:, :]


def attend_kernel(
    here, seat, own, other, table, marks, cache_hbm, values_hbm, keys, one_q, one_f, old, mine, theirs,
    give0, give1, give2, give3, keep0, keep1, keep2, keep3,
    cache, values, query, lse, mixed, sems,
):
    copies = (
        pltpu.make_async_copy(cache_hbm, cache, sems.at[0]),
        pltpu.make_async_copy(values_hbm, values, sems.at[1]),
    )
    start_all(copies)
    raw = own[...] + other[...]
    cos, sin = table[0:TOKENS, :], table[TOKENS : 2 * TOKENS, :]
    qg, kg = table[2 * TOKENS : 2 * TOKENS + 1, :], table[2 * TOKENS + 1 : 2 * TOKENS + 2, :]
    lens = marks
    for h in range(2):
        query[h * TOKENS : (h + 1) * TOKENS, :] = (
            head_norm_rotate(raw[:, h * HEAD : (h + 1) * HEAD], qg, cos, sin)
            .astype(BF16)
            .astype(F32)
        )
    fresh = head_norm_rotate(raw[:, 256:384], kg, cos, sin).astype(BF16)
    fresh_v = raw[:, 384:512].astype(BF16)
    for copy in copies:
        copy.wait()
    for g in range(GROUPS):
        at = slice(g * GROUP * CTX, (g + 1) * GROUP * CTX)
        past, new, total, log_sum = group_scores(g, query, cache[at, :], fresh, lens)
        put_groups(g, lse, jnp.broadcast_to(log_sum, (log_sum.shape[0], HEAD)))
        mix = dot((past / total).astype(BF16), values[at, :])
        mix = mix + dot((new / total).astype(BF16), fresh_v)
        put_groups(g, mixed, mix)
    attended = jnp.concatenate([mixed[0:TOKENS, :], mixed[TOKENS:, :]], axis=1).astype(BF16)
    gives, keeps = (give0, give1, give2, give3), (keep0, keep1, keep2, keep3)
    me = seat[0]

    def place_parts(even, odd):
        for c, trips in enumerate(TRIPS):
            for i, dz in enumerate(trips):
                rows = odd if dz & 1 else even
                for dx, target in ((1, gives[c]), (0, keeps[c])):
                    j = (((me >> 3) ^ dx) << 2) + (((me + dz) & 7) >> 1)
                    for half in range(2):
                        part = dot_nt(rows[j, :, half * 256 : (half + 1) * 256], attended)
                        at = slice(half * FOLD, (half + 1) * FOLD)
                        target[i, at, :] = part.astype(target.dtype)

    same = ((here[0] ^ me) & 1) == 0
    pl.when(same)(lambda: place_parts(mine, theirs))
    pl.when(jnp.logical_not(same))(lambda: place_parts(theirs, mine))
    now = sample_logp(query, keys[...] + dot(one_f[...], fresh), one_q[...], lse)
    term = (now[0] - old[0]) + (now[1] - old[1])
    tail = split_line(term.T[0:1, :])
    for target in gives + keeps:
        for i in range(2):
            target[i, OWN:SENT, :] = tail.astype(target.dtype)


def split_line(line):
    high = line.astype(BF16).astype(F32)
    middle = (line - high).astype(BF16).astype(F32)
    low = line - high - middle
    return jnp.concatenate([high, middle, low, jnp.zeros((TAIL - 3, TOKENS), F32)], axis=0)


def merge_kernel(keep, recv, first, second):
    for i, out in enumerate((first, second)):
        total = keep[i] + recv[i].astype(F32)
        out[0:OWN, :] = total[0:OWN, :].astype(out.dtype)
        line = (total[OWN + 2 : OWN + 3, :] + total[OWN + 1 : OWN + 2, :]) + total[OWN : OWN + 1, :]
        out[OWN:SENT, :] = split_line(line).astype(out.dtype)


def finish_kernel(own, r1, r2, r3, r4, r5, r6, r7, out, ratio):
    for k, n in ((0, 128), (128, 128), (256, 80)):
        total = own[k : k + n, :]
        for part in (r1, r2, r3, r4, r5, r6, r7):
            total = total + part[k : k + n, :].astype(F32)
        if n == 128:
            out[:, k : k + n] = total.T.astype(BF16)
        else:
            tail = total[64:67, :]
            ratio[...] = ((tail[2:3, :] + tail[1:2, :]) + tail[0:1, :]) * (1.0 / HQ)
            out[:, k : k + 64] = total[0:64, :].T.astype(BF16)


def params(mib):
    return pltpu.CompilerParams(vmem_limit_bytes=mib * 1024 * 1024)


def shape(dims, dtype):
    return jax.ShapeDtypeStruct(dims, dtype)


def whole(*dims):
    return pl.BlockSpec(dims, lambda i: (0,) * len(dims))


def scalars(n=1):
    return [pl.BlockSpec(memory_space=pltpu.SMEM)] * n


def far_away(n=1):
    return [pl.BlockSpec(memory_space=pltpu.HBM)] * n


def spec_of(out):
    return whole(*out.shape)


def call(kernel, name, outs, in_specs, scratch, far=False, mib=56):
    several = isinstance(outs, tuple)
    return pl.pallas_call(
        kernel,
        name=name,
        grid=(1,),
        out_shape=outs,
        in_specs=in_specs,
        out_specs=far_away()[0] if far else tuple(map(spec_of, outs)) if several else spec_of(outs),
        scratch_shapes=scratch,
        compiler_params=params(mib),
    )


def local(
    hidden,
    norm_gain,
    query_gain,
    key_gain,
    base_query,
    base_key,
    base_value,
    base_output,
    delta_query,
    scale_query,
    key_delta_codes,
    key_scale_codes,
    value_delta_codes,
    value_scale_codes,
    delta_output,
    scale_output,
    cache_keys,
    cache_values,
    lengths,
    stale_rows,
    stale_steps,
    stale_back,
):
    here = lax.axis_index("replica").astype(jnp.int32).reshape(1)
    seat = lax.axis_index("shard").astype(jnp.int32).reshape(1)
    dma = pltpu.SemaphoreType.DMA
    packed, turned = call(
        pack_kernel,
        "pack",
        (shape((PARTS, BLOCK, HEAD), BF16), shape((OWN, TOKENS), BF16)),
        far_away(9),
        [
            VMEM((TOKENS, OWN), BF16),
            VMEM((CUT, HQ * HEAD), BF16),
            VMEM((CUT, KV * HEAD), BF16),
            VMEM((CUT, KV * HEAD), BF16),
            VMEM((CUT, HQ * HEAD), BF16),
            VMEM((CUT, HQ), jnp.int32),
            VMEM((CUT, HQ), jnp.int32),
            VMEM((KV, CUT), jnp.int32),
            VMEM((KV, CUT), jnp.int32),
            VMEM((BLOCK, HEAD), F32),
            dma((9,)),
        ],
        mib=56,
    )(
        hidden.reshape(TOKENS, OWN), delta_query, key_delta_codes, value_delta_codes, delta_output,
        scale_query, scale_output, key_scale_codes.T, value_scale_codes.T,
    )
    across = along_shard(turned, 1, 0)
    arrived = lax.all_to_all(packed, "shard", split_axis=0, concat_axis=0, tiled=False)
    spread = call(
        spread_kernel,
        "spread",
        shape((8, 2 * OWN, TOKENS), BF16),
        [whole(OWN, TOKENS)] * 2,
        [VMEM((2 * OWN, TOKENS), BF16), dma((8,))],
        True,
        mib=24,
    )(turned, across)
    arrived, spread, lengths, stale_rows, stale_steps, stale_back = lax.optimization_barrier(
        (arrived, spread, lengths, stale_rows, stale_steps, stale_back)
    )
    upper, lower = call(
        refresh_kernel,
        "refresh",
        (shape((UPPER, 512), BF16), shape((LOWER, 512), BF16)),
        scalars() + [whole(PARTS, BLOCK, HEAD)] + far_away(4),
        [
            VMEM((OWN, 256), BF16),
            VMEM((OWN, 128), BF16),
            VMEM((OWN, 128), BF16),
            VMEM((OWN, 256), BF16),
            VMEM((2, BLOCK, HEAD), F32),
            VMEM((OWN, 768), F32),
            dma((4,)),
        ],
        mib=56,
    )(here, arrived, base_query, base_key, base_value, base_output)
    uppers, lowers = gather_blocks(upper, 1), gather_blocks(lower, -1)
    rings = [[8 * x + z for z in range(8)] for x in range(2)]
    hidden_t = lax.all_to_all(
        spread,
        "shard",
        split_axis=0,
        concat_axis=0,
        tiled=False,
        axis_index_groups=rings,
    )

    position = (lengths[None, :] + jnp.arange(STEPS)[:, None]).reshape(TOKENS)
    freq = THETA ** (-(jnp.arange(HEAD // 2).astype(F32) * 2.0) / HEAD)
    angle = position.astype(F32)[:, None] * freq
    cos, sin = jnp.cos(angle), jnp.sin(angle)
    table = jnp.concatenate(
        [
            jnp.concatenate([cos, cos], axis=1),
            jnp.concatenate([-sin, sin], axis=1),
            query_gain.reshape(1, HEAD),
            key_gain.reshape(1, HEAD),
            jnp.zeros((6, HEAD), F32),
        ],
        axis=0,
    )
    rows_s, steps_s, back_s = stale_rows, stale_steps, stale_back
    lens_s = jnp.sum(
        jnp.where(rows_s[0][None, :] == jnp.arange(ROWS)[:, None], lengths[:, None], 0),
        axis=0,
        keepdims=True,
    )
    at = lens_s + steps_s - back_s % (lens_s + steps_s + 1)
    place = jnp.where(
        at >= lens_s, ROWS * CTX + (at - lens_s) * ROWS + rows_s, rows_s * CTX + at
    ).astype(jnp.int32)
    token = (steps_s * ROWS + rows_s).astype(jnp.int32)
    marks = jnp.concatenate(
        [
            jnp.broadcast_to(lengths[:, None], (ROWS, HEAD)),
            token,
            place,
            jnp.zeros((6, HEAD), jnp.int32),
        ],
        axis=0,
    )
    cache = cache_keys.reshape(ROWS * CTX, HEAD)
    values = cache_values.reshape(ROWS * CTX, HEAD)

    keys, one_q, one_f = call(
        select_kernel,
        "select",
        (
            shape((TOKENS, HEAD), F32),
            shape((TOKENS, TOKENS), BF16),
            shape((TOKENS, TOKENS), BF16),
        ),
        [whole(ROWS + 8, HEAD)] + far_away(),
        [VMEM((ROWS * CTX, HEAD), BF16), dma((1,))],
        mib=8,
    )(marks, cache)
    later = uppers + lowers
    hidden_t, keys, one_q, one_f, table, _ = lax.optimization_barrier(
        (hidden_t, keys, one_q, one_f, table, later)
    )
    keep, give = call(
        normalise_kernel,
        "normalise",
        (
            shape((HALF, TOKENS, WIDE), BF16),
            shape((HALF, TOKENS, WIDE), BF16),
        ),
        scalars(2) + [whole(PARTS, 1, OWN)] + [whole(8, 2 * OWN, TOKENS)],
        [],
        mib=16,
    )(here, seat, norm_gain.reshape(PARTS, 1, OWN), hidden_t)
    given = fetch(give, 0, 0, 1)

    old = call(
        old_kernel,
        "old",
        shape((2, TOKENS, HEAD), F32),
        scalars()
        + [whole(HALF, TOKENS, WIDE)] * 2
        + [whole(2 * TOKENS + 8, HEAD), whole(ROWS + 8, HEAD)]
        + [whole(TOKENS, HEAD)] * 3
        + far_away(3),
        [
            VMEM((WIDTH, 256), BF16),
            VMEM((WIDTH, HEAD), BF16),
            VMEM((ROWS * CTX, HEAD), BF16),
            VMEM((2 * TOKENS, HEAD), F32),
            VMEM((2 * TOKENS, HEAD), F32),
            dma((9,)),
        ],
        mib=24,
    )(here, keep, give, table, marks, keys, one_q, one_f, base_query, base_key, cache)

    own, other, mine = call(
        project_kernel,
        "project",
        (
            shape((TOKENS, 512), F32),
            shape((TOKENS, 512), F32),
            shape((HALF, FOLD, 512), BF16),
        ),
        scalars()
        + [whole(HALF, TOKENS, WIDE)] * 2
        + [whole(UPPER, 512)] * 8
        + [whole(LOWER, 512)] * 8,
        [],
        mib=24,
    )(here, keep, given, *uppers, *lowers)
    other = fetch(other, 0, 0, 1)
    theirs = fetch(mine, 0, 0, 1)

    parts = call(
        attend_kernel,
        "attend",
        (shape((2, SENT, HEAD), BF16),) * 4 + (shape((2, SENT, HEAD), F32),) * 4,
        scalars(2)
        + [whole(TOKENS, 512)] * 2
        + [whole(2 * TOKENS + 8, HEAD), whole(ROWS + 8, HEAD)]
        + far_away(2)
        + [whole(TOKENS, HEAD)] * 3
        + [whole(2, TOKENS, HEAD)]
        + [whole(HALF, FOLD, 512)] * 2,
        [
            VMEM((ROWS * CTX, HEAD), BF16),
            VMEM((ROWS * CTX, HEAD), BF16),
            VMEM((2 * TOKENS, HEAD), F32),
            VMEM((2 * TOKENS, HEAD), F32),
            VMEM((2 * TOKENS, HEAD), F32),
            dma((2,)),
        ],
        mib=24,
    )(here, seat, own, other, table, marks, cache, values, keys, one_q, one_f, old, mine, theirs)
    crossed = [along_shard(give, 1, 0) for give in parts[:4]]
    landed, sums = [], parts[4:5]
    for trips, keep_part, recv in zip(TRIPS, parts[4:], crossed):
        keep_part, _ = lax.optimization_barrier((keep_part, tuple(sums)))
        kinds = tuple(shape((SENT, HEAD), BF16 if dz else F32) for dz in trips)
        sums = call(
            merge_kernel, "merge", kinds, [whole(2, SENT, HEAD)] * 2, [], mib=8
        )(keep_part, recv)
        landed += [along_shard(part, 0, -dz) if dz else part for dz, part in zip(trips, sums)]
    out, ratio = call(
        finish_kernel,
        "finish",
        (shape((TOKENS, OWN), BF16), shape((1, TOKENS), F32)),
        [whole(SENT, HEAD)] * 8,
        [],
        mib=16,
    )(landed[-1], *landed[:-1])
    return out.reshape(STEPS, ROWS, OWN), ratio


def solution(mesh):
    return jax.shard_map(
        local,
        mesh=mesh,
        in_specs=(
            P(None, "replica", "shard"),
            P(),
            P(),
            P(),
            P(None, "shard"),
            P(None, "shard"),
            P(None, "shard"),
            P(None, "shard"),
            P(("replica", "shard"), None),
            P(("replica", "shard"), None),
            P(("replica", "shard"), None),
            P(("replica", "shard"), None),
            P(("replica", "shard"), None),
            P(("replica", "shard"), None),
            P(("replica", "shard"), None),
            P(("replica", "shard"), None),
            P("replica", None, "shard"),
            P("replica", None, "shard"),
            P("replica"),
            P("replica", None),
            P("replica", None),
            P("replica", None),
        ),
        out_specs=(P(None, "replica", "shard"), P("replica", None)),
        check_vma=False,
    )
```

```python
import jax
import jax.numpy as jnp
from jax import lax
from jax.experimental import pallas as pl
from jax.experimental.pallas import tpu as pltpu
from jax.sharding import PartitionSpec as P

HQ = 32
KV = 8
HEAD = 128
WIDTH = 5120
STEPS = 4
ROWS = 32
TOKENS = STEPS * ROWS
CTX = 64
PARTS = 16
OWN = WIDTH // PARTS
CUT = 20
FIRST = {"q": 0, "k": 32, "v": 40, "o": 48}
TIDY = 32
GROUP = 8
GROUPS = ROWS // GROUP
TAIL = 16
EPSILON = 1e-06
THETA = 1000000.0
SCALE = HEAD ** (-0.5)
NEG = -1e30
TILES = ((0, 128), (128, 128), (256, 64))
BLOCK = 128
HALF = PARTS // 2
FOLD = OWN // 2
UPPER = 256
LOWER = OWN - UPPER + FOLD
WIDE = 384
SENT = OWN + TAIL
TRIPS = ((3, -3), (4, 2), (-2, 1), (-1, 0))
F32 = jnp.float32
BF16 = jnp.bfloat16
VMEM = pltpu.VMEM


def fetch(value, dx, dy, dc):
    pairs = []
    for i in range(16):
        x, y, c = i >> 3, (i >> 1) & 3, i & 1
        pairs.append((((x ^ dx) << 3) + (((y + dy) & 3) << 1) + (c ^ dc), i))
    return lax.ppermute(value, "replica", pairs)


PLACES = tuple((dx, dy) for dx in range(2) for dy in range(4))


def owner(here, place):
    return (((here >> 3) ^ place[0]) << 2) + (((here >> 1) + place[1]) & 3)


def gather_blocks(own, turn):
    over, first, back = fetch(own, 1, 0, 0), fetch(own, 0, turn, 0), fetch(own, 0, -turn, 0)
    over_first, far, over_back = fetch(first, 1, 0, 0), fetch(first, 0, turn, 0), fetch(over, 0, -turn, 0)
    held = {(0, 0): own, (1, 0): over, (0, turn & 3): first, (0, -turn & 3): back}
    held.update({(1, turn & 3): over_first, (0, 2): far, (1, -turn & 3): over_back})
    if turn == 1:
        held[1, 2] = fetch(far, 1, 0, 0)
    else:
        held[1, 2] = fetch(over_back, 0, 1, 0)
    return [held[place] for place in PLACES]


def along_shard(value, dx, dz):
    pairs = [((((i >> 3) ^ dx) << 3) + ((i + dz) & 7), i) for i in range(16)]
    return lax.ppermute(value, "shard", pairs)


def factors(codes):
    out = jnp.ones(codes.shape, F32)
    for bit in range(5):
        out = out * jnp.where((codes >> bit) & 1 == 1, F32(2.0 ** -(2**bit)), F32(1.0))
    return out


def start_all(copies):
    for copy in copies:
        copy.start()


def pack_kernel(
    hidden, codes, sq, so, skt, svt,
    out, turned,
    vh, rows, vsq, vso, vsk, vsv, buf, sems,
):
    pairs = [(hidden, vh), (sq, vsq), (so, vso), (skt, vsk), (svt, vsv)]
    pairs.append((codes, rows))
    copies = [pltpu.make_async_copy(a, b, sems.at[i]) for i, (a, b) in enumerate(pairs)]
    start_all(copies)
    for copy in copies[:5]:
        copy.wait()
    for at, n in TILES:
        turned[at : at + n, :] = vh[:, at : at + n].astype(F32).T.astype(BF16)
    fq, fo, fk, fv = factors(vsq[...]), factors(vso[...]), factors(vsk[...]), factors(vsv[...])
    line = lax.broadcasted_iota(jnp.int32, (CUT, CUT), 0)
    lane = lax.broadcasted_iota(jnp.int32, (CUT, CUT), 1)

    def column(factor, head):
        spread = jnp.where(line == lane, factor[head : head + 1, :], 0.0)
        return jnp.sum(spread, axis=1, keepdims=True)

    def piece(codes, head, factor):
        at = (FIRST[codes] + head) * HEAD
        return rows[:, at : at + HEAD].astype(F32)[0:CUT] * factor

    for copy in copies[5:]:
        copy.wait()
    buf[6 * CUT : BLOCK, :] = jnp.zeros((BLOCK - 6 * CUT, HEAD), F32)
    for half in range(PARTS // 2):
        key, value = piece("k", half, column(fk, half)), piece("v", half, column(fv, half))
        for dest in (2 * half, 2 * half + 1):
            pieces = (
                piece("q", 2 * dest, fq[:, 2 * dest : 2 * dest + 1]),
                piece("q", 2 * dest + 1, fq[:, 2 * dest + 1 : 2 * dest + 2]),
                key,
                value,
                piece("o", 2 * dest, fo[:, 2 * dest : 2 * dest + 1]),
                piece("o", 2 * dest + 1, fo[:, 2 * dest + 1 : 2 * dest + 2]),
            )
            for c, item in enumerate(pieces):
                buf[CUT * c : CUT * (c + 1), :] = item
            out[dest] = buf[...].astype(BF16)


def spread_kernel(turned, across, out, pair, sems):
    pair[0:OWN, :] = turned[...]
    pair[OWN:, :] = across[...]
    copies = [pltpu.make_async_copy(pair, out.at[z], sems.at[z]) for z in range(8)]
    start_all(copies)
    for copy in copies:
        copy.wait()


def refresh_kernel(
    here, recv, bq, bk, bv, bo, upper, lower, vq, vk, vv, vo, buf, delta, sems,
):
    at = pl.ds(pl.multiple_of(OWN * here[0], 64), OWN)
    bases = ((bq, vq), (bk, vk), (bv, vv), (bo, vo))
    copies = [
        pltpu.make_async_copy(a.at[at, :], b, sems.at[i]) for i, (a, b) in enumerate(bases)
    ]
    start_all(copies)
    for src in range(PARTS):
        buf[src % 2] = recv[src].astype(F32)
        for c in range(6):
            delta[CUT * src : CUT * (src + 1), HEAD * c : HEAD * (c + 1)] = buf[
                src % 2, CUT * c : CUT * (c + 1), :
            ]
    for copy in copies:
        copy.wait()
    for at, n, base in ((0, 256, vq), (256, 128, vk), (384, 128, vv)):
        value = (base[...].astype(F32) + delta[:, at : at + n]).astype(BF16)
        upper[:, at : at + n] = value[0:UPPER]
        lower[0 : OWN - UPPER, at : at + n] = value[UPPER:]
    for half in range(2):
        at = slice(half * FOLD, (half + 1) * FOLD)
        value = vo[at, :].astype(F32) + delta[at, 512:768]
        lower[OWN - UPPER :, half * 256 : (half + 1) * 256] = value.astype(BF16)


def dot_nt(a, b):
    return lax.dot_general(a, b, (((1,), (1,)), ((), ())), preferred_element_type=F32)


def dot(a, b):
    return jnp.dot(a, b, preferred_element_type=F32)


def head_norm_rotate(raw, gain, cosine, sine):
    value = raw * lax.rsqrt(jnp.mean(raw * raw, axis=-1, keepdims=True) + EPSILON) * gain
    swapped = jnp.concatenate([value[:, HEAD // 2 :], value[:, : HEAD // 2]], axis=-1)
    return value * cosine + swapped * sine


def group_scores(group, query, cache, fresh, lens):
    picked = [
        query[h * TOKENS + t * ROWS + group * GROUP : h * TOKENS + t * ROWS + (group + 1) * GROUP, :]
        for h in range(2)
        for t in range(STEPS)
    ]
    q = jnp.concatenate(picked, axis=0).astype(BF16)
    past = dot_nt(q, cache) * SCALE
    new = dot_nt(q, fresh) * SCALE
    n = 2 * STEPS * GROUP
    length = jnp.concatenate([lens[group * GROUP : (group + 1) * GROUP, :]] * (2 * STEPS), axis=0)
    column = lax.broadcasted_iota(jnp.int32, past.shape, 1)
    line = lax.broadcasted_iota(jnp.int32, past.shape, 0)
    past_ok = ((column >> 6) == (line & 7)) & ((column & 63) < length[:, 0:1])
    column = lax.broadcasted_iota(jnp.int32, (n, TOKENS), 1)
    line = lax.broadcasted_iota(jnp.int32, (n, TOKENS), 0)
    new_ok = ((column & 31) == group * GROUP + (line & 7)) & ((column >> 5) <= ((line >> 3) & 3))
    past = jnp.where(past_ok, past, NEG)
    new = jnp.where(new_ok, new, NEG)
    top = jnp.maximum(
        jnp.max(past, axis=-1, keepdims=True), jnp.max(new, axis=-1, keepdims=True)
    )
    past = jnp.exp(past - top)
    new = jnp.exp(new - top)
    total = jnp.sum(past, axis=-1, keepdims=True) + jnp.sum(new, axis=-1, keepdims=True)
    return past, new, total, top + jnp.log(total)


def put_groups(group, ref, value):
    for h in range(2):
        for t in range(STEPS):
            at = h * TOKENS + t * ROWS + group * GROUP
            i = (h * STEPS + t) * GROUP
            ref[at : at + GROUP, :] = value[i : i + GROUP, :]


def sample_logp(query, keys, one_query, lse):
    out = []
    for h in range(2):
        q = dot(one_query, query[h * TOKENS : (h + 1) * TOKENS, :].astype(BF16))
        score = jnp.sum(q * keys, axis=-1, keepdims=True) * SCALE
        line = lse[h * TOKENS : (h + 1) * TOKENS, :].T
        picked = jnp.sum(one_query.astype(F32) * line, axis=-1, keepdims=True)
        out.append(jnp.broadcast_to(score - picked, (TOKENS, HEAD)))
    return out


def normalise_kernel(here, seat, gain, pairs, keep, give):
    total = jnp.zeros((1, TOKENS), F32)
    for z in range(8):
        x = pairs[z].astype(F32)
        total = total + jnp.sum(x * x, axis=0, keepdims=True)
    scale = lax.rsqrt(total * (1.0 / WIDTH) + EPSILON)
    me, core = seat[0], here[0] & 1

    def put(z, target):
        for half in range(2):
            src = (((me >> 3) ^ half) << 3) + z
            for at, n in TILES:
                x = pairs[z, half * OWN + at : half * OWN + at + n, :].astype(F32) * scale
                value = (x.T * gain[src, :, at : at + n]).astype(BF16)
                target[src >> 1, :, at : at + n] = value
            target[src >> 1, :, OWN:] = jnp.zeros((TOKENS, WIDE - OWN), BF16)

    for z in range(8):
        pl.when(core == z & 1)(lambda z=z: put(z, keep))
        pl.when(core != z & 1)(lambda z=z: put(z, give))


def select_kernel(marks, cache_hbm, keys_out, one_q_out, one_f_out, cache, sems):
    copy = pltpu.make_async_copy(cache_hbm, cache, sems.at[0])
    copy.start()
    tokens = jnp.broadcast_to(marks[ROWS : ROWS + 1, :], (TOKENS, TOKENS)).T
    places = jnp.broadcast_to(marks[ROWS + 1 : ROWS + 2, :], (TOKENS, TOKENS)).T
    lane = lax.broadcasted_iota(jnp.int32, (TOKENS, TOKENS), 1)
    one_q = jnp.where(tokens == lane, F32(1.0), F32(0.0)).astype(BF16)
    one_f = jnp.where(places == lane + ROWS * CTX, F32(1.0), F32(0.0)).astype(BF16)
    copy.wait()
    keys = jnp.zeros((TOKENS, HEAD), F32)
    for k in range(ROWS * CTX // HEAD):
        one = jnp.where(places == lane + k * HEAD, F32(1.0), F32(0.0)).astype(BF16)
        keys = keys + dot(one, cache[k * HEAD : (k + 1) * HEAD, :])
    keys_out[...] = keys
    one_q_out[...] = one_q
    one_f_out[...] = one_f


def old_kernel(
    here, keep, give, table, marks, keys, one_q, one_f, base_q, base_k, cache_hbm,
    old_out,
    wq, wk, cache, query, lse, sems,
):
    quarter = WIDTH // 4
    copies = []
    for i in range(4):
        at = pl.ds(i * quarter, quarter)
        copies += [
            pltpu.make_async_copy(base_q.at[at, :], wq.at[at, :], sems.at[2 * i]),
            pltpu.make_async_copy(base_k.at[at, :], wk.at[at, :], sems.at[2 * i + 1]),
        ]
    copies.append(pltpu.make_async_copy(cache_hbm, cache, sems.at[8]))
    start_all(copies)
    core = here[0] & 1
    raw = jnp.zeros((TOKENS, 256), F32)
    raw_k = jnp.zeros((TOKENS, HEAD), F32)
    for j in range(HALF):
        if j % 2 == 0:
            copies[j].wait()
            copies[j + 1].wait()
        for lines, src in ((keep, 2 * j + core), (give, 2 * j + 1 - core)):
            at = pl.ds(pl.multiple_of(OWN * src, 64), OWN)
            raw = raw + dot(lines[j, :, 0:OWN], wq[at, :])
            raw_k = raw_k + dot(lines[j, :, 0:OWN], wk[at, :])
    copies[8].wait()
    cos, sin = table[0:TOKENS, :], table[TOKENS : 2 * TOKENS, :]
    qg, kg = table[2 * TOKENS : 2 * TOKENS + 1, :], table[2 * TOKENS + 1 : 2 * TOKENS + 2, :]
    lens = marks
    for h in range(2):
        query[h * TOKENS : (h + 1) * TOKENS, :] = (
            head_norm_rotate(raw[:, h * HEAD : (h + 1) * HEAD], qg, cos, sin)
            .astype(BF16)
            .astype(F32)
        )
    fresh = head_norm_rotate(raw_k, kg, cos, sin).astype(BF16)
    for g in range(GROUPS):
        _, _, _, log_sum = group_scores(
            g, query, cache[g * GROUP * CTX : (g + 1) * GROUP * CTX, :], fresh, lens
        )
        put_groups(g, lse, jnp.broadcast_to(log_sum, (log_sum.shape[0], HEAD)))
    old = sample_logp(query, keys[...] + dot(one_f[...], fresh), one_q[...], lse)
    old_out[0] = old[0]
    old_out[1] = old[1]


def project_kernel(here, keep, given, *rest):
    uppers, lowers, (own, other, below) = rest[0:8], rest[8:16], rest[16:]
    raw = jnp.zeros((2 * TOKENS, 512), F32)
    for place, upper, lower in zip(PLACES, uppers, lowers):
        j = owner(here[0], place)
        for at, n, weight in ((0, UPPER, upper), (UPPER, OWN - UPPER, lower)):
            lines = jnp.concatenate([keep[j, :, at : at + n], given[j, :, at : at + n]], axis=0)
            raw = raw + dot(lines, weight[0:n, :])
        below[j] = lower[OWN - UPPER :, :]
    own[...] = raw[0:TOKENS, :]
    other[...] = raw[TOKENS:, :]


def attend_kernel(
    here, seat, own, other, table, marks, cache_hbm, values_hbm, keys, one_q, one_f, old, mine, theirs,
    give0, give1, give2, give3, keep0, keep1, keep2, keep3,
    cache, values, query, lse, mixed, sems,
):
    copies = (
        pltpu.make_async_copy(cache_hbm, cache, sems.at[0]),
        pltpu.make_async_copy(values_hbm, values, sems.at[1]),
    )
    start_all(copies)
    raw = own[...] + other[...]
    cos, sin = table[0:TOKENS, :], table[TOKENS : 2 * TOKENS, :]
    qg, kg = table[2 * TOKENS : 2 * TOKENS + 1, :], table[2 * TOKENS + 1 : 2 * TOKENS + 2, :]
    lens = marks
    for h in range(2):
        query[h * TOKENS : (h + 1) * TOKENS, :] = (
            head_norm_rotate(raw[:, h * HEAD : (h + 1) * HEAD], qg, cos, sin)
            .astype(BF16)
            .astype(F32)
        )
    fresh = head_norm_rotate(raw[:, 256:384], kg, cos, sin).astype(BF16)
    fresh_v = raw[:, 384:512].astype(BF16)
    for copy in copies:
        copy.wait()
    for g in range(GROUPS):
        at = slice(g * GROUP * CTX, (g + 1) * GROUP * CTX)
        past, new, total, log_sum = group_scores(g, query, cache[at, :], fresh, lens)
        put_groups(g, lse, jnp.broadcast_to(log_sum, (log_sum.shape[0], HEAD)))
        mix = dot((past / total).astype(BF16), values[at, :])
        mix = mix + dot((new / total).astype(BF16), fresh_v)
        put_groups(g, mixed, mix)
    attended = jnp.concatenate([mixed[0:TOKENS, :], mixed[TOKENS:, :]], axis=1).astype(BF16)
    gives, keeps = (give0, give1, give2, give3), (keep0, keep1, keep2, keep3)
    me = seat[0]

    def place_parts(even, odd):
        for c, trips in enumerate(TRIPS):
            for i, dz in enumerate(trips):
                rows = odd if dz & 1 else even
                for dx, target in ((1, gives[c]), (0, keeps[c])):
                    j = (((me >> 3) ^ dx) << 2) + (((me + dz) & 7) >> 1)
                    for half in range(2):
                        part = dot_nt(rows[j, :, half * 256 : (half + 1) * 256], attended)
                        at = slice(half * FOLD, (half + 1) * FOLD)
                        target[i, at, :] = part.astype(target.dtype)

    same = ((here[0] ^ me) & 1) == 0
    pl.when(same)(lambda: place_parts(mine, theirs))
    pl.when(jnp.logical_not(same))(lambda: place_parts(theirs, mine))
    now = sample_logp(query, keys[...] + dot(one_f[...], fresh), one_q[...], lse)
    term = (now[0] - old[0]) + (now[1] - old[1])
    tail = split_line(term.T[0:1, :])
    for target in gives + keeps:
        for i in range(2):
            target[i, OWN:SENT, :] = tail.astype(target.dtype)


def split_line(line):
    high = line.astype(BF16).astype(F32)
    middle = (line - high).astype(BF16).astype(F32)
    low = line - high - middle
    return jnp.concatenate([high, middle, low, jnp.zeros((TAIL - 3, TOKENS), F32)], axis=0)


def merge_kernel(keep, recv, first, second):
    for i, out in enumerate((first, second)):
        total = keep[i] + recv[i].astype(F32)
        out[0:OWN, :] = total[0:OWN, :].astype(out.dtype)
        line = (total[OWN + 2 : OWN + 3, :] + total[OWN + 1 : OWN + 2, :]) + total[OWN : OWN + 1, :]
        out[OWN:SENT, :] = split_line(line).astype(out.dtype)


def finish_kernel(own, r1, r2, r3, r4, r5, r6, r7, out, ratio):
    for k, n in ((0, 128), (128, 128), (256, 80)):
        total = own[k : k + n, :]
        for part in (r1, r2, r3, r4, r5, r6, r7):
            total = total + part[k : k + n, :].astype(F32)
        if n == 128:
            out[:, k : k + n] = total.T.astype(BF16)
        else:
            tail = total[64:67, :]
            ratio[...] = ((tail[2:3, :] + tail[1:2, :]) + tail[0:1, :]) * (1.0 / HQ)
            out[:, k : k + 64] = total[0:64, :].T.astype(BF16)


def params(mib):
    return pltpu.CompilerParams(vmem_limit_bytes=mib * 1024 * 1024)


def shape(dims, dtype):
    return jax.ShapeDtypeStruct(dims, dtype)


def whole(*dims):
    return pl.BlockSpec(dims, lambda i: (0,) * len(dims))


def scalars(n=1):
    return [pl.BlockSpec(memory_space=pltpu.SMEM)] * n


def far_away(n=1):
    return [pl.BlockSpec(memory_space=pltpu.HBM)] * n


def spec_of(out):
    return whole(*out.shape)


def call(kernel, name, outs, in_specs, scratch, far=False, mib=56):
    several = isinstance(outs, tuple)
    return pl.pallas_call(
        kernel,
        name=name,
        grid=(1,),
        out_shape=outs,
        in_specs=in_specs,
        out_specs=far_away()[0] if far else tuple(map(spec_of, outs)) if several else spec_of(outs),
        scratch_shapes=scratch,
        compiler_params=params(mib),
    )


def local(
    hidden,
    norm_gain,
    query_gain,
    key_gain,
    base_query,
    base_key,
    base_value,
    base_output,
    delta_query,
    scale_query,
    key_delta_codes,
    key_scale_codes,
    value_delta_codes,
    value_scale_codes,
    delta_output,
    scale_output,
    cache_keys,
    cache_values,
    lengths,
    stale_rows,
    stale_steps,
    stale_back,
):
    here = lax.axis_index("replica").astype(jnp.int32).reshape(1)
    seat = lax.axis_index("shard").astype(jnp.int32).reshape(1)
    dma = pltpu.SemaphoreType.DMA
    codes = [delta_query, key_delta_codes, value_delta_codes, delta_output]
    codes = jnp.pad(jnp.concatenate(codes, axis=1), ((0, TIDY - CUT), (0, 0)))
    packed, turned = call(
        pack_kernel,
        "pack",
        (shape((PARTS, BLOCK, HEAD), BF16), shape((OWN, TOKENS), BF16)),
        far_away(6),
        [
            VMEM((TOKENS, OWN), BF16),
            VMEM((TIDY, 80 * HEAD), BF16),
            VMEM((CUT, HQ), jnp.int32),
            VMEM((CUT, HQ), jnp.int32),
            VMEM((KV, CUT), jnp.int32),
            VMEM((KV, CUT), jnp.int32),
            VMEM((BLOCK, HEAD), F32),
            dma((6,)),
        ],
        mib=56,
    )(
        hidden.reshape(TOKENS, OWN), codes,
        scale_query, scale_output, key_scale_codes.T, value_scale_codes.T,
    )
    across = along_shard(turned, 1, 0)
    arrived = lax.all_to_all(packed, "shard", split_axis=0, concat_axis=0, tiled=False)
    spread = call(
        spread_kernel,
        "spread",
        shape((8, 2 * OWN, TOKENS), BF16),
        [whole(OWN, TOKENS)] * 2,
        [VMEM((2 * OWN, TOKENS), BF16), dma((8,))],
        True,
        mib=24,
    )(turned, across)
    arrived, spread, lengths, stale_rows, stale_steps, stale_back = lax.optimization_barrier(
        (arrived, spread, lengths, stale_rows, stale_steps, stale_back)
    )
    upper, lower = call(
        refresh_kernel,
        "refresh",
        (shape((UPPER, 512), BF16), shape((LOWER, 512), BF16)),
        scalars() + [whole(PARTS, BLOCK, HEAD)] + far_away(4),
        [
            VMEM((OWN, 256), BF16),
            VMEM((OWN, 128), BF16),
            VMEM((OWN, 128), BF16),
            VMEM((OWN, 256), BF16),
            VMEM((2, BLOCK, HEAD), F32),
            VMEM((OWN, 768), F32),
            dma((4,)),
        ],
        mib=56,
    )(here, arrived, base_query, base_key, base_value, base_output)
    uppers, lowers = gather_blocks(upper, 1), gather_blocks(lower, -1)
    rings = [[8 * x + z for z in range(8)] for x in range(2)]
    hidden_t = lax.all_to_all(
        spread,
        "shard",
        split_axis=0,
        concat_axis=0,
        tiled=False,
        axis_index_groups=rings,
    )

    position = (lengths[None, :] + jnp.arange(STEPS)[:, None]).reshape(TOKENS)
    freq = THETA ** (-(jnp.arange(HEAD // 2).astype(F32) * 2.0) / HEAD)
    angle = position.astype(F32)[:, None] * freq
    cos, sin = jnp.cos(angle), jnp.sin(angle)
    table = jnp.concatenate(
        [
            jnp.concatenate([cos, cos], axis=1),
            jnp.concatenate([-sin, sin], axis=1),
            query_gain.reshape(1, HEAD),
            key_gain.reshape(1, HEAD),
            jnp.zeros((6, HEAD), F32),
        ],
        axis=0,
    )
    rows_s, steps_s, back_s = stale_rows, stale_steps, stale_back
    lens_s = jnp.sum(
        jnp.where(rows_s[0][None, :] == jnp.arange(ROWS)[:, None], lengths[:, None], 0),
        axis=0,
        keepdims=True,
    )
    at = lens_s + steps_s - back_s % (lens_s + steps_s + 1)
    place = jnp.where(
        at >= lens_s, ROWS * CTX + (at - lens_s) * ROWS + rows_s, rows_s * CTX + at
    ).astype(jnp.int32)
    token = (steps_s * ROWS + rows_s).astype(jnp.int32)
    marks = jnp.concatenate(
        [
            jnp.broadcast_to(lengths[:, None], (ROWS, HEAD)),
            token,
            place,
            jnp.zeros((6, HEAD), jnp.int32),
        ],
        axis=0,
    )
    cache = cache_keys.reshape(ROWS * CTX, HEAD)
    values = cache_values.reshape(ROWS * CTX, HEAD)

    keys, one_q, one_f = call(
        select_kernel,
        "select",
        (
            shape((TOKENS, HEAD), F32),
            shape((TOKENS, TOKENS), BF16),
            shape((TOKENS, TOKENS), BF16),
        ),
        [whole(ROWS + 8, HEAD)] + far_away(),
        [VMEM((ROWS * CTX, HEAD), BF16), dma((1,))],
        mib=8,
    )(marks, cache)
    later = uppers + lowers
    hidden_t, keys, one_q, one_f, table, _ = lax.optimization_barrier(
        (hidden_t, keys, one_q, one_f, table, later)
    )
    keep, give = call(
        normalise_kernel,
        "normalise",
        (
            shape((HALF, TOKENS, WIDE), BF16),
            shape((HALF, TOKENS, WIDE), BF16),
        ),
        scalars(2) + [whole(PARTS, 1, OWN)] + [whole(8, 2 * OWN, TOKENS)],
        [],
        mib=16,
    )(here, seat, norm_gain.reshape(PARTS, 1, OWN), hidden_t)
    given = fetch(give, 0, 0, 1)

    old = call(
        old_kernel,
        "old",
        shape((2, TOKENS, HEAD), F32),
        scalars()
        + [whole(HALF, TOKENS, WIDE)] * 2
        + [whole(2 * TOKENS + 8, HEAD), whole(ROWS + 8, HEAD)]
        + [whole(TOKENS, HEAD)] * 3
        + far_away(3),
        [
            VMEM((WIDTH, 256), BF16),
            VMEM((WIDTH, HEAD), BF16),
            VMEM((ROWS * CTX, HEAD), BF16),
            VMEM((2 * TOKENS, HEAD), F32),
            VMEM((2 * TOKENS, HEAD), F32),
            dma((9,)),
        ],
        mib=24,
    )(here, keep, give, table, marks, keys, one_q, one_f, base_query, base_key, cache)

    own, other, mine = call(
        project_kernel,
        "project",
        (
            shape((TOKENS, 512), F32),
            shape((TOKENS, 512), F32),
            shape((HALF, FOLD, 512), BF16),
        ),
        scalars()
        + [whole(HALF, TOKENS, WIDE)] * 2
        + [whole(UPPER, 512)] * 8
        + [whole(LOWER, 512)] * 8,
        [],
        mib=24,
    )(here, keep, given, *uppers, *lowers)
    other = fetch(other, 0, 0, 1)
    theirs = fetch(mine, 0, 0, 1)

    parts = call(
        attend_kernel,
        "attend",
        (shape((2, SENT, HEAD), BF16),) * 4 + (shape((2, SENT, HEAD), F32),) * 4,
        scalars(2)
        + [whole(TOKENS, 512)] * 2
        + [whole(2 * TOKENS + 8, HEAD), whole(ROWS + 8, HEAD)]
        + far_away(2)
        + [whole(TOKENS, HEAD)] * 3
        + [whole(2, TOKENS, HEAD)]
        + [whole(HALF, FOLD, 512)] * 2,
        [
            VMEM((ROWS * CTX, HEAD), BF16),
            VMEM((ROWS * CTX, HEAD), BF16),
            VMEM((2 * TOKENS, HEAD), F32),
            VMEM((2 * TOKENS, HEAD), F32),
            VMEM((2 * TOKENS, HEAD), F32),
            dma((2,)),
        ],
        mib=24,
    )(here, seat, own, other, table, marks, cache, values, keys, one_q, one_f, old, mine, theirs)
    crossed = [along_shard(give, 1, 0) for give in parts[:4]]
    landed, sums = [], parts[4:5]
    for trips, keep_part, recv in zip(TRIPS, parts[4:], crossed):
        keep_part, _ = lax.optimization_barrier((keep_part, tuple(sums)))
        kinds = tuple(shape((SENT, HEAD), BF16 if dz else F32) for dz in trips)
        sums = call(
            merge_kernel, "merge", kinds, [whole(2, SENT, HEAD)] * 2, [], mib=8
        )(keep_part, recv)
        landed += [along_shard(part, 0, -dz) if dz else part for dz, part in zip(trips, sums)]
    out, ratio = call(
        finish_kernel,
        "finish",
        (shape((TOKENS, OWN), BF16), shape((1, TOKENS), F32)),
        [whole(SENT, HEAD)] * 8,
        [],
        mib=16,
    )(landed[-1], *landed[:-1])
    return out.reshape(STEPS, ROWS, OWN), ratio


def solution(mesh):
    return jax.shard_map(
        local,
        mesh=mesh,
        in_specs=(
            P(None, "replica", "shard"),
            P(),
            P(),
            P(),
            P(None, "shard"),
            P(None, "shard"),
            P(None, "shard"),
            P(None, "shard"),
            P(("replica", "shard"), None),
            P(("replica", "shard"), None),
            P(("replica", "shard"), None),
            P(("replica", "shard"), None),
            P(("replica", "shard"), None),
            P(("replica", "shard"), None),
            P(("replica", "shard"), None),
            P(("replica", "shard"), None),
            P("replica", None, "shard"),
            P("replica", None, "shard"),
            P("replica"),
            P("replica", None),
            P("replica", None),
            P("replica", None),
        ),
        out_specs=(P(None, "replica", "shard"), P("replica", None)),
        check_vma=False,
    )
```
